512 devices in a mesh: tile: 64 (over z, y_lo, core), led: 8 (over y_hi, x).
Axes of the slice: x: 4, y: 4 (y_hi: 2, y_lo: 2; y = y_hi * 2 + y_lo), z: 16, core: 2. Of those that a mesh axis runs over, the one named last changes fastest.
Arguments:
- spectrum: bfloat16 [64, 2, 512, 512], P('tile'), may hold values from -4 to 4
- pupil: bfloat16 [64, 2, 128, 128], P('tile'), may hold values from -4 to 4
- offsets: int32 [64, 224, 2], P('tile', 'led'), may hold values from 0 to 384, as said below
- widths: int32 [63], replicated, may hold values from 1 to 16
- live: int32 [224], P('led'), may hold values 0 or 1
- measured: bfloat16 [224, 7168, 128], P('led', 'tile'), may hold values from 0 to 2
Outputs:
- spectrum_grad: float32 [64, 2, 512, 512], P('tile', None, 'led')
- pupil_grad: float32 [64, 2, 128, 128], P('tile', None, 'led')
The draws below stay inside these ranges and needn't reach their ends.
Inputs may be any that keep to these rules, and one draw needn't show every extreme that they name: offsets[t, l] belongs to LED l at row l // 15 and column l % 15 of a 15 x 15 LED grid whose last LED is left out; an LED's offsets vary by at most 16 from tile to tile.
All inputs are finite; a program needn't handle non-finite values. No bound on the sum of `live` on one device may be relied on, other than what follows from the above.
Results may differ from the reference program's by a relative error of at most 0.0003.
Values may be sent and summed in bfloat16 or wider, within the bound.
A program may use at most 64 MiB of HBM per device.

```python
import math
import jax
import jax.numpy as jnp
from jax import lax

SPEC = 512
PUP = 128
OV = 16
SHIFT = 8
LED_SIDE = 15
TILES = 64
LEDS = 224
HALF = 8
STRIDE = 112
ROWS = 7168
BOUNDS = 63


def draw_offsets(key, part):
    key = jax.random.fold_in(key, 11)
    lamps = jnp.arange(LEDS)
    span = SPEC - PUP + 2 * SHIFT
    steps_total = LED_SIDE - 1
    base_row = lamps // LED_SIDE * span // steps_total - SHIFT
    base_col = lamps % LED_SIDE * span // steps_total - SHIFT
    nominal = jnp.stack([base_row, base_col], -1)
    moves = jax.random.randint(key, (TILES, LEDS, 2), -SHIFT, SHIFT + 1)
    return jnp.clip(nominal[None] + moves, 0, SPEC - PUP).astype(jnp.int32)


def set_ends(drawn, stream_key, low, top_value):
    spot = [jax.random.randint(jax.random.fold_in(stream_key, axis), (), 0, length) for axis, length in enumerate(drawn.shape)]
    widest = drawn.shape.index(max(drawn.shape))
    beside = spot[:widest] + [(spot[widest] + 1) % drawn.shape[widest]] + spot[widest + 1:]
    return drawn.at[tuple(spot)].set(low).at[tuple(beside)].set(top_value)


def block_scale(key, shape, split, least, top_value):
    factor_of, own = 1.0, jax.random.fold_in(key, 6)
    for position, parts in split:
        draws = jnp.exp(jax.random.uniform(jax.random.fold_in(own, position), (parts,), jnp.float32, least / len(split), top_value / len(split)))
        factor_of = factor_of * jnp.repeat(draws, shape[position] // parts).reshape([-1 if axis == position else 1 for axis in range(len(shape))])
    return factor_of


def normal_values(own_key, dims, width, bound, shards=(), dtype=jnp.bfloat16):
    result = width * jax.random.normal(own_key, dims, jnp.float32)
    if shards:
        result = result * block_scale(own_key, dims, shards, -0.22, 0.18)
    return jnp.clip(result, -bound, bound).astype(dtype)


def setup_inputs(seed: int = 0) -> dict:
    seeds = jax.random.split(jax.random.key(seed), 7)
    spectrum = normal_values(seeds[0], (TILES, 2, SPEC, SPEC), 0.7, 4.0, ((0, 64),))
    pupil = normal_values(seeds[1], (TILES, 2, PUP, PUP), 0.7, 4.0, ((0, 64),))
    offsets = draw_offsets(jax.random.fold_in(seeds[6], 71), 0)
    widths = set_ends(jax.random.randint(seeds[3], (BOUNDS,), 1, OV + 1), jax.random.fold_in(seeds[3], 1), 1, OV).astype(jnp.int32)
    live = set_ends((jax.random.randint(seeds[4], (LEDS,), 0, 3) < 2).astype(jnp.int32), jax.random.fold_in(seeds[4], 1), 0, 1)
    measured = jnp.clip(2.0 * jax.random.uniform(seeds[5], (LEDS, ROWS, PUP), jnp.float32) ** block_scale(seeds[5], (LEDS, ROWS, PUP), ((0, 8), (1, 64)), -0.2, 0.2), 0.0, 2.0).astype(jnp.bfloat16)
    return dict(spectrum=spectrum, pupil=pupil, offsets=offsets, widths=widths, live=live, measured=measured)


def blend_weights(widths, index, tiles):
    rows = jnp.arange(PUP)
    place = rows.astype(jnp.float32)
    half = OV // 2
    stride = PUP - OV
    above_width = widths[jnp.maximum(index - 1, 0)].astype(jnp.float32)
    below_width = widths[jnp.minimum(index, tiles - 2)].astype(jnp.float32)
    ramp_above = jnp.clip(0.5 + (half - 0.5 - place) / above_width, 0.0, 1.0)
    ramp_below = jnp.clip(0.5 + (half - 0.5 - (place - stride)) / below_width, 0.0, 1.0)
    weights = jnp.where((rows < OV) & (index > 0), 1.0 - ramp_above, jnp.ones_like(ramp_above))
    weights = jnp.where((rows >= stride) & (index < tiles - 1), ramp_below, weights)
    return weights

def take_window(source, start):
    zero = jnp.zeros((), jnp.int32)
    return lax.dynamic_slice(source, (zero, start[0].astype(jnp.int32), start[1].astype(jnp.int32)), (2, PUP, PUP))

def add_window(total, piece, start):
    zero = jnp.zeros((), jnp.int32)
    place = (zero, start[0].astype(jnp.int32), start[1].astype(jnp.int32))
    current = lax.dynamic_slice(total, place, piece.shape)
    return lax.dynamic_update_slice(total, current + piece, place)

def reference(spectrum, pupil, offsets, widths, live, measured):
    spectra = spectrum.astype(jnp.float32)
    pupils = pupil.astype(jnp.float32)
    weights = blend_weights(widths, jnp.arange(TILES)[:, None], TILES)[:, :, None]
    scale = 1.0 / math.sqrt(LEDS)
    images = measured.reshape(LEDS, TILES, STRIDE, PUP)
    starts_all = jnp.transpose(offsets, (1, 0, 2))
    pupil_re = pupils[:, 0]
    pupil_im = pupils[:, 1]
    empty_rows = jnp.zeros((1, HALF, PUP), jnp.float32)

    def one_led(carry, inputs):
        spec_total, pupil_total = carry
        starts, image, alive = inputs
        windows = jax.vmap(take_window)(spectra, starts)
        crop_re = windows[:, 0]
        crop_im = windows[:, 1]
        field_re = pupil_re * crop_re - pupil_im * crop_im
        field_im = pupil_re * crop_im + pupil_im * crop_re
        wave = jnp.fft.ifft2(field_re + 1j * field_im, norm='ortho')
        wave_re = jnp.real(wave)
        wave_im = jnp.imag(wave)
        weighted = weights * (wave_re * wave_re + wave_im * wave_im)
        above = jnp.concatenate([empty_rows, weighted[:-1, PUP - HALF:]], 0)
        below = jnp.concatenate([weighted[1:, :HALF], empty_rows], 0)
        blended = weighted[:, HALF:HALF + STRIDE]
        blended = blended + jnp.pad(above, ((0, 0), (0, STRIDE - HALF), (0, 0)))
        blended = blended + jnp.pad(below, ((0, 0), (STRIDE - HALF, 0), (0, 0)))
        residual = scale * alive * (blended - image.astype(jnp.float32))
        upper = jnp.concatenate([empty_rows, residual[:-1, STRIDE - HALF:]], 0)
        lower = jnp.concatenate([residual[1:, :HALF], empty_rows], 0)
        local = jnp.concatenate([upper, residual, lower], 1)
        grad_int = weights * local
        grad_wave = 2.0 * grad_int * wave_re + 1j * (2.0 * grad_int * wave_im)
        grad_field = jnp.fft.fft2(grad_wave, norm='ortho')
        grad_re = jnp.real(grad_field)
        grad_im = jnp.imag(grad_field)
        crop_grad = jnp.stack([pupil_re * grad_re + pupil_im * grad_im, pupil_re * grad_im - pupil_im * grad_re], 1)
        pupil_total = pupil_total + jnp.stack([crop_re * grad_re + crop_im * grad_im, crop_re * grad_im - crop_im * grad_re], 1)
        spec_total = jax.vmap(add_window)(spec_total, crop_grad, starts)
        return ((spec_total, pupil_total), jnp.zeros((), jnp.float32))
    start_state = (jnp.zeros((TILES, 2, SPEC, SPEC), jnp.float32), jnp.zeros((TILES, 2, PUP, PUP), jnp.float32))
    finals = lax.scan(one_led, start_state, (starts_all, images, live.astype(jnp.float32)))[0]
    return (finals[0], finals[1])
```

```python
from functools import partial
import math

import jax
import jax.numpy as jnp
import ml_dtypes
import numpy as np
from jax import lax
from jax.experimental import pallas as pl
from jax.experimental.pallas import tpu as pltpu
from jax.sharding import PartitionSpec as P

PUP = 128
OV = 16
HALF = 8
STRIDE = PUP - OV
BLOCKS = 4
MESH = pl.DeviceIdType.MESH
F32 = jnp.float32
BF16 = jnp.bfloat16
PAIRS = 2
GROUP = 2 * PAIRS
VMEM_LIMIT = 48 * 1024 * 1024


def dft_tables():
    k = np.arange(PUP)
    angle = 2.0 * np.pi * ((k[:, None] * k[None, :]) % PUP) / PUP
    cosine, sine = np.cos(angle), np.sin(angle)
    inverse = np.block([[cosine, sine], [-sine, cosine]]) / PUP
    forward = np.block([[cosine, -sine], [sine, cosine]])
    parts = []
    for table in (inverse, forward):
        high = table.astype(ml_dtypes.bfloat16)
        low = (table - high.astype(np.float64)).astype(ml_dtypes.bfloat16)
        parts += [high, low]
    return np.stack(parts)


def split(x):
    high = x.astype(BF16)
    return high, (x - high.astype(F32)).astype(BF16)


def right_product(x, high, low):
    xh, xl = split(x)
    data = jnp.concatenate([xh, xl, xh], axis=1)
    table = jnp.concatenate([high, high, low], axis=0)
    return jnp.dot(data, table, preferred_element_type=F32)


def left_product(high, low, x):
    xh, xl = split(x)
    data = jnp.concatenate([xh, xl, xh], axis=0)
    table = jnp.concatenate([high, high, low], axis=1)
    return jnp.dot(table, data, preferred_element_type=F32)


def swap_blocks(x):
    top = jnp.concatenate([x[:PUP, :PUP], x[PUP:, :PUP]], axis=1)
    bottom = jnp.concatenate([x[:PUP, PUP:], x[PUP:, PUP:]], axis=1)
    return jnp.concatenate([top, bottom], axis=0)


def ramp_weights(widths_ref, tile, tiles):
    place = lax.broadcasted_iota(jnp.int32, (OV, PUP), 0).astype(F32)
    above = widths_ref[jnp.maximum(tile - 1, 0)].astype(F32)
    below = widths_ref[jnp.minimum(tile, tiles - 2)].astype(F32)
    top = 1.0 - jnp.clip(0.5 + (HALF - 0.5 - place) / above, 0.0, 1.0)
    bottom = jnp.clip(0.5 + (HALF - 0.5 - place) / below, 0.0, 1.0)
    ones = jnp.ones_like(place)
    return jnp.where(tile > 0, top, ones), jnp.where(tile < tiles - 1, bottom, ones)


def list_live(live_ref, order_ref):
    def body(led, count):
        order_ref[count] = led
        return count + live_ref[led]

    lamps = live_ref.shape[0]
    count = lax.fori_loop(0, lamps, body, jnp.int32(0))
    for extra in range(GROUP):
        order_ref[count + extra] = 0
    return count


def load_spectrum(spec_ref, planes):
    for block in range(BLOCKS):
        for part in range(2):
            planes[block, part] = spec_ref[part, :, block * PUP : (block + 1) * PUP].astype(F32)


def window_of(planes, row, col):
    first = col // PUP
    second = jnp.minimum(first + 1, BLOCKS - 1)
    lanes = lax.broadcasted_iota(jnp.int32, (PUP, PUP), 1)
    inside = lanes >= col % PUP
    return [
        jnp.where(inside, planes[first, part, pl.ds(row, PUP), :], planes[second, part, pl.ds(row, PUP), :])
        for part in range(2)
    ]


def forward_kernel(offsets_ref, widths_ref, live_ref, spec_ref, pupil_ref, table_ref, wave_out, edge_out, planes, waves, order_ref, sems):
    tiles = lax.axis_size("tile")
    tile = lax.axis_index("tile")
    count = list_live(live_ref, order_ref)
    load_spectrum(spec_ref, planes)
    top, bottom = ramp_weights(widths_ref, tile, tiles)
    top2 = jnp.concatenate([top, top], axis=1)
    bottom2 = jnp.concatenate([bottom, bottom], axis=1)

    def field_of(slot):
        led = order_ref[slot]
        row, col = offsets_ref[led, 0], offsets_ref[led, 1]
        win_re, win_im = window_of(planes, row, col)
        shift = col % PUP
        pup_re = pltpu.roll(pupil_ref[0].astype(F32), shift, axis=1)
        pup_im = pltpu.roll(pupil_ref[1].astype(F32), shift, axis=1)
        return jnp.concatenate(
            [pup_re * win_re - pup_im * win_im, pup_re * win_im + pup_im * win_re], axis=1
        )

    def step(number, carry):
        for inner in range(PAIRS):
            pair = number * PAIRS + inner
            field = jnp.concatenate([field_of(2 * pair), field_of(2 * pair + 1)], axis=0)
            mixed = right_product(field, table_ref[0], table_ref[1])
            wave = left_product(table_ref[2], table_ref[3], swap_blocks(mixed))
            waves[pair] = wave
            first = wave[:OV], wave[PUP : PUP + OV]
            last = wave[STRIDE:PUP], wave[PUP + STRIDE :]
            edge_out[0, pair] = top2 * (first[0] * first[0] + first[1] * first[1])
            edge_out[1, pair] = bottom2 * (last[0] * last[0] + last[1] * last[1])
        here = pl.ds(number * PAIRS, PAIRS)
        pltpu.make_async_copy(waves.at[here], wave_out.at[here], sems.at[number]).start()
        return carry

    steps = (count + GROUP - 1) // GROUP
    lax.fori_loop(0, steps, step, 0)

    def finish(number, carry):
        here = pl.ds(number * PAIRS, PAIRS)
        pltpu.make_async_copy(waves.at[here], wave_out.at[here], sems.at[number]).wait()
        return carry

    lax.fori_loop(0, steps, finish, 0)


def backward_kernel(
    scale, offsets_ref, widths_ref, live_ref, spec_ref, pupil_ref, table_ref, measured_ref, above_ref, below_ref, edge_ref, wave_in,
    spec_out, pupil_out, planes, waves, order_ref, sems
):
    tiles = lax.axis_size("tile")
    tile = lax.axis_index("tile")
    count = list_live(live_ref, order_ref)
    steps = (count + GROUP - 1) // GROUP

    def fetch(number, carry):
        here = pl.ds(number * PAIRS, PAIRS)
        pltpu.make_async_copy(wave_in.at[here], waves.at[here], sems.at[number]).start()
        return carry

    lax.fori_loop(0, steps, fetch, 0)
    load_spectrum(spec_ref, planes)
    spec_out[...] = jnp.zeros_like(spec_out)
    pupil_out[...] = jnp.zeros_like(pupil_out)
    top, bottom = ramp_weights(widths_ref, tile, tiles)
    top2 = jnp.concatenate([top, top], axis=1)
    bottom2 = jnp.concatenate([bottom, bottom], axis=1)
    rows = lax.broadcasted_iota(jnp.int32, (OV, 2 * PUP), 0)
    top_grad = jnp.where((tile > 0) | (rows >= HALF), 2.0 * top2, 0.0)
    bottom_grad = jnp.where((tile < tiles - 1) | (rows < HALF), 2.0 * bottom2, 0.0)
    has_above = tile > 0
    has_below = tile < tiles - 1
    lanes = lax.broadcasted_iota(jnp.int32, (PUP, PUP), 1)

    def images(ref, leds, low, high):
        return jnp.concatenate([ref[led, low:high].astype(F32) for led in leds], axis=1)

    def step(number, carry):
        here = pl.ds(number * PAIRS, PAIRS)
        pltpu.make_async_copy(wave_in.at[here], waves.at[here], sems.at[number]).wait()
        for inner in range(PAIRS):
            pair = number * PAIRS + inner
            leds = order_ref[2 * pair], order_ref[2 * pair + 1]
            side_of = lax.broadcasted_iota(jnp.int32, (1, 2 * PUP), 1) // PUP
            alive = jnp.where(2 * pair + side_of < count, scale, 0.0)
            wave = waves[pair]
            wave_re, wave_im = wave[:PUP], wave[PUP:]
            intensity = wave_re * wave_re + wave_im * wave_im
            own = images(measured_ref, leds, 0, STRIDE)
            upper = images(above_ref, leds, OV - HALF, OV)
            lower = images(below_ref, leds, 0, HALF)
            near_top = jnp.where(has_above, edge_ref[1, pair], 0.0)
            near_bottom = jnp.where(has_below, edge_ref[0, pair], 0.0)
            first = top_grad * (top2 * intensity[:OV] + near_top - jnp.concatenate([upper, own[: OV - HALF]], axis=0))
            middle = 2.0 * (intensity[OV:STRIDE] - own[HALF : STRIDE - HALF])
            last = bottom_grad * (bottom2 * intensity[STRIDE:] + near_bottom - jnp.concatenate([own[STRIDE - HALF :], lower], axis=0))
            grad = alive * jnp.concatenate([first, middle, last], axis=0)
            grad_wave = jnp.concatenate([grad * wave_re, grad * wave_im], axis=0)
            back = right_product(swap_blocks(grad_wave), table_ref[2], table_ref[3])
            grad_field = left_product(table_ref[0], table_ref[1], swap_blocks(back))
            for side in range(2):
                led = leds[side]
                row, col = offsets_ref[led, 0], offsets_ref[led, 1]
                shift = col % PUP
                lo = side * PUP
                grad_re = grad_field[:PUP, lo : lo + PUP]
                grad_im = grad_field[PUP:, lo : lo + PUP]
                pup_re = pltpu.roll(pupil_ref[0].astype(F32), shift, axis=1)
                pup_im = pltpu.roll(pupil_ref[1].astype(F32), shift, axis=1)
                win_re, win_im = window_of(planes, row, col)
                pieces = (pup_re * grad_re + pup_im * grad_im, pup_re * grad_im - pup_im * grad_re)
                shares = (win_re * grad_re + win_im * grad_im, win_re * grad_im - win_im * grad_re)
                first_block = col // PUP
                second_block = jnp.minimum(first_block + 1, BLOCKS - 1)
                inside = lanes >= shift
                for part in range(2):
                    here_rows = pl.ds(row, PUP)
                    pupil_out[part] += pltpu.roll(shares[part], PUP - shift, axis=1)
                    spec_out[first_block, part, here_rows, :] += jnp.where(inside, pieces[part], 0.0)
                    spec_out[second_block, part, here_rows, :] += jnp.where(inside, 0.0, pieces[part])
        return carry

    lax.fori_loop(0, steps, step, 0)


def vmem():
    return pl.BlockSpec(memory_space=pltpu.VMEM)


def smem():
    return pl.BlockSpec(memory_space=pltpu.SMEM)


def hbm():
    return pl.BlockSpec(memory_space=pl.ANY)


def forward_call(offsets, widths, live, spectrum, pupil, tables):
    lamps = offsets.shape[0]
    side = spectrum.shape[-1]
    chunks = -(-lamps // GROUP)
    pairs = chunks * PAIRS
    return pl.pallas_call(
        forward_kernel,
        out_shape=(
            jax.ShapeDtypeStruct((pairs, 2 * PUP, 2 * PUP), F32),
            jax.ShapeDtypeStruct((2, pairs, OV, 2 * PUP), F32),
        ),
        in_specs=[smem()] * 3 + [vmem()] * 3,
        out_specs=(hbm(), vmem()),
        scratch_shapes=[
            pltpu.VMEM((BLOCKS, 2, side, PUP), F32),
            pltpu.VMEM((pairs, 2 * PUP, 2 * PUP), F32),
            pltpu.SMEM((lamps + GROUP,), jnp.int32),
            pltpu.SemaphoreType.DMA((chunks,)),
        ],
        compiler_params=pltpu.CompilerParams(vmem_limit_bytes=VMEM_LIMIT),
        name="forward",
    )(offsets, widths, live, spectrum, pupil, tables)


def backward_call(scale, offsets, widths, live, spectrum, pupil, tables, measured, above, below, edges, waves):
    lamps = offsets.shape[0]
    side = spectrum.shape[-1]
    chunks = -(-lamps // GROUP)
    pairs = chunks * PAIRS
    return pl.pallas_call(
        partial(backward_kernel, scale),
        out_shape=(
            jax.ShapeDtypeStruct((BLOCKS, 2, side, PUP), F32),
            jax.ShapeDtypeStruct((2, PUP, PUP), F32),
        ),
        in_specs=[smem()] * 3 + [vmem()] * 7 + [hbm()],
        out_specs=(vmem(), vmem()),
        scratch_shapes=[
            pltpu.VMEM((BLOCKS, 2, side, PUP), F32),
            pltpu.VMEM((pairs, 2 * PUP, 2 * PUP), F32),
            pltpu.SMEM((lamps + GROUP,), jnp.int32),
            pltpu.SemaphoreType.DMA((chunks,)),
        ],
        compiler_params=pltpu.CompilerParams(vmem_limit_bytes=VMEM_LIMIT),
        name="backward",
    )(offsets, widths, live, spectrum, pupil, tables, measured, above, below, edges, waves)


def exchange_kernel(edge_ref, measured_ref, near_ref, above_ref, below_ref, send_sems, recv_sems):
    tiles = lax.axis_size("tile")
    me = lax.axis_index("tile")
    up, down = lax.rem(me + tiles - 1, tiles), lax.rem(me + 1, tiles)
    barrier = pltpu.get_barrier_semaphore()
    for other in (up, down):
        pl.semaphore_signal(barrier, inc=1, device_id={"tile": other}, device_id_type=MESH)
    pl.semaphore_wait(barrier, 2)

    def send(number, source, target, other):
        return pltpu.make_async_remote_copy(
            src_ref=source, dst_ref=target, send_sem=send_sems.at[number], recv_sem=recv_sems.at[number],
            device_id={"tile": other}, device_id_type=MESH,
        )

    copies = [
        send(0, edge_ref.at[0], near_ref.at[0], up),
        send(1, edge_ref.at[1], near_ref.at[1], down),
        send(2, measured_ref.at[:, pl.ds(0, OV)], below_ref, up),
        send(3, measured_ref.at[:, pl.ds(STRIDE - OV, OV)], above_ref, down),
    ]
    for copy in copies:
        copy.start()
    for copy in copies:
        copy.wait()


def exchange_call(edges, measured):
    lamps = measured.shape[0]
    rows = jax.ShapeDtypeStruct((lamps, OV, PUP), measured.dtype)
    return pl.pallas_call(
        exchange_kernel,
        out_shape=(jax.ShapeDtypeStruct(edges.shape, edges.dtype), rows, rows),
        in_specs=[hbm()] * 2,
        out_specs=(hbm(), hbm(), hbm()),
        scratch_shapes=[pltpu.SemaphoreType.DMA((4,)), pltpu.SemaphoreType.DMA((4,))],
        compiler_params=pltpu.CompilerParams(collective_id=1, has_side_effects=True),
        name="exchange",
    )(edges, measured)


LEVELS = 32767.0


def gather_kernel(groups, spec_ref, pupil_ref, spec_out, pupil_out, codes, scales, held, held_scales, held_pupil, send_sems, recv_sems):
    me = lax.axis_index("led")
    depth = spec_ref.shape[2] // groups
    width = pupil_ref.shape[1] // groups

    def peer(step):
        return lax.rem(me + step, groups)

    barrier = pltpu.get_barrier_semaphore()
    for step in range(1, groups):
        pl.semaphore_signal(barrier, inc=1, device_id={"led": peer(step)}, device_id_type=MESH)
    pl.semaphore_wait(barrier, groups - 1)

    def copies(step):
        other = peer(step)
        slot = groups - step
        sources = (codes.at[step - 1], scales.at[step - 1], pupil_ref.at[:, pl.ds(pl.multiple_of(other * width, width), width)])
        targets = (held.at[step - 1], held_scales.at[step - 1], held_pupil.at[step - 1])
        return [
            pltpu.make_async_remote_copy(
                src_ref=source, dst_ref=target, send_sem=send_sems.at[step - 1, kind], recv_sem=recv_sems.at[step - 1, kind],
                device_id={"led": other}, device_id_type=MESH,
            )
            for kind, (source, target) in enumerate(zip(sources, targets))
        ]

    for step in range(1, groups):
        start = pl.multiple_of(peer(step) * depth, depth)
        for block in range(BLOCKS):
            for part in range(2):
                x = spec_ref[block, part, pl.ds(start, depth), :]
                most = jnp.maximum(jnp.max(jnp.abs(x), axis=0, keepdims=True), 1e-30)
                codes[step - 1, block, part] = jnp.round(x * (LEVELS / most)).astype(jnp.int16)
                scales[step - 1, block * 2 + part : block * 2 + part + 1, :] = most * (1.0 / LEVELS)
        for copy in copies(step):
            copy.start()
    mine = pl.multiple_of(me * depth, depth)
    for part in range(2):
        pupil_out[part] = pupil_ref[part, pl.ds(pl.multiple_of(me * width, width), width)]
        for block in range(BLOCKS):
            spec_out[part, :, block * PUP : (block + 1) * PUP] = spec_ref[block, part, pl.ds(mine, depth), :]
    for step in range(1, groups):
        for copy in copies(step):
            copy.wait()
        for part in range(2):
            pupil_out[part] += held_pupil[step - 1, part]
            for block in range(BLOCKS):
                scale = held_scales[step - 1, block * 2 + part : block * 2 + part + 1, :]
                spec_out[part, :, block * PUP : (block + 1) * PUP] += held[step - 1, block, part].astype(F32) * scale


def gather_call(spec_part, pupil_part, groups):
    blocks, parts, side, _ = spec_part.shape
    depth, width = side // groups, PUP // groups
    others = groups - 1
    return pl.pallas_call(
        partial(gather_kernel, groups),
        out_shape=(
            jax.ShapeDtypeStruct((parts, depth, blocks * PUP), F32),
            jax.ShapeDtypeStruct((parts, width, PUP), F32),
        ),
        in_specs=[vmem(), vmem()],
        out_specs=(vmem(), vmem()),
        scratch_shapes=[
            pltpu.VMEM((others, blocks, parts, depth, PUP), jnp.int16),
            pltpu.VMEM((others, blocks * parts, PUP), F32),
            pltpu.VMEM((others, blocks, parts, depth, PUP), jnp.int16),
            pltpu.VMEM((others, blocks * parts, PUP), F32),
            pltpu.VMEM((others, parts, width, PUP), F32),
            pltpu.SemaphoreType.DMA((others, 3)),
            pltpu.SemaphoreType.DMA((others, 3)),
        ],
        compiler_params=pltpu.CompilerParams(
            collective_id=2, has_side_effects=True, vmem_limit_bytes=VMEM_LIMIT
        ),
        name="reduce_scatter",
    )(spec_part, pupil_part)


def on_device(tables, spectrum, pupil, offsets, widths, live, measured):
    groups = lax.axis_size("led")
    lamps = measured.shape[0]
    scale = 1.0 / math.sqrt(lamps * groups)
    spectrum, pupil, offsets = spectrum[0], pupil[0], offsets[0]
    waves, edges = forward_call(offsets, widths, live, spectrum, pupil, tables)
    near, above, below = exchange_call(edges, measured)
    spec_part, pupil_part = backward_call(
        scale, offsets, widths, live, spectrum, pupil, tables, measured, above, below, near, waves
    )
    spec_share, pupil_share = gather_call(spec_part, pupil_part, groups)
    return spec_share[None], pupil_share[None]


def solution(mesh):
    tables = dft_tables()

    def run(spectrum, pupil, offsets, widths, live, measured):
        return jax.shard_map(
            on_device,
            mesh=mesh,
            in_specs=(
                P(),
                P("tile", None, None, None),
                P("tile", None, None, None),
                P("tile", "led", None),
                P(),
                P("led"),
                P("led", "tile", None),
            ),
            out_specs=(P("tile", None, "led", None), P("tile", None, "led", None)),
            check_vma=False,
        )(jnp.asarray(tables), spectrum, pupil, offsets, widths, live, measured)

    return run
```

```python
from functools import partial
import math

import jax
import jax.numpy as jnp
import ml_dtypes
import numpy as np
from jax import lax
from jax.experimental import pallas as pl
from jax.experimental.pallas import tpu as pltpu
from jax.sharding import PartitionSpec as P

PUP = 128
OV = 16
HALF = 8
STRIDE = PUP - OV
BLOCKS = 4
MESH = pl.DeviceIdType.MESH
F32 = jnp.float32
BF16 = jnp.bfloat16
XS, YS = 4, 2
SPEC_ROWS = 512 // (XS * YS)
PUP_ROWS = PUP // (XS * YS)
ROWS_B = 4 * SPEC_ROWS
ROWS_A = ROWS_B + 2 * PUP_ROWS
LEVELS = 32767.0
PAIRS = 2
GROUP = 2 * PAIRS
VMEM_LIMIT = 63 * 1024 * 1024
GATHER_LIMIT = 62 * 1024 * 1024


def dft_tables():
    k = np.arange(PUP)
    angle = 2.0 * np.pi * ((k[:, None] * k[None, :]) % PUP) / PUP
    cosine, sine = np.cos(angle), np.sin(angle)
    inverse = np.block([[cosine, sine], [-sine, cosine]]) / PUP
    forward = np.block([[cosine, -sine], [sine, cosine]])
    parts = []
    for table in (inverse, forward):
        high = table.astype(ml_dtypes.bfloat16)
        low = (table - high.astype(np.float64)).astype(ml_dtypes.bfloat16)
        parts += [high, low]
    return np.stack(parts)


def split(x):
    high = x.astype(BF16)
    return high, (x - high.astype(F32)).astype(BF16)


def right_product(x, high, low):
    xh, xl = split(x)
    data = jnp.concatenate([xh, xl, xh], axis=1)
    table = jnp.concatenate([high, high, low], axis=0)
    return jnp.dot(data, table, preferred_element_type=F32)


def left_product(high, low, x):
    xh, xl = split(x)
    data = jnp.concatenate([xh, xl, xh], axis=0)
    table = jnp.concatenate([high, high, low], axis=1)
    return jnp.dot(table, data, preferred_element_type=F32)


def swap_blocks(x):
    top = jnp.concatenate([x[:PUP, :PUP], x[PUP:, :PUP]], axis=1)
    bottom = jnp.concatenate([x[:PUP, PUP:], x[PUP:, PUP:]], axis=1)
    return jnp.concatenate([top, bottom], axis=0)


def ramp_weights(widths_ref, tile, tiles):
    place = lax.broadcasted_iota(jnp.int32, (OV, PUP), 0).astype(F32)
    above = widths_ref[jnp.maximum(tile - 1, 0)].astype(F32)
    below = widths_ref[jnp.minimum(tile, tiles - 2)].astype(F32)
    top = 1.0 - jnp.clip(0.5 + (HALF - 0.5 - place) / above, 0.0, 1.0)
    bottom = jnp.clip(0.5 + (HALF - 0.5 - place) / below, 0.0, 1.0)
    ones = jnp.ones_like(place)
    return jnp.where(tile > 0, top, ones), jnp.where(tile < tiles - 1, bottom, ones)


def list_live(live_ref, order_ref):
    def body(led, count):
        order_ref[count] = led
        return count + live_ref[led]

    lamps = live_ref.shape[0]
    count = lax.fori_loop(0, lamps, body, jnp.int32(0))
    for extra in range(GROUP):
        order_ref[count + extra] = 0
    return count


def load_spectrum(spec_ref, planes):
    for block in range(BLOCKS):
        for part in range(2):
            planes[block, part] = spec_ref[part, :, block * PUP : (block + 1) * PUP].astype(F32)


def window_of(planes, row, col):
    first = col // PUP
    second = jnp.minimum(first + 1, BLOCKS - 1)
    lanes = lax.broadcasted_iota(jnp.int32, (PUP, PUP), 1)
    inside = lanes >= col % PUP
    return [
        jnp.where(inside, planes[first, part, pl.ds(row, PUP), :], planes[second, part, pl.ds(row, PUP), :])
        for part in range(2)
    ]


def forward_kernel(
    offsets_hbm, widths_hbm, spec_hbm, pupil_hbm, table_hbm, measured_hbm,
    wave_out, near, above, below,
    waves, edges, planes, offsets_ref, widths_ref, spec_ref, pupil_ref, table_ref,
    local_sems, wave_sems, send_sems, recv_sems, image_send, image_recv
):
    tiles = lax.axis_size("tile")
    tile = lax.axis_index("tile")
    up, down = lax.rem(tile + tiles - 1, tiles), lax.rem(tile + 1, tiles)
    steps = waves.shape[0] // GROUP
    local = [
        pltpu.make_async_copy(source, target, local_sems.at[number])
        for number, (source, target) in enumerate(
            (
                (offsets_hbm, offsets_ref),
                (widths_hbm, widths_ref),
                (spec_hbm, spec_ref),
                (pupil_hbm, pupil_ref),
                (table_hbm, table_ref),
            )
        )
    ]
    for copy in local:
        copy.start()
    barrier = pltpu.get_barrier_semaphore()
    for other in (up, down):
        pl.semaphore_signal(barrier, inc=1, device_id={"tile": other}, device_id_type=MESH)
    for copy in local[:3]:
        copy.wait()
    load_spectrum(spec_ref, planes)
    top, bottom = ramp_weights(widths_ref, tile, tiles)
    top2 = jnp.concatenate([top, top], axis=1)
    bottom2 = jnp.concatenate([bottom, bottom], axis=1)
    for copy in local[3:]:
        copy.wait()
    pl.semaphore_wait(barrier, 2)

    def remote(source, target, send_sem, recv_sem, other):
        return pltpu.make_async_remote_copy(
            src_ref=source, dst_ref=target, send_sem=send_sem, recv_sem=recv_sem,
            device_id={"tile": other}, device_id_type=MESH,
        )

    images = [
        remote(measured_hbm.at[:, pl.ds(0, OV)], below, image_send.at[0], image_recv.at[0], up),
        remote(measured_hbm.at[:, pl.ds(STRIDE - OV, OV)], above, image_send.at[1], image_recv.at[1], down),
    ]
    for copy in images:
        copy.start()

    def edge_copies(number):
        here = pl.ds(number * GROUP, GROUP)
        return [
            remote(edges.at[end, here], near.at[end, here], send_sems.at[end, number], recv_sems.at[end, number], other)
            for end, other in ((0, up), (1, down))
        ]

    def wave_copy(number):
        here = pl.ds(number * GROUP, GROUP)
        return pltpu.make_async_copy(waves.at[here], wave_out.at[here], wave_sems.at[number])

    def field_of(led):
        row, col = offsets_ref[0, led], offsets_ref[1, led]
        win_re, win_im = window_of(planes, row, col)
        shift = col % PUP
        pup_re = pltpu.roll(pupil_ref[0].astype(F32), shift, axis=1)
        pup_im = pltpu.roll(pupil_ref[1].astype(F32), shift, axis=1)
        return jnp.concatenate(
            [pup_re * win_re - pup_im * win_im, pup_re * win_im + pup_im * win_re], axis=1
        )

    def step(number, carry):
        for inner in range(PAIRS):
            pair = number * PAIRS + inner
            field = jnp.concatenate([field_of(2 * pair), field_of(2 * pair + 1)], axis=0)
            mixed = right_product(field, table_ref[0], table_ref[1])
            wave = left_product(table_ref[2], table_ref[3], swap_blocks(mixed))
            first = wave[:OV], wave[PUP : PUP + OV]
            last = wave[STRIDE:PUP], wave[PUP + STRIDE :]
            first = (top2 * (first[0] * first[0] + first[1] * first[1])).astype(BF16)
            last = (bottom2 * (last[0] * last[0] + last[1] * last[1])).astype(BF16)
            for side in range(2):
                lo = side * PUP
                led = 2 * pair + side
                waves[led] = wave[:, lo : lo + PUP]
                edges[0, led] = first[:, lo : lo + PUP]
                edges[1, led] = last[:, lo : lo + PUP]
        wave_copy(number).start()
        for copy in edge_copies(number):
            copy.start()
        return carry

    lax.fori_loop(0, steps, step, 0)

    def finish(number, carry):
        wave_copy(number).wait()
        for copy in edge_copies(number):
            copy.wait()
        return carry

    lax.fori_loop(0, steps, finish, 0)
    for copy in images:
        copy.wait()


def my_place():
    me = lax.axis_index("led")
    return me // XS, me % XS


def dest_of(line, place):
    return (line % YS) * XS + place % XS


def backward_kernel(
    scale, offsets_hbm, widths_hbm, live_hbm, spec_hbm, pupil_hbm, table_hbm, measured_hbm, above_hbm, below_hbm, edge_hbm, wave_hbm,
    codes_a_hbm, scales_a_hbm, own_a_hbm, codes_b_hbm, scales_b_hbm, own_b_hbm,
    spec_out, pupil_out, codes_a, scales_a, own_a, codes_b, scales_b, own_b, waves, planes, offsets_ref, widths_ref, live_ref, order_ref, spec_ref, pupil_ref, table_ref, measured_ref,
    above_ref, below_ref, edge_ref, sems, wave_sems, out_sems
):
    tiles = lax.axis_size("tile")
    tile = lax.axis_index("tile")
    local = [
        pltpu.make_async_copy(source, target, sems.at[number])
        for number, (source, target) in enumerate(
            (
                (offsets_hbm, offsets_ref),
                (widths_hbm, widths_ref),
                (live_hbm, live_ref),
                (spec_hbm, spec_ref),
                (pupil_hbm, pupil_ref),
                (table_hbm, table_ref),
                (measured_hbm, measured_ref),
                (above_hbm, above_ref),
                (below_hbm, below_ref),
                (edge_hbm, edge_ref),
            )
        )
    ]
    for copy in local:
        copy.start()

    for copy in local[:3]:
        copy.wait()
    count = list_live(live_ref, order_ref)
    steps = (count + GROUP - 1) // GROUP

    def wave_copy(slot):
        return pltpu.make_async_copy(wave_hbm.at[order_ref[slot]], waves.at[slot], wave_sems.at[slot])

    def fetch(slot, carry):
        wave_copy(slot).start()
        return carry

    lax.fori_loop(0, steps * GROUP, fetch, 0)

    spec_out[...] = jnp.zeros_like(spec_out)
    pupil_out[...] = jnp.zeros_like(pupil_out)
    local[3].wait()
    load_spectrum(spec_ref, planes)
    for copy in local[4:]:
        copy.wait()
    top, bottom = ramp_weights(widths_ref, tile, tiles)
    top2 = jnp.concatenate([top, top], axis=1)
    bottom2 = jnp.concatenate([bottom, bottom], axis=1)
    rows = lax.broadcasted_iota(jnp.int32, (OV, 2 * PUP), 0)
    top_grad = jnp.where((tile > 0) | (rows >= HALF), 2.0 * top2, 0.0)
    bottom_grad = jnp.where((tile < tiles - 1) | (rows < HALF), 2.0 * bottom2, 0.0)
    has_above = tile > 0
    has_below = tile < tiles - 1
    lanes = lax.broadcasted_iota(jnp.int32, (PUP, PUP), 1)

    def edges_of(end, leds):
        return jnp.concatenate([edge_ref[end, led].astype(F32) for led in leds], axis=1)

    def images(ref, leds, low, high):
        return jnp.concatenate([ref[led, low:high].astype(F32) for led in leds], axis=1)

    def step(number, carry):
        for inner in range(GROUP):
            wave_copy(number * GROUP + inner).wait()
        for inner in range(PAIRS):
            pair = number * PAIRS + inner
            leds = order_ref[2 * pair], order_ref[2 * pair + 1]
            side_of = lax.broadcasted_iota(jnp.int32, (1, 2 * PUP), 1) // PUP
            alive = jnp.where(2 * pair + side_of < count, scale, 0.0)
            wave = jnp.concatenate([waves[2 * pair], waves[2 * pair + 1]], axis=1)
            wave_re, wave_im = wave[:PUP], wave[PUP:]
            intensity = wave_re * wave_re + wave_im * wave_im
            own = images(measured_ref, leds, 0, STRIDE)
            upper = images(above_ref, leds, OV - HALF, OV)
            lower = images(below_ref, leds, 0, HALF)
            near_top = jnp.where(has_above, edges_of(1, leds), 0.0)
            near_bottom = jnp.where(has_below, edges_of(0, leds), 0.0)
            first = top_grad * (top2 * intensity[:OV] + near_top - jnp.concatenate([upper, own[: OV - HALF]], axis=0))
            middle = 2.0 * (intensity[OV:STRIDE] - own[HALF : STRIDE - HALF])
            last = bottom_grad * (bottom2 * intensity[STRIDE:] + near_bottom - jnp.concatenate([own[STRIDE - HALF :], lower], axis=0))
            grad = alive * jnp.concatenate([first, middle, last], axis=0)
            grad_wave = jnp.concatenate([grad * wave_re, grad * wave_im], axis=0)
            back = right_product(swap_blocks(grad_wave), table_ref[2], table_ref[3])
            grad_field = left_product(table_ref[0], table_ref[1], swap_blocks(back))
            for side in range(2):
                led = leds[side]
                row, col = offsets_ref[0, led], offsets_ref[1, led]
                shift = col % PUP
                lo = side * PUP
                grad_re = grad_field[:PUP, lo : lo + PUP]
                grad_im = grad_field[PUP:, lo : lo + PUP]
                pup_re = pltpu.roll(pupil_ref[0].astype(F32), shift, axis=1)
                pup_im = pltpu.roll(pupil_ref[1].astype(F32), shift, axis=1)
                win_re, win_im = window_of(planes, row, col)
                pieces = (pup_re * grad_re + pup_im * grad_im, pup_re * grad_im - pup_im * grad_re)
                shares = (win_re * grad_re + win_im * grad_im, win_re * grad_im - win_im * grad_re)
                first_block = col // PUP
                second_block = jnp.minimum(first_block + 1, BLOCKS - 1)
                inside = lanes >= shift
                for part in range(2):
                    here_rows = pl.ds(row, PUP)
                    pupil_out[part] += pltpu.roll(shares[part], PUP - shift, axis=1)
                    spec_out[first_block, part, here_rows, :] += jnp.where(inside, pieces[part], 0.0)
                    spec_out[second_block, part, here_rows, :] += jnp.where(inside, 0.0, pieces[part])
        return carry

    lax.fori_loop(0, steps, step, 0)
    line, place = my_place()
    depth = SPEC_ROWS
    sends = []

    def keep(source, target):
        sends.append(pltpu.make_async_copy(source, target, out_sems.at[len(sends)]))
        sends[-1].start()

    def pieces_of(half, dest):
        rows = pl.ds(pl.multiple_of(dest * depth, depth), depth)
        pieces = [spec_out[2 * half + block, part, rows, :] for block in range(2) for part in range(2)]
        if half == 0:
            width = PUP_ROWS
            rows = pl.ds(pl.multiple_of(dest * width, width), width)
            pieces += [pupil_out[part, rows, :] for part in range(2)]
        return pieces

    def encode(pieces, codes, scales):
        start = 0
        for number, piece in enumerate(pieces):
            most = jnp.maximum(jnp.max(jnp.abs(piece), axis=0, keepdims=True), 1e-30)
            stop = start + piece.shape[0]
            codes[start:stop, :] = jnp.round(piece * (LEVELS / most)).astype(jnp.int16)
            scales[number : number + 1, :] = most * (1.0 / LEVELS)
            start = stop

    def store(pieces, target):
        start = 0
        for piece in pieces:
            stop = start + piece.shape[0]
            target[start:stop, :] = piece
            start = stop

    for hop in range(XS):
        encode(pieces_of(1, dest_of(line + 1, place + 1 + hop)), codes_b.at[hop], scales_b.at[hop])
        keep(codes_b.at[hop], codes_b_hbm.at[hop])
    for turn in range(2):
        for hop in range(XS - 1):
            encode(pieces_of(0, dest_of(line + 1 + turn, place + 1 + hop)), codes_a.at[turn, hop], scales_a.at[turn, hop])
            keep(codes_a.at[turn, hop], codes_a_hbm.at[turn, hop])
        store(pieces_of(0, dest_of(line + 1 + turn, place)), own_a.at[turn])
    for hop in range(XS):
        store(pieces_of(1, dest_of(line, place + 1 + hop)), own_b.at[hop])
    keep(scales_a, scales_a_hbm)
    keep(scales_b, scales_b_hbm)
    keep(own_a, own_a_hbm)
    keep(own_b, own_b_hbm)
    for copy in sends:
        copy.wait()


def vmem():
    return pl.BlockSpec(memory_space=pltpu.VMEM)


def smem():
    return pl.BlockSpec(memory_space=pltpu.SMEM)


def hbm():
    return pl.BlockSpec(memory_space=pltpu.HBM)


def shape(dims, dtype):
    return jax.ShapeDtypeStruct(dims, dtype)


def forward_call(offsets, widths, spectrum, pupil, tables, measured):
    lamps = measured.shape[0]
    side = spectrum.shape[-1]
    rows = shape((lamps, OV, PUP), measured.dtype)
    wave = (lamps, 2 * PUP, PUP)
    edge = (2, lamps, OV, PUP)
    chunks = lamps // GROUP
    return pl.pallas_call(
        forward_kernel,
        out_shape=(shape(wave, F32), shape(edge, BF16), rows, rows),
        in_specs=[hbm()] * 6,
        out_specs=(hbm(),) * 4,
        scratch_shapes=[
            pltpu.VMEM(wave, F32),
            pltpu.VMEM(edge, BF16),
            pltpu.VMEM((BLOCKS, 2, side, PUP), F32),
            pltpu.SMEM(offsets.shape, jnp.int32),
            pltpu.SMEM(widths.shape, jnp.int32),
            pltpu.VMEM(spectrum.shape, spectrum.dtype),
            pltpu.VMEM(pupil.shape, pupil.dtype),
            pltpu.VMEM(tables.shape, tables.dtype),
            pltpu.SemaphoreType.DMA((5,)),
            pltpu.SemaphoreType.DMA((chunks,)),
            pltpu.SemaphoreType.DMA((2, chunks)),
            pltpu.SemaphoreType.DMA((2, chunks)),
            pltpu.SemaphoreType.DMA((2,)),
            pltpu.SemaphoreType.DMA((2,)),
        ],
        compiler_params=pltpu.CompilerParams(
            collective_id=1, has_side_effects=True, vmem_limit_bytes=VMEM_LIMIT
        ),
        name="forward",
    )(offsets, widths, spectrum, pupil, tables, measured)


UNITS = (
    ((2, XS - 1, ROWS_A, PUP), jnp.int16),
    ((2, XS - 1, 8, PUP), F32),
    ((2, ROWS_A, PUP), F32),
    ((XS, ROWS_B, PUP), jnp.int16),
    ((XS, 8, PUP), F32),
    ((XS, ROWS_B, PUP), F32),
)


def backward_call(scale, offsets, widths, live, spectrum, pupil, tables, measured, above, below, edges, waves):
    lamps = measured.shape[0]
    side = spectrum.shape[-1]
    planes = pltpu.VMEM((BLOCKS, 2, side, PUP), F32)
    return pl.pallas_call(
        partial(backward_kernel, scale),
        out_shape=tuple(shape(*unit) for unit in UNITS),
        in_specs=[hbm()] * 11,
        out_specs=(hbm(),) * 6,
        scratch_shapes=[
            planes,
            pltpu.VMEM(pupil.shape, F32),
            *(pltpu.VMEM(*unit) for unit in UNITS),
            pltpu.VMEM(waves.shape, F32),
            planes,
            pltpu.SMEM(offsets.shape, jnp.int32),
            pltpu.SMEM(widths.shape, jnp.int32),
            pltpu.SMEM(live.shape, jnp.int32),
            pltpu.SMEM((lamps + GROUP,), jnp.int32),
            pltpu.VMEM(spectrum.shape, spectrum.dtype),
            pltpu.VMEM(pupil.shape, pupil.dtype),
            pltpu.VMEM(tables.shape, tables.dtype),
            pltpu.VMEM(measured.shape, measured.dtype),
            pltpu.VMEM(above.shape, above.dtype),
            pltpu.VMEM(below.shape, below.dtype),
            pltpu.VMEM(edges.shape, edges.dtype),
            pltpu.SemaphoreType.DMA((10,)),
            pltpu.SemaphoreType.DMA((lamps,)),
            pltpu.SemaphoreType.DMA((14,)),
        ],
        compiler_params=pltpu.CompilerParams(vmem_limit_bytes=VMEM_LIMIT),
        name="backward",
    )(offsets, widths, live, spectrum, pupil, tables, measured, above, below, edges, waves)


def gather_kernel(
    codes_a, scales_a, own_a_hbm, codes_b, scales_b, own_b_hbm, spec_out, pupil_out,
    own_a, own_b, held_a, held_scales_a, held_b, held_scales_b, code_a2, scale_a2, held_a2, held_scales_a2,
    codes_b2, scales_b2, held_b2, held_scales_b2, local_sems, send_sems, recv_sems
):
    line, place = my_place()
    local = [
        pltpu.make_async_copy(own_a_hbm, own_a, local_sems.at[0]),
        pltpu.make_async_copy(own_b_hbm, own_b, local_sems.at[1]),
    ]
    for copy in local:
        copy.start()
    opposite = dest_of(line + 1, place)
    beside = [dest_of(line, place + 1 + hop) for hop in range(XS - 1)]
    barrier = pltpu.get_barrier_semaphore()
    for other in [opposite, *beside]:
        pl.semaphore_signal(barrier, inc=1, device_id={"led": other}, device_id_type=MESH)
    pl.semaphore_wait(barrier, XS)
    used = [0]

    def send(source, target, scale_source, scale_target, other):
        pair = []
        for src, dst in ((source, target), (scale_source, scale_target)):
            number = used[0]
            used[0] += 1
            pair.append(
                pltpu.make_async_remote_copy(
                    src_ref=src, dst_ref=dst, send_sem=send_sems.at[number], recv_sem=recv_sems.at[number],
                    device_id={"led": other}, device_id_type=MESH,
                )
            )
            pair[-1].start()
        return pair

    first_a = [[None] * (XS - 1), [None] * (XS - 1)]
    first_b = [None] * XS
    for hop in range(XS):
        first_b[hop] = send(codes_b.at[hop], held_b.at[hop], scales_b.at[hop], held_scales_b.at[hop], opposite)
        if hop < XS - 1:
            first_a[0][hop] = send(
                codes_a.at[0, hop], held_a.at[0, hop], scales_a.at[0, hop], held_scales_a.at[0, hop], beside[hop]
            )
    for hop in range(XS - 1):
        first_a[1][hop] = send(
            codes_a.at[1, hop], held_a.at[1, hop], scales_a.at[1, hop], held_scales_a.at[1, hop], beside[hop]
        )
    for copy in local:
        copy.wait()

    def arrived(pair):
        for copy in pair:
            copy.wait()

    bounds_b = [(number * SPEC_ROWS, (number + 1) * SPEC_ROWS) for number in range(4)]
    bounds_a = bounds_b + [(ROWS_B + part * PUP_ROWS, ROWS_B + (part + 1) * PUP_ROWS) for part in range(2)]

    def total(own, parts, number, start, stop):
        value = own[start:stop, :]
        for codes, scales in parts:
            value += codes[start:stop, :].astype(F32) * scales[number : number + 1, :]
        return value

    def encode(own, parts, bounds, codes, scales):
        for number, (start, stop) in enumerate(bounds):
            value = total(own, parts, number, start, stop)
            most = jnp.maximum(jnp.max(jnp.abs(value), axis=0, keepdims=True), 1e-30)
            codes[start:stop, :] = jnp.round(value * (LEVELS / most)).astype(jnp.int16)
            scales[number : number + 1, :] = most * (1.0 / LEVELS)

    second_b = [None] * (XS - 1)

    def pass_on(hop):
        arrived(first_b[hop])
        parts = [(held_b.at[hop], held_scales_b.at[hop])]
        encode(own_b.at[hop], parts, bounds_b, codes_b2.at[hop], scales_b2.at[hop])
        second_b[hop] = send(codes_b2.at[hop], held_b2.at[hop], scales_b2.at[hop], held_scales_b2.at[hop], beside[hop])

    pass_on(0)
    pass_on(1)
    for hop in range(XS - 1):
        arrived(first_a[0][hop])
    parts = [(held_a.at[0, hop], held_scales_a.at[0, hop]) for hop in range(XS - 1)]
    encode(own_a.at[0], parts, bounds_a, code_a2, scale_a2)
    second_a = send(code_a2, held_a2, scale_a2, held_scales_a2, opposite)
    pass_on(2)
    for hop in range(XS - 1):
        arrived(first_a[1][hop])
    arrived(second_a)
    parts = [(held_a.at[1, hop], held_scales_a.at[1, hop]) for hop in range(XS - 1)] + [(held_a2, held_scales_a2)]
    for number, (start, stop) in enumerate(bounds_a):
        value = total(own_a.at[1], parts, number, start, stop)
        if number < 4:
            block, part = number // 2, number % 2
            spec_out[part, :, block * PUP : (block + 1) * PUP] = value
        else:
            pupil_out[number - 4] = value
    arrived(first_b[XS - 1])
    for hop in range(XS - 1):
        arrived(second_b[hop])
    parts = [(held_b.at[XS - 1], held_scales_b.at[XS - 1])]
    parts += [(held_b2.at[hop], held_scales_b2.at[hop]) for hop in range(XS - 1)]
    for number, (start, stop) in enumerate(bounds_b):
        block, part = 2 + number // 2, number % 2
        spec_out[part, :, block * PUP : (block + 1) * PUP] = total(own_b.at[XS - 1], parts, number, start, stop)


def gather_call(codes_a, scales_a, own_a, codes_b, scales_b, own_b):
    moved = 2 * (2 * (XS - 1) + XS + 1 + XS - 1)
    code2 = pltpu.VMEM((ROWS_A, PUP), jnp.int16)
    scale2 = pltpu.VMEM((8, PUP), F32)
    codes2 = pltpu.VMEM((XS - 1, ROWS_B, PUP), jnp.int16)
    scales2 = pltpu.VMEM((XS - 1, 8, PUP), F32)
    return pl.pallas_call(
        gather_kernel,
        out_shape=(shape((2, SPEC_ROWS, BLOCKS * PUP), F32), shape((2, PUP_ROWS, PUP), F32)),
        in_specs=[hbm()] * 6,
        out_specs=(vmem(), vmem()),
        scratch_shapes=[
            pltpu.VMEM(own_a.shape, F32),
            pltpu.VMEM(own_b.shape, F32),
            pltpu.VMEM(codes_a.shape, codes_a.dtype),
            pltpu.VMEM(scales_a.shape, F32),
            pltpu.VMEM(codes_b.shape, codes_b.dtype),
            pltpu.VMEM(scales_b.shape, F32),
            code2,
            scale2,
            code2,
            scale2,
            codes2,
            scales2,
            codes2,
            scales2,
            pltpu.SemaphoreType.DMA((2,)),
            pltpu.SemaphoreType.DMA((moved,)),
            pltpu.SemaphoreType.DMA((moved,)),
        ],
        compiler_params=pltpu.CompilerParams(
            collective_id=2, has_side_effects=True, vmem_limit_bytes=GATHER_LIMIT
        ),
        name="reduce_scatter",
    )(codes_a, scales_a, own_a, codes_b, scales_b, own_b)


def on_device(tables, spectrum, pupil, offsets, widths, live, measured):
    groups = lax.axis_size("led")
    lamps = measured.shape[0]
    scale = 1.0 / math.sqrt(lamps * groups)
    spectrum, pupil, offsets = spectrum[0], pupil[0], offsets[0].T
    waves, near, above, below = forward_call(offsets, widths, spectrum, pupil, tables, measured)
    parts = backward_call(
        scale, offsets, widths, live, spectrum, pupil, tables, measured, above, below, near, waves
    )
    spec_share, pupil_share = gather_call(*parts)
    return spec_share[None], pupil_share[None]


def solution(mesh):
    tables = dft_tables()

    def run(spectrum, pupil, offsets, widths, live, measured):
        return jax.shard_map(
            on_device,
            mesh=mesh,
            in_specs=(
                P(),
                P("tile", None, None, None),
                P("tile", None, None, None),
                P("tile", "led", None),
                P(),
                P("led"),
                P("led", "tile", None),
            ),
            out_specs=(P("tile", None, "led", None), P("tile", None, "led", None)),
            check_vma=False,
        )(jnp.asarray(tables), spectrum, pupil, offsets, widths, live, measured)

    return run
```

```python
from functools import partial
import math

import jax
import jax.numpy as jnp
import ml_dtypes
import numpy as np
from jax import lax
from jax.experimental import pallas as pl
from jax.experimental.pallas import tpu as pltpu
from jax.sharding import PartitionSpec as P

PUP = 128
OV = 16
HALF = 8
STRIDE = PUP - OV
BLOCKS = 4
MESH = pl.DeviceIdType.MESH
F32 = jnp.float32
BF16 = jnp.bfloat16
XS, YS = 4, 2
SPEC_ROWS = 512 // (XS * YS)
PUP_ROWS = PUP // (XS * YS)
CHUNKS = [(block, part) for block in range(BLOCKS) for part in range(2)]
CHUNKS_A, CHUNKS_B = CHUNKS[:3], CHUNKS[3:]
BOUNDS_B = [(number * SPEC_ROWS, (number + 1) * SPEC_ROWS) for number in range(len(CHUNKS_B))]
ROWS_B = len(CHUNKS_B) * SPEC_ROWS
BOUNDS_A = BOUNDS_B[: len(CHUNKS_A)]
BOUNDS_A += [(len(CHUNKS_A) * SPEC_ROWS + part * PUP_ROWS, len(CHUNKS_A) * SPEC_ROWS + (part + 1) * PUP_ROWS) for part in range(2)]
ROWS_A = len(CHUNKS_A) * SPEC_ROWS + 2 * PUP_ROWS
SENT_A, SENT_B = 2 * (XS - 1), XS
CODE_ROWS = SENT_A * ROWS_A + SENT_B * ROWS_B
OWN_ROWS = 2 * ROWS_A + SENT_B * ROWS_B
FLOAT_ROWS = OWN_ROWS + 8 * (SENT_A + SENT_B)
LEVELS = 32767.0
FORWARD_PAIRS = 7
PAIRS = 4
GROUP = 2 * PAIRS
VMEM_LIMIT = 63 * 1024 * 1024
GATHER_LIMIT = 213 * 256 * 1024


def dft_tables():
    k = np.arange(PUP)
    angle = 2.0 * np.pi * ((k[:, None] * k[None, :]) % PUP) / PUP
    cosine, sine = np.cos(angle), np.sin(angle)
    inverse = np.block([[cosine, sine], [-sine, cosine]]) / PUP
    forward = np.block([[cosine, -sine], [sine, cosine]])
    parts = []
    for table in (inverse, forward):
        high = table.astype(ml_dtypes.bfloat16)
        low = (table - high.astype(np.float64)).astype(ml_dtypes.bfloat16)
        parts += [high, low]
    return np.stack(parts)


def split(x):
    high = x.astype(BF16)
    return high, (x - high.astype(F32)).astype(BF16)


def right_product(x, high, low):
    xh, xl = split(x)
    data = jnp.concatenate([xh, xl, xh], axis=1)
    table = jnp.concatenate([high, high, low], axis=0)
    return jnp.dot(data, table, preferred_element_type=F32)


def left_product(high, low, x):
    xh, xl = split(x)
    data = jnp.concatenate([xh, xl, xh], axis=0)
    table = jnp.concatenate([high, high, low], axis=1)
    return jnp.dot(table, data, preferred_element_type=F32)


def swap_blocks(x):
    top = jnp.concatenate([x[:PUP, :PUP], x[PUP:, :PUP]], axis=1)
    bottom = jnp.concatenate([x[:PUP, PUP:], x[PUP:, PUP:]], axis=1)
    return jnp.concatenate([top, bottom], axis=0)


def ramp_weights(widths_ref, tile, tiles):
    place = lax.broadcasted_iota(jnp.int32, (OV, PUP), 0).astype(F32)
    above = widths_ref[jnp.maximum(tile - 1, 0)].astype(F32)
    below = widths_ref[jnp.minimum(tile, tiles - 2)].astype(F32)
    top = 1.0 - jnp.clip(0.5 + (HALF - 0.5 - place) / above, 0.0, 1.0)
    bottom = jnp.clip(0.5 + (HALF - 0.5 - place) / below, 0.0, 1.0)
    ones = jnp.ones_like(place)
    return jnp.where(tile > 0, top, ones), jnp.where(tile < tiles - 1, bottom, ones)


def list_live(live_ref, order_ref):
    def body(led, count):
        order_ref[count] = led
        return count + live_ref[led]

    lamps = live_ref.shape[0]
    count = lax.fori_loop(0, lamps, body, jnp.int32(0))
    for extra in range(GROUP):
        order_ref[count + extra] = 0
    return count


def load_spectrum(spec_ref, planes):
    for block in range(BLOCKS):
        for part in range(2):
            planes[block, part] = spec_ref[part, :, block * PUP : (block + 1) * PUP].astype(F32)


def window_of(planes, row, col):
    first = col // PUP
    second = jnp.minimum(first + 1, BLOCKS - 1)
    lanes = lax.broadcasted_iota(jnp.int32, (PUP, PUP), 1)
    inside = lanes >= col % PUP
    return [
        jnp.where(inside, planes[first, part, pl.ds(row, PUP), :], planes[second, part, pl.ds(row, PUP), :])
        for part in range(2)
    ]


def forward_kernel(
    offsets_hbm, widths_hbm, spec_hbm, pupil_hbm, table_hbm, measured_hbm,
    wave_out, near, above, below,
    waves, edges, planes, offsets_ref, widths_ref, spec_ref, pupil_ref, table_ref,
    local_sems, wave_sems, send_sems, recv_sems, image_send, image_recv
):
    tiles = lax.axis_size("tile")
    tile = lax.axis_index("tile")
    up, down = jnp.maximum(tile - 1, 0), jnp.minimum(tile + 1, tiles - 1)
    width = 2 * FORWARD_PAIRS
    steps = waves.shape[0] // width
    local = [
        pltpu.make_async_copy(source, target, local_sems.at[number])
        for number, (source, target) in enumerate(
            (
                (offsets_hbm, offsets_ref),
                (widths_hbm, widths_ref),
                (spec_hbm, spec_ref),
                (pupil_hbm, pupil_ref),
                (table_hbm, table_ref),
            )
        )
    ]
    for copy in local:
        copy.start()
    barrier = pltpu.get_barrier_semaphore()
    has_above, has_below = tile > 0, tile < tiles - 1

    def signal(other):
        pl.semaphore_signal(barrier, inc=1, device_id={"tile": other}, device_id_type=MESH)

    pl.when(has_above)(lambda: signal(up))
    pl.when(has_below)(lambda: signal(down))
    for copy in local[:3]:
        copy.wait()
    load_spectrum(spec_ref, planes)
    top, bottom = ramp_weights(widths_ref, tile, tiles)
    top2 = jnp.concatenate([top, top], axis=1)
    bottom2 = jnp.concatenate([bottom, bottom], axis=1)
    for copy in local[3:]:
        copy.wait()
    pl.semaphore_wait(barrier, has_above.astype(jnp.int32) + has_below.astype(jnp.int32))

    def remote(source, target, send_sem, recv_sem, other):
        return pltpu.make_async_remote_copy(
            src_ref=source, dst_ref=target, send_sem=send_sem, recv_sem=recv_sem,
            device_id={"tile": other}, device_id_type=MESH,
        )

    sides = ((0, has_above, up), (1, has_below, down))
    strips = ((pl.ds(0, OV), below), (pl.ds(STRIDE - OV, OV), above))

    def image_copy(end, other):
        rows, target = strips[end]
        return remote(measured_hbm.at[:, rows], target, image_send.at[end], image_recv.at[end], other)

    def edge_copy(end, other, number):
        here = pl.ds(number * width, width)
        return remote(edges.at[end, here], near.at[end, here], send_sems.at[end, number], recv_sems.at[end, number], other)

    for end, present, other in sides:
        pl.when(present)(lambda: image_copy(end, other).start())

    def wave_copy(number):
        here = pl.ds(number * width, width)
        return pltpu.make_async_copy(waves.at[here], wave_out.at[here], wave_sems.at[number])

    def field_of(led):
        row, col = offsets_ref[0, led], offsets_ref[1, led]
        win_re, win_im = window_of(planes, row, col)
        shift = col % PUP
        pup_re = pltpu.roll(pupil_ref[0].astype(F32), shift, axis=1)
        pup_im = pltpu.roll(pupil_ref[1].astype(F32), shift, axis=1)
        return jnp.concatenate(
            [pup_re * win_re - pup_im * win_im, pup_re * win_im + pup_im * win_re], axis=1
        )

    def step(number, carry):
        for inner in range(FORWARD_PAIRS):
            pair = number * FORWARD_PAIRS + inner
            field = jnp.concatenate([field_of(2 * pair), field_of(2 * pair + 1)], axis=0)
            mixed = right_product(field, table_ref[0], table_ref[1])
            wave = left_product(table_ref[2], table_ref[3], swap_blocks(mixed))
            first = wave[:OV], wave[PUP : PUP + OV]
            last = wave[STRIDE:PUP], wave[PUP + STRIDE :]
            first = (top2 * (first[0] * first[0] + first[1] * first[1])).astype(BF16)
            last = (bottom2 * (last[0] * last[0] + last[1] * last[1])).astype(BF16)
            for side in range(2):
                lo = side * PUP
                led = 2 * pair + side
                waves[led] = wave[:, lo : lo + PUP]
                edges[0, led] = first[:, lo : lo + PUP]
                edges[1, led] = last[:, lo : lo + PUP]
        wave_copy(number).start()
        for end, present, other in sides:
            pl.when(present)(lambda: edge_copy(end, other, number).start())
        return carry

    lax.fori_loop(0, steps, step, 0)

    def finish(number, carry):
        wave_copy(number).wait()
        for end, present, other in sides:
            pl.when(present)(lambda: edge_copy(end, other, number).wait_send())
            pl.when(sides[1 - end][1])(lambda: edge_copy(end, other, number).wait_recv())
        return carry

    lax.fori_loop(0, steps, finish, 0)
    for end, present, other in sides:
        pl.when(present)(lambda: image_copy(end, other).wait_send())
        pl.when(sides[1 - end][1])(lambda: image_copy(end, other).wait_recv())


def my_place():
    me = lax.axis_index("led")
    return me // XS, me % XS


def dest_of(line, place):
    return (line % YS) * XS + place % XS


def backward_kernel(
    scale, offsets_hbm, widths_hbm, live_hbm, spec_hbm, pupil_hbm, table_hbm, measured_hbm, above_hbm, below_hbm, edge_hbm, wave_hbm,
    code_hbm, float_hbm,
    spec_out, pupil_out, codes, floats, waves, planes, offsets_ref, widths_ref, live_ref, order_ref, spec_ref, pupil_ref, table_ref, measured_ref,
    above_ref, below_ref, edge_ref, sems, wave_sems, out_sems
):
    tiles = lax.axis_size("tile")
    tile = lax.axis_index("tile")
    local = [
        pltpu.make_async_copy(source, target, sems.at[number])
        for number, (source, target) in enumerate(
            (
                (offsets_hbm, offsets_ref),
                (widths_hbm, widths_ref),
                (live_hbm, live_ref),
                (spec_hbm, spec_ref),
                (pupil_hbm, pupil_ref),
                (table_hbm, table_ref),
                (measured_hbm, measured_ref),
                (above_hbm, above_ref),
                (below_hbm, below_ref),
                (edge_hbm, edge_ref),
            )
        )
    ]
    for copy in local:
        copy.start()

    for copy in local[:3]:
        copy.wait()
    count = list_live(live_ref, order_ref)
    steps = (count + GROUP - 1) // GROUP

    def wave_copy(slot):
        return pltpu.make_async_copy(wave_hbm.at[order_ref[slot]], waves.at[slot], wave_sems.at[slot])

    def fetch(slot, carry):
        wave_copy(slot).start()
        return carry

    lax.fori_loop(0, steps * GROUP, fetch, 0)

    spec_out[...] = jnp.zeros_like(spec_out)
    pupil_out[...] = jnp.zeros_like(pupil_out)
    local[3].wait()
    load_spectrum(spec_ref, planes)
    for copy in local[4:]:
        copy.wait()
    top, bottom = ramp_weights(widths_ref, tile, tiles)
    top2 = jnp.concatenate([top, top], axis=1)
    bottom2 = jnp.concatenate([bottom, bottom], axis=1)
    rows = lax.broadcasted_iota(jnp.int32, (OV, 2 * PUP), 0)
    top_inside = (tile > 0) | (rows >= HALF)
    bottom_inside = (tile < tiles - 1) | (rows < HALF)
    has_above = tile > 0
    has_below = tile < tiles - 1
    lanes = lax.broadcasted_iota(jnp.int32, (PUP, PUP), 1)

    def edges_of(end, leds):
        return jnp.concatenate([edge_ref[end, led].astype(F32) for led in leds], axis=1)

    def images(ref, leds, low, high):
        return jnp.concatenate([ref[led, low:high].astype(F32) for led in leds], axis=1)

    def step(number, carry):
        for inner in range(GROUP):
            wave_copy(number * GROUP + inner).wait()
        for inner in range(PAIRS):
            pair = number * PAIRS + inner
            leds = order_ref[2 * pair], order_ref[2 * pair + 1]
            side_of = lax.broadcasted_iota(jnp.int32, (1, 2 * PUP), 1) // PUP
            alive = jnp.where(2 * pair + side_of < count, scale, 0.0)
            wave = jnp.concatenate([waves[2 * pair], waves[2 * pair + 1]], axis=1)
            wave_re, wave_im = wave[:PUP], wave[PUP:]
            intensity = wave_re * wave_re + wave_im * wave_im
            own = images(measured_ref, leds, 0, STRIDE)
            upper = images(above_ref, leds, OV - HALF, OV)
            lower = images(below_ref, leds, 0, HALF)
            near_top = jnp.where(has_above, edges_of(1, leds), 0.0)
            near_bottom = jnp.where(has_below, edges_of(0, leds), 0.0)
            first = 2.0 * top2 * (top2 * intensity[:OV] + near_top - jnp.concatenate([upper, own[: OV - HALF]], axis=0))
            middle = 2.0 * (intensity[OV:STRIDE] - own[HALF : STRIDE - HALF])
            last = 2.0 * bottom2 * (bottom2 * intensity[STRIDE:] + near_bottom - jnp.concatenate([own[STRIDE - HALF :], lower], axis=0))
            grad = alive * jnp.concatenate(
                [jnp.where(top_inside, first, 0.0), middle, jnp.where(bottom_inside, last, 0.0)], axis=0
            )
            grad_wave = jnp.concatenate([grad * wave_re, grad * wave_im], axis=0)
            back = right_product(swap_blocks(grad_wave), table_ref[2], table_ref[3])
            grad_field = left_product(table_ref[0], table_ref[1], swap_blocks(back))
            for side in range(2):
                led = leds[side]
                row, col = offsets_ref[0, led], offsets_ref[1, led]
                shift = col % PUP
                lo = side * PUP
                grad_re = grad_field[:PUP, lo : lo + PUP]
                grad_im = grad_field[PUP:, lo : lo + PUP]
                pup_re = pltpu.roll(pupil_ref[0].astype(F32), shift, axis=1)
                pup_im = pltpu.roll(pupil_ref[1].astype(F32), shift, axis=1)
                win_re, win_im = window_of(planes, row, col)
                pieces = (pup_re * grad_re + pup_im * grad_im, pup_re * grad_im - pup_im * grad_re)
                shares = (win_re * grad_re + win_im * grad_im, win_re * grad_im - win_im * grad_re)
                first_block = col // PUP
                second_block = jnp.minimum(first_block + 1, BLOCKS - 1)
                inside = lanes >= shift
                for part in range(2):
                    here_rows = pl.ds(row, PUP)
                    pupil_out[part] += pltpu.roll(shares[part], PUP - shift, axis=1)
                    spec_out[first_block, part, here_rows, :] += jnp.where(inside, pieces[part], 0.0)
                    spec_out[second_block, part, here_rows, :] += jnp.where(inside, 0.0, pieces[part])
        return carry

    lax.fori_loop(0, steps, step, 0)
    line, place = my_place()
    sends = []

    def keep(source, target):
        sends.append(pltpu.make_async_copy(source, target, out_sems.at[len(sends)]))
        sends[-1].start()

    def pieces_of(chunks, dest):
        rows = pl.ds(pl.multiple_of(dest * SPEC_ROWS, SPEC_ROWS), SPEC_ROWS)
        pieces = [spec_out[block, part, rows, :] for block, part in chunks]
        if chunks is CHUNKS_A:
            rows = pl.ds(pl.multiple_of(dest * PUP_ROWS, PUP_ROWS), PUP_ROWS)
            pieces += [pupil_out[part, rows, :] for part in range(2)]
        return pieces

    code_rows, float_rows, scale_rows = [0], [0], [OWN_ROWS]

    def encode(pieces):
        begin = code_rows[0]
        for number, piece in enumerate(pieces):
            most = jnp.maximum(jnp.max(jnp.abs(piece), axis=0, keepdims=True), 1e-30)
            start, stop = code_rows[0], code_rows[0] + piece.shape[0]
            codes[start:stop, :] = jnp.round(piece * (LEVELS / most)).astype(jnp.int16)
            floats[scale_rows[0] + number : scale_rows[0] + number + 1, :] = most * (1.0 / LEVELS)
            code_rows[0] = stop
        scale_rows[0] += 8
        here = pl.ds(begin, code_rows[0] - begin)
        keep(codes.at[here], code_hbm.at[here])

    def store(pieces):
        for piece in pieces:
            start, stop = float_rows[0], float_rows[0] + piece.shape[0]
            floats[start:stop, :] = piece
            float_rows[0] = stop

    for turn in range(2):
        for hop in range(XS - 1):
            encode(pieces_of(CHUNKS_A, dest_of(line + 1 + turn, place + 1 + hop)))
        store(pieces_of(CHUNKS_A, dest_of(line + 1 + turn, place)))
    for hop in range(XS):
        encode(pieces_of(CHUNKS_B, dest_of(line + 1, place + 1 + hop)))
    for hop in range(XS):
        store(pieces_of(CHUNKS_B, dest_of(line, place + 1 + hop)))
    keep(floats, float_hbm)
    for copy in sends:
        copy.wait()


def vmem():
    return pl.BlockSpec(memory_space=pltpu.VMEM)


def smem():
    return pl.BlockSpec(memory_space=pltpu.SMEM)


def hbm():
    return pl.BlockSpec(memory_space=pltpu.HBM)


def shape(dims, dtype):
    return jax.ShapeDtypeStruct(dims, dtype)


def forward_call(offsets, widths, spectrum, pupil, tables, measured):
    lamps = measured.shape[0]
    side = spectrum.shape[-1]
    rows = shape((lamps, OV, PUP), measured.dtype)
    wave = (lamps, 2 * PUP, PUP)
    edge = (2, lamps, OV, PUP)
    chunks = lamps // (2 * FORWARD_PAIRS)
    return pl.pallas_call(
        forward_kernel,
        out_shape=(shape(wave, F32), shape(edge, BF16), rows, rows),
        in_specs=[hbm()] * 6,
        out_specs=(hbm(),) * 4,
        scratch_shapes=[
            pltpu.VMEM(wave, F32),
            pltpu.VMEM(edge, BF16),
            pltpu.VMEM((BLOCKS, 2, side, PUP), F32),
            pltpu.SMEM(offsets.shape, jnp.int32),
            pltpu.SMEM(widths.shape, jnp.int32),
            pltpu.VMEM(spectrum.shape, spectrum.dtype),
            pltpu.VMEM(pupil.shape, pupil.dtype),
            pltpu.VMEM(tables.shape, tables.dtype),
            pltpu.SemaphoreType.DMA((5,)),
            pltpu.SemaphoreType.DMA((chunks,)),
            pltpu.SemaphoreType.DMA((2, chunks)),
            pltpu.SemaphoreType.DMA((2, chunks)),
            pltpu.SemaphoreType.DMA((2,)),
            pltpu.SemaphoreType.DMA((2,)),
        ],
        compiler_params=pltpu.CompilerParams(
            collective_id=1, has_side_effects=True, vmem_limit_bytes=VMEM_LIMIT
        ),
        name="forward",
    )(offsets, widths, spectrum, pupil, tables, measured)


def backward_call(scale, offsets, widths, live, spectrum, pupil, tables, measured, above, below, edges, waves):
    lamps = measured.shape[0]
    side = spectrum.shape[-1]
    planes = pltpu.VMEM((BLOCKS, 2, side, PUP), F32)
    slots = -(-lamps // GROUP) * GROUP
    return pl.pallas_call(
        partial(backward_kernel, scale),
        out_shape=(shape((CODE_ROWS, PUP), jnp.int16), shape((FLOAT_ROWS, PUP), F32)),
        in_specs=[hbm()] * 11,
        out_specs=(hbm(),) * 2,
        scratch_shapes=[
            planes,
            pltpu.VMEM(pupil.shape, F32),
            pltpu.VMEM((CODE_ROWS, PUP), jnp.int16),
            pltpu.VMEM((FLOAT_ROWS, PUP), F32),
            pltpu.VMEM((slots, 2 * PUP, PUP), F32),
            planes,
            pltpu.SMEM(offsets.shape, jnp.int32),
            pltpu.SMEM(widths.shape, jnp.int32),
            pltpu.SMEM(live.shape, jnp.int32),
            pltpu.SMEM((lamps + GROUP,), jnp.int32),
            pltpu.VMEM(spectrum.shape, spectrum.dtype),
            pltpu.VMEM(pupil.shape, pupil.dtype),
            pltpu.VMEM(tables.shape, tables.dtype),
            pltpu.VMEM(measured.shape, measured.dtype),
            pltpu.VMEM(above.shape, above.dtype),
            pltpu.VMEM(below.shape, below.dtype),
            pltpu.VMEM(edges.shape, edges.dtype),
            pltpu.SemaphoreType.DMA((10,)),
            pltpu.SemaphoreType.DMA((slots,)),
            pltpu.SemaphoreType.DMA((SENT_A + SENT_B + 1,)),
        ],
        compiler_params=pltpu.CompilerParams(vmem_limit_bytes=VMEM_LIMIT),
        name="backward",
    )(offsets, widths, live, spectrum, pupil, tables, measured, above, below, edges, waves)


def gather_kernel(
    code_hbm, float_hbm, spec_out, pupil_out, own, held, held_scales, codes2, scales2, held2, held_scales2, own_sem, send_sems, recv_sems
):
    line, place = my_place()
    own_copy = pltpu.make_async_copy(float_hbm.at[pl.ds(0, OWN_ROWS)], own, own_sem)
    own_copy.start()
    opposite = dest_of(line + 1, place)
    beside = [dest_of(line, place + 1 + hop) for hop in range(XS - 1)]
    barrier = pltpu.get_barrier_semaphore()
    for other in [opposite, *beside]:
        pl.semaphore_signal(barrier, inc=1, device_id={"led": other}, device_id_type=MESH)
    pl.semaphore_wait(barrier, XS)
    used = [0]

    def send(codes, scales, targets, other):
        pair = []
        for src, dst in zip((codes, scales), targets):
            number = used[0]
            used[0] += 1
            pair.append(
                pltpu.make_async_remote_copy(
                    src_ref=src, dst_ref=dst, send_sem=send_sems.at[number], recv_sem=recv_sems.at[number],
                    device_id={"led": other}, device_id_type=MESH,
                )
            )
            pair[-1].start()
        return pair, targets

    def arrive(message):
        for copy in message[0]:
            copy.wait()
        return message[1]

    def first(number, other):
        rows = ROWS_A if number < SENT_A else ROWS_B
        start = number * ROWS_A if number < SENT_A else SENT_A * ROWS_A + (number - SENT_A) * ROWS_B
        here, scale = pl.ds(start, rows), pl.ds(8 * number, 8)
        source_scale = pl.ds(OWN_ROWS + 8 * number, 8)
        return send(code_hbm.at[here], float_hbm.at[source_scale], (held.at[here], held_scales.at[scale]), other)

    def second(number, other):
        here, scale = second_rows(number), pl.ds(8 * number, 8)
        return send(codes2.at[here], scales2.at[scale], (held2.at[here], held_scales2.at[scale]), other)

    def second_rows(number):
        return pl.ds(0, ROWS_A) if number == 0 else pl.ds(ROWS_A + (number - 1) * ROWS_B, ROWS_B)

    def total(start, parts, number, bounds):
        value = own[start + bounds[0] : start + bounds[1], :]
        for codes, scales in parts:
            value += codes[bounds[0] : bounds[1], :].astype(F32) * scales[number : number + 1, :]
        return value

    def encode(start, parts, bounds, number):
        codes, scales = codes2.at[second_rows(number)], scales2.at[pl.ds(8 * number, 8)]
        for index, (low, high) in enumerate(bounds):
            value = total(start, parts, index, (low, high))
            most = jnp.maximum(jnp.max(jnp.abs(value), axis=0, keepdims=True), 1e-30)
            codes[low:high, :] = jnp.round(value * (LEVELS / most)).astype(jnp.int16)
            scales[index : index + 1, :] = most * (1.0 / LEVELS)

    hops = range(XS - 1)
    start_b = 2 * ROWS_A
    first_b, first_a, last_a, second_b = [], [], [], []
    for hop in hops:
        first_b.append(first(SENT_A + hop, opposite))
        first_a.append(first(hop, beside[hop]))
    first_b.append(first(SENT_A + XS - 1, opposite))
    own_copy.wait()
    for hop in hops:
        if hop == XS - 2:
            encode(0, [arrive(message) for message in first_a], BOUNDS_A, 0)
            second_a = second(0, opposite)
        encode(start_b + hop * ROWS_B, [arrive(first_b[hop])], BOUNDS_B, 1 + hop)
        second_b.append(second(1 + hop, beside[hop]))
        last_a.append(first(XS - 1 + hop, beside[hop]))

    def put(chunks, number, value):
        if number < len(chunks):
            block, part = chunks[number]
            spec_out[part, :, block * PUP : (block + 1) * PUP] = value
        else:
            pupil_out[number - len(chunks)] = value

    parts = [arrive(first_b[XS - 1]), *(arrive(message) for message in second_b)]
    for number, bounds in enumerate(BOUNDS_B):
        put(CHUNKS_B, number, total(start_b + (XS - 1) * ROWS_B, parts, number, bounds))
    parts = [*(arrive(message) for message in last_a), arrive(second_a)]
    for number, bounds in enumerate(BOUNDS_A):
        put(CHUNKS_A, number, total(ROWS_A, parts, number, bounds))


def gather_call(codes, floats):
    moved = 2 * (SENT_A + SENT_B + XS)
    second = (ROWS_A + (XS - 1) * ROWS_B, PUP)
    return pl.pallas_call(
        gather_kernel,
        out_shape=(shape((2, SPEC_ROWS, BLOCKS * PUP), F32), shape((2, PUP_ROWS, PUP), F32)),
        in_specs=[hbm()] * 2,
        out_specs=(vmem(), vmem()),
        scratch_shapes=[
            pltpu.VMEM((OWN_ROWS, PUP), F32),
            pltpu.VMEM((CODE_ROWS, PUP), jnp.int16),
            pltpu.VMEM((8 * (SENT_A + SENT_B), PUP), F32),
            pltpu.VMEM(second, jnp.int16),
            pltpu.VMEM((8 * XS, PUP), F32),
            pltpu.VMEM(second, jnp.int16),
            pltpu.VMEM((8 * XS, PUP), F32),
            pltpu.SemaphoreType.DMA,
            pltpu.SemaphoreType.DMA((moved,)),
            pltpu.SemaphoreType.DMA((moved,)),
        ],
        compiler_params=pltpu.CompilerParams(
            collective_id=2, has_side_effects=True, vmem_limit_bytes=GATHER_LIMIT
        ),
        name="reduce_scatter",
    )(codes, floats)


def on_device(tables, spectrum, pupil, offsets, widths, live, measured):
    groups = lax.axis_size("led")
    lamps = measured.shape[0]
    scale = 1.0 / math.sqrt(lamps * groups)
    spectrum, pupil, offsets = spectrum[0], pupil[0], offsets[0].T
    waves, near, above, below = forward_call(offsets, widths, spectrum, pupil, tables, measured)
    parts = backward_call(
        scale, offsets, widths, live, spectrum, pupil, tables, measured, above, below, near, waves
    )
    spec_share, pupil_share = gather_call(*parts)
    return spec_share[None], pupil_share[None]


def solution(mesh):
    tables = dft_tables()

    def run(spectrum, pupil, offsets, widths, live, measured):
        return jax.shard_map(
            on_device,
            mesh=mesh,
            in_specs=(
                P(),
                P("tile", None, None, None),
                P("tile", None, None, None),
                P("tile", "led", None),
                P(),
                P("led"),
                P("led", "tile", None),
            ),
            out_specs=(P("tile", None, "led", None), P("tile", None, "led", None)),
            check_vma=False,
        )(jnp.asarray(tables), spectrum, pupil, offsets, widths, live, measured)

    return run
```

```python
from functools import partial
import math

import jax
import jax.numpy as jnp
import ml_dtypes
import numpy as np
from jax import lax
from jax.experimental import pallas as pl
from jax.experimental.pallas import tpu as pltpu
from jax.sharding import PartitionSpec as P

PUP = 128
OV = 16
HALF = 8
STRIDE = PUP - OV
BLOCKS = 4
MESH = pl.DeviceIdType.MESH
F32 = jnp.float32
BF16 = jnp.bfloat16
XS, YS = 4, 2
SPEC_ROWS = 512 // (XS * YS)
PUP_ROWS = PUP // (XS * YS)
CHUNKS = [(block, part) for block in range(BLOCKS) for part in range(2)]
CHUNKS_A, CHUNKS_B = CHUNKS[:3], CHUNKS[3:]
BOUNDS_B = [(number * SPEC_ROWS, (number + 1) * SPEC_ROWS) for number in range(len(CHUNKS_B))]
ROWS_B = len(CHUNKS_B) * SPEC_ROWS
BOUNDS_A = BOUNDS_B[: len(CHUNKS_A)]
BOUNDS_A += [(len(CHUNKS_A) * SPEC_ROWS + part * PUP_ROWS, len(CHUNKS_A) * SPEC_ROWS + (part + 1) * PUP_ROWS) for part in range(2)]
ROWS_A = len(CHUNKS_A) * SPEC_ROWS + 2 * PUP_ROWS
SENT_A, SENT_B = 2 * (XS - 1), XS
CODE_ROWS = SENT_A * ROWS_A + SENT_B * ROWS_B
OWN_ROWS = 2 * ROWS_A + SENT_B * ROWS_B
FLOAT_ROWS = OWN_ROWS + 8 * (SENT_A + SENT_B)
LEVELS = 32767.0
FORWARD_PAIRS = 7
PAIRS = 4
GROUP = 2 * PAIRS
VMEM_LIMIT = 24 * 1024 * 1024


def dft_tables():
    k = np.arange(PUP)
    angle = 2.0 * np.pi * ((k[:, None] * k[None, :]) % PUP) / PUP
    cosine, sine = np.cos(angle), np.sin(angle)
    inverse = np.block([[cosine, sine], [-sine, cosine]]) / PUP
    forward = np.block([[cosine, -sine], [sine, cosine]])
    parts = []
    for table in (inverse, forward):
        high = table.astype(ml_dtypes.bfloat16)
        low = (table - high.astype(np.float64)).astype(ml_dtypes.bfloat16)
        parts += [high, low]
    return np.stack(parts)


def split(x):
    high = x.astype(BF16)
    return high, (x - high.astype(F32)).astype(BF16)


def right_product(x, high, low):
    xh, xl = split(x)
    data = jnp.concatenate([xh, xl, xh], axis=1)
    table = jnp.concatenate([high, high, low], axis=0)
    return jnp.dot(data, table, preferred_element_type=F32)


def left_product(high, low, x):
    xh, xl = split(x)
    data = jnp.concatenate([xh, xl, xh], axis=0)
    table = jnp.concatenate([high, high, low], axis=1)
    return jnp.dot(table, data, preferred_element_type=F32)


def swap_blocks(x):
    top = jnp.concatenate([x[:PUP, :PUP], x[PUP:, :PUP]], axis=1)
    bottom = jnp.concatenate([x[:PUP, PUP:], x[PUP:, PUP:]], axis=1)
    return jnp.concatenate([top, bottom], axis=0)


def ramp_weights(widths_ref, tile, tiles):
    place = lax.broadcasted_iota(jnp.int32, (OV, PUP), 0).astype(F32)
    above = widths_ref[jnp.maximum(tile - 1, 0)].astype(F32)
    below = widths_ref[jnp.minimum(tile, tiles - 2)].astype(F32)
    top = 1.0 - jnp.clip(0.5 + (HALF - 0.5 - place) / above, 0.0, 1.0)
    bottom = jnp.clip(0.5 + (HALF - 0.5 - place) / below, 0.0, 1.0)
    ones = jnp.ones_like(place)
    return jnp.where(tile > 0, top, ones), jnp.where(tile < tiles - 1, bottom, ones)


def list_live(live_ref, order_ref):
    def body(led, count):
        order_ref[count] = led
        return count + live_ref[led]

    lamps = live_ref.shape[0]
    count = lax.fori_loop(0, lamps, body, jnp.int32(0))
    for extra in range(GROUP):
        order_ref[count + extra] = 0
    return count


def load_spectrum(spec_ref, planes):
    for block in range(BLOCKS):
        for part in range(2):
            planes[block, part] = spec_ref[part, :, block * PUP : (block + 1) * PUP].astype(F32)


def window_of(planes, row, col):
    first = col // PUP
    second = jnp.minimum(first + 1, BLOCKS - 1)
    lanes = lax.broadcasted_iota(jnp.int32, (PUP, PUP), 1)
    inside = lanes >= col % PUP
    return [
        jnp.where(inside, planes[first, part, pl.ds(row, PUP), :], planes[second, part, pl.ds(row, PUP), :])
        for part in range(2)
    ]


def forward_kernel(
    offsets_hbm, widths_hbm, spec_hbm, pupil_hbm, table_hbm, measured_hbm,
    waves, near, above, below, planes, pupil_ref, table_ref, measured_ref,
    edges, offsets_ref, widths_ref, spec_ref, local_sems, send_sems, recv_sems, image_send, image_recv
):
    tiles = lax.axis_size("tile")
    tile = lax.axis_index("tile")
    up, down = jnp.maximum(tile - 1, 0), jnp.minimum(tile + 1, tiles - 1)
    width = 2 * FORWARD_PAIRS
    steps = waves.shape[0] // width
    local = [
        pltpu.make_async_copy(source, target, local_sems.at[number])
        for number, (source, target) in enumerate(
            (
                (offsets_hbm, offsets_ref),
                (widths_hbm, widths_ref),
                (spec_hbm, spec_ref),
                (pupil_hbm, pupil_ref),
                (table_hbm, table_ref),
                (measured_hbm, measured_ref),
            )
        )
    ]
    for copy in local:
        copy.start()
    barrier = pltpu.get_barrier_semaphore()
    has_above, has_below = tile > 0, tile < tiles - 1

    def signal(other):
        pl.semaphore_signal(barrier, inc=1, device_id={"tile": other}, device_id_type=MESH)

    pl.when(has_above)(lambda: signal(up))
    pl.when(has_below)(lambda: signal(down))
    for copy in local[:3]:
        copy.wait()
    load_spectrum(spec_ref, planes)
    top, bottom = ramp_weights(widths_ref, tile, tiles)
    top2 = jnp.concatenate([top, top], axis=1)
    bottom2 = jnp.concatenate([bottom, bottom], axis=1)
    for copy in local[3:5]:
        copy.wait()
    pl.semaphore_wait(barrier, has_above.astype(jnp.int32) + has_below.astype(jnp.int32))

    def remote(source, target, send_sem, recv_sem, other):
        return pltpu.make_async_remote_copy(
            src_ref=source, dst_ref=target, send_sem=send_sem, recv_sem=recv_sem,
            device_id={"tile": other}, device_id_type=MESH,
        )

    sides = ((0, has_above, up), (1, has_below, down))
    strips = ((pl.ds(0, OV), below), (pl.ds(STRIDE - OV, OV), above))

    def image_copy(end, other):
        rows, target = strips[end]
        return remote(measured_hbm.at[:, rows], target, image_send.at[end], image_recv.at[end], other)

    def edge_copy(end, other, number):
        here = pl.ds(number * width, width)
        return remote(edges.at[end, here], near.at[end, here], send_sems.at[end, number], recv_sems.at[end, number], other)

    for end, present, other in sides:
        pl.when(present)(lambda: image_copy(end, other).start())

    def field_of(led):
        row, col = offsets_ref[0, led], offsets_ref[1, led]
        win_re, win_im = window_of(planes, row, col)
        shift = col % PUP
        pup_re = pltpu.roll(pupil_ref[0].astype(F32), shift, axis=1)
        pup_im = pltpu.roll(pupil_ref[1].astype(F32), shift, axis=1)
        return jnp.concatenate(
            [pup_re * win_re - pup_im * win_im, pup_re * win_im + pup_im * win_re], axis=1
        )

    def step(number, carry):
        for inner in range(FORWARD_PAIRS):
            pair = number * FORWARD_PAIRS + inner
            field = jnp.concatenate([field_of(2 * pair), field_of(2 * pair + 1)], axis=0)
            mixed = right_product(field, table_ref[0], table_ref[1])
            wave = left_product(table_ref[2], table_ref[3], swap_blocks(mixed))
            first = wave[:OV], wave[PUP : PUP + OV]
            last = wave[STRIDE:PUP], wave[PUP + STRIDE :]
            first = (top2 * (first[0] * first[0] + first[1] * first[1])).astype(BF16)
            last = (bottom2 * (last[0] * last[0] + last[1] * last[1])).astype(BF16)
            for side in range(2):
                lo = side * PUP
                led = 2 * pair + side
                waves[led] = wave[:, lo : lo + PUP]
                edges[0, led] = first[:, lo : lo + PUP]
                edges[1, led] = last[:, lo : lo + PUP]
        for end, present, other in sides:
            pl.when(present)(lambda: edge_copy(end, other, number).start())
        return carry

    lax.fori_loop(0, steps, step, 0)

    def finish(number, carry):
        for end, present, other in sides:
            pl.when(present)(lambda: edge_copy(end, other, number).wait_send())
            pl.when(sides[1 - end][1])(lambda: edge_copy(end, other, number).wait_recv())
        return carry

    lax.fori_loop(0, steps, finish, 0)
    local[5].wait()
    for end, present, other in sides:
        pl.when(present)(lambda: image_copy(end, other).wait_send())
        pl.when(sides[1 - end][1])(lambda: image_copy(end, other).wait_recv())


def my_place():
    me = lax.axis_index("led")
    return me // XS, me % XS


def dest_of(line, place):
    return (line % YS) * XS + place % XS


def backward_kernel(
    scale, offsets_hbm, widths_hbm, live_hbm, planes, pupil_ref, table_ref, measured_ref, above_ref, below_ref, edge_ref, waves,
    codes, floats, spec_out, pupil_out, offsets_ref, widths_ref, live_ref, order_ref, sems
):
    tiles = lax.axis_size("tile")
    tile = lax.axis_index("tile")
    local = [
        pltpu.make_async_copy(source, target, sems.at[number])
        for number, (source, target) in enumerate(
            ((offsets_hbm, offsets_ref), (widths_hbm, widths_ref), (live_hbm, live_ref))
        )
    ]
    for copy in local:
        copy.start()
    spec_out[...] = jnp.zeros_like(spec_out)
    pupil_out[...] = jnp.zeros_like(pupil_out)
    for copy in local:
        copy.wait()
    count = list_live(live_ref, order_ref)
    steps = (count + GROUP - 1) // GROUP

    top, bottom = ramp_weights(widths_ref, tile, tiles)
    top2 = jnp.concatenate([top, top], axis=1)
    bottom2 = jnp.concatenate([bottom, bottom], axis=1)
    rows = lax.broadcasted_iota(jnp.int32, (OV, 2 * PUP), 0)
    top_inside = (tile > 0) | (rows >= HALF)
    bottom_inside = (tile < tiles - 1) | (rows < HALF)
    has_above = tile > 0
    has_below = tile < tiles - 1
    lanes = lax.broadcasted_iota(jnp.int32, (PUP, PUP), 1)

    def edges_of(end, leds):
        return jnp.concatenate([edge_ref[end, led].astype(F32) for led in leds], axis=1)

    def images(ref, leds, low, high):
        return jnp.concatenate([ref[led, low:high].astype(F32) for led in leds], axis=1)

    def step(number, carry):
        for inner in range(PAIRS):
            pair = number * PAIRS + inner
            leds = order_ref[2 * pair], order_ref[2 * pair + 1]
            side_of = lax.broadcasted_iota(jnp.int32, (1, 2 * PUP), 1) // PUP
            alive = jnp.where(2 * pair + side_of < count, scale, 0.0)
            wave = jnp.concatenate([waves[led] for led in leds], axis=1)
            wave_re, wave_im = wave[:PUP], wave[PUP:]
            intensity = wave_re * wave_re + wave_im * wave_im
            own = images(measured_ref, leds, 0, STRIDE)
            upper = images(above_ref, leds, OV - HALF, OV)
            lower = images(below_ref, leds, 0, HALF)
            near_top = jnp.where(has_above, edges_of(1, leds), 0.0)
            near_bottom = jnp.where(has_below, edges_of(0, leds), 0.0)
            first = 2.0 * top2 * (top2 * intensity[:OV] + near_top - jnp.concatenate([upper, own[: OV - HALF]], axis=0))
            middle = 2.0 * (intensity[OV:STRIDE] - own[HALF : STRIDE - HALF])
            last = 2.0 * bottom2 * (bottom2 * intensity[STRIDE:] + near_bottom - jnp.concatenate([own[STRIDE - HALF :], lower], axis=0))
            grad = alive * jnp.concatenate(
                [jnp.where(top_inside, first, 0.0), middle, jnp.where(bottom_inside, last, 0.0)], axis=0
            )
            grad_wave = jnp.concatenate([grad * wave_re, grad * wave_im], axis=0)
            back = right_product(swap_blocks(grad_wave), table_ref[2], table_ref[3])
            grad_field = left_product(table_ref[0], table_ref[1], swap_blocks(back))
            for side in range(2):
                led = leds[side]
                row, col = offsets_ref[0, led], offsets_ref[1, led]
                shift = col % PUP
                lo = side * PUP
                grad_re = grad_field[:PUP, lo : lo + PUP]
                grad_im = grad_field[PUP:, lo : lo + PUP]
                pup_re = pltpu.roll(pupil_ref[0].astype(F32), shift, axis=1)
                pup_im = pltpu.roll(pupil_ref[1].astype(F32), shift, axis=1)
                win_re, win_im = window_of(planes, row, col)
                pieces = (pup_re * grad_re + pup_im * grad_im, pup_re * grad_im - pup_im * grad_re)
                shares = (win_re * grad_re + win_im * grad_im, win_re * grad_im - win_im * grad_re)
                first_block = col // PUP
                second_block = jnp.minimum(first_block + 1, BLOCKS - 1)
                inside = lanes >= shift
                for part in range(2):
                    here_rows = pl.ds(row, PUP)
                    pupil_out[part] += pltpu.roll(shares[part], PUP - shift, axis=1)
                    spec_out[first_block, part, here_rows, :] += jnp.where(inside, pieces[part], 0.0)
                    spec_out[second_block, part, here_rows, :] += jnp.where(inside, 0.0, pieces[part])
        return carry

    lax.fori_loop(0, steps, step, 0)
    line, place = my_place()

    def pieces_of(chunks, dest):
        rows = pl.ds(pl.multiple_of(dest * SPEC_ROWS, SPEC_ROWS), SPEC_ROWS)
        pieces = [spec_out[block, part, rows, :] for block, part in chunks]
        if chunks is CHUNKS_A:
            rows = pl.ds(pl.multiple_of(dest * PUP_ROWS, PUP_ROWS), PUP_ROWS)
            pieces += [pupil_out[part, rows, :] for part in range(2)]
        return pieces

    code_rows, float_rows, scale_rows = [0], [0], [OWN_ROWS]

    def encode(pieces):
        for number, piece in enumerate(pieces):
            most = jnp.maximum(jnp.max(jnp.abs(piece), axis=0, keepdims=True), 1e-30)
            start, stop = code_rows[0], code_rows[0] + piece.shape[0]
            codes[start:stop, :] = jnp.round(piece * (LEVELS / most)).astype(jnp.int16)
            floats[scale_rows[0] + number : scale_rows[0] + number + 1, :] = most * (1.0 / LEVELS)
            code_rows[0] = stop
        scale_rows[0] += 8

    def store(pieces):
        for piece in pieces:
            start, stop = float_rows[0], float_rows[0] + piece.shape[0]
            floats[start:stop, :] = piece
            float_rows[0] = stop

    for turn in range(2):
        for hop in range(XS - 1):
            encode(pieces_of(CHUNKS_A, dest_of(line + 1 + turn, place + 1 + hop)))
        store(pieces_of(CHUNKS_A, dest_of(line + 1 + turn, place)))
    for hop in range(XS):
        encode(pieces_of(CHUNKS_B, dest_of(line + 1, place + 1 + hop)))
    for hop in range(XS):
        store(pieces_of(CHUNKS_B, dest_of(line, place + 1 + hop)))


def vmem():
    return pl.BlockSpec(memory_space=pltpu.VMEM)


def hbm():
    return pl.BlockSpec(memory_space=pltpu.HBM)


def in_hbm(*arrays):
    return [pltpu.with_memory_space_constraint(array, pltpu.HBM) for array in arrays]


def in_vmem(*arrays):
    return [pltpu.with_memory_space_constraint(array, pltpu.VMEM) for array in arrays]


def forward_call(offsets, widths, spectrum, pupil, tables, measured):
    lamps = measured.shape[0]
    side = spectrum.shape[-1]
    rows = pltpu.VMEM((lamps, OV, PUP), measured.dtype)
    edge = pltpu.VMEM((2, lamps, OV, PUP), BF16)
    chunks = lamps // (2 * FORWARD_PAIRS)
    return pl.pallas_call(
        forward_kernel,
        out_shape=(
            pltpu.VMEM((lamps, 2 * PUP, PUP), F32),
            edge,
            rows,
            rows,
            pltpu.VMEM((BLOCKS, 2, side, PUP), F32),
            pltpu.VMEM(pupil.shape, pupil.dtype),
            pltpu.VMEM(tables.shape, tables.dtype),
            pltpu.VMEM(measured.shape, measured.dtype),
        ),
        in_specs=[hbm()] * 6,
        out_specs=(vmem(),) * 8,
        scratch_shapes=[
            edge,
            pltpu.SMEM(offsets.shape, jnp.int32),
            pltpu.SMEM(widths.shape, jnp.int32),
            pltpu.VMEM(spectrum.shape, spectrum.dtype),
            pltpu.SemaphoreType.DMA((6,)),
            pltpu.SemaphoreType.DMA((2, chunks)),
            pltpu.SemaphoreType.DMA((2, chunks)),
            pltpu.SemaphoreType.DMA((2,)),
            pltpu.SemaphoreType.DMA((2,)),
        ],
        compiler_params=pltpu.CompilerParams(
            collective_id=1, has_side_effects=True, vmem_limit_bytes=VMEM_LIMIT
        ),
        name="forward",
    )(*in_hbm(offsets, widths, spectrum, pupil, tables, measured))


def backward_call(scale, offsets, widths, live, planes, pupil, tables, measured, above, below, edges, waves):
    lamps = measured.shape[0]
    return pl.pallas_call(
        partial(backward_kernel, scale),
        out_shape=(pltpu.VMEM((CODE_ROWS, PUP), jnp.int16), pltpu.VMEM((FLOAT_ROWS, PUP), F32)),
        in_specs=[hbm()] * 3 + [vmem()] * 8,
        out_specs=(vmem(), vmem()),
        scratch_shapes=[
            pltpu.VMEM(planes.shape, F32),
            pltpu.VMEM(pupil.shape, F32),
            pltpu.SMEM(offsets.shape, jnp.int32),
            pltpu.SMEM(widths.shape, jnp.int32),
            pltpu.SMEM(live.shape, jnp.int32),
            pltpu.SMEM((lamps + GROUP,), jnp.int32),
            pltpu.SemaphoreType.DMA((3,)),
        ],
        compiler_params=pltpu.CompilerParams(vmem_limit_bytes=VMEM_LIMIT),
        name="backward",
    )(*in_hbm(offsets, widths, live), *in_vmem(planes, pupil, tables, measured, above, below, edges, waves))


def gather_kernel(
    codes, floats, spec_out, pupil_out, held, held_scales, codes2, scales2, held2, held_scales2, send_sems, recv_sems
):
    line, place = my_place()
    opposite = dest_of(line + 1, place)
    beside = [dest_of(line, place + 1 + hop) for hop in range(XS - 1)]
    barrier = pltpu.get_barrier_semaphore()
    for other in [opposite, *beside]:
        pl.semaphore_signal(barrier, inc=1, device_id={"led": other}, device_id_type=MESH)
    pl.semaphore_wait(barrier, XS)
    used = [0]

    def send(code, scale, targets, other):
        pair = []
        for src, dst in zip((code, scale), targets):
            number = used[0]
            used[0] += 1
            pair.append(
                pltpu.make_async_remote_copy(
                    src_ref=src, dst_ref=dst, send_sem=send_sems.at[number], recv_sem=recv_sems.at[number],
                    device_id={"led": other}, device_id_type=MESH,
                )
            )
            pair[-1].start()
        return pair, targets

    def arrive(message):
        for copy in message[0]:
            copy.wait()
        return message[1]

    def first(number, other):
        rows = ROWS_A if number < SENT_A else ROWS_B
        start = number * ROWS_A if number < SENT_A else SENT_A * ROWS_A + (number - SENT_A) * ROWS_B
        here, scale = pl.ds(start, rows), pl.ds(8 * number, 8)
        source_scale = pl.ds(OWN_ROWS + 8 * number, 8)
        return send(codes.at[here], floats.at[source_scale], (held.at[here], held_scales.at[scale]), other)

    def second(number, other):
        here, scale = second_rows(number), pl.ds(8 * number, 8)
        return send(codes2.at[here], scales2.at[scale], (held2.at[here], held_scales2.at[scale]), other)

    def second_rows(number):
        return pl.ds(0, ROWS_A) if number == 0 else pl.ds(ROWS_A + (number - 1) * ROWS_B, ROWS_B)

    def total(start, parts, number, bounds):
        value = floats[start + bounds[0] : start + bounds[1], :]
        for code, scale in parts:
            value += code[bounds[0] : bounds[1], :].astype(F32) * scale[number : number + 1, :]
        return value

    def encode(start, parts, bounds, number):
        code, scale = codes2.at[second_rows(number)], scales2.at[pl.ds(8 * number, 8)]
        for index, (low, high) in enumerate(bounds):
            value = total(start, parts, index, (low, high))
            most = jnp.maximum(jnp.max(jnp.abs(value), axis=0, keepdims=True), 1e-30)
            code[low:high, :] = jnp.round(value * (LEVELS / most)).astype(jnp.int16)
            scale[index : index + 1, :] = most * (1.0 / LEVELS)

    hops = range(XS - 1)
    start_b = 2 * ROWS_A
    first_b, first_a, last_a, second_b = [], [], [], []
    for hop in hops:
        first_b.append(first(SENT_A + hop, opposite))
        first_a.append(first(hop, beside[hop]))
    first_b.append(first(SENT_A + XS - 1, opposite))
    for hop in hops:
        if hop == XS - 2:
            encode(0, [arrive(message) for message in first_a], BOUNDS_A, 0)
            second_a = second(0, opposite)
        encode(start_b + hop * ROWS_B, [arrive(first_b[hop])], BOUNDS_B, 1 + hop)
        second_b.append(second(1 + hop, beside[hop]))
        last_a.append(first(XS - 1 + hop, beside[hop]))

    def put(chunks, number, value):
        if number < len(chunks):
            block, part = chunks[number]
            spec_out[part, :, block * PUP : (block + 1) * PUP] = value
        else:
            pupil_out[number - len(chunks)] = value

    parts = [arrive(first_b[XS - 1]), *(arrive(message) for message in second_b)]
    for number, bounds in enumerate(BOUNDS_B):
        put(CHUNKS_B, number, total(start_b + (XS - 1) * ROWS_B, parts, number, bounds))
    parts = [*(arrive(message) for message in last_a), arrive(second_a)]
    for number, bounds in enumerate(BOUNDS_A):
        put(CHUNKS_A, number, total(ROWS_A, parts, number, bounds))


def gather_call(codes, floats):
    moved = 2 * (SENT_A + SENT_B + XS)
    second = (ROWS_A + (XS - 1) * ROWS_B, PUP)
    return pl.pallas_call(
        gather_kernel,
        out_shape=(
            pltpu.VMEM((2, SPEC_ROWS, BLOCKS * PUP), F32),
            pltpu.VMEM((2, PUP_ROWS, PUP), F32),
        ),
        in_specs=[vmem()] * 2,
        out_specs=(vmem(), vmem()),
        scratch_shapes=[
            pltpu.VMEM((CODE_ROWS, PUP), jnp.int16),
            pltpu.VMEM((8 * (SENT_A + SENT_B), PUP), F32),
            pltpu.VMEM(second, jnp.int16),
            pltpu.VMEM((8 * XS, PUP), F32),
            pltpu.VMEM(second, jnp.int16),
            pltpu.VMEM((8 * XS, PUP), F32),
            pltpu.SemaphoreType.DMA((moved,)),
            pltpu.SemaphoreType.DMA((moved,)),
        ],
        compiler_params=pltpu.CompilerParams(
            collective_id=2, has_side_effects=True, vmem_limit_bytes=VMEM_LIMIT
        ),
        name="reduce_scatter",
    )(*in_vmem(codes, floats))


def on_device(tables, spectrum, pupil, offsets, widths, live, measured):
    groups = lax.axis_size("led")
    lamps = measured.shape[0]
    scale = 1.0 / math.sqrt(lamps * groups)
    spectrum, pupil, offsets = spectrum[0], pupil[0], offsets[0].T
    waves, near, above, below, planes, pupil, tables, measured = forward_call(
        offsets, widths, spectrum, pupil, tables, measured
    )
    parts = backward_call(
        scale, offsets, widths, live, planes, pupil, tables, measured, above, below, near, waves
    )
    spec_share, pupil_share = gather_call(*parts)
    return spec_share[None], pupil_share[None]


def solution(mesh):
    tables = dft_tables()

    def run(spectrum, pupil, offsets, widths, live, measured):
        return jax.shard_map(
            on_device,
            mesh=mesh,
            in_specs=(
                P(),
                P("tile", None, None, None),
                P("tile", None, None, None),
                P("tile", "led", None),
                P(),
                P("led"),
                P("led", "tile", None),
            ),
            out_specs=(P("tile", None, "led", None), P("tile", None, "led", None)),
            check_vma=False,
        )(jnp.asarray(tables), spectrum, pupil, offsets, widths, live, measured)

    return run
```

```python
from functools import partial
import math

import jax
import jax.numpy as jnp
import ml_dtypes
import numpy as np
from jax import lax
from jax.experimental import pallas as pl
from jax.experimental.pallas import tpu as pltpu
from jax.sharding import PartitionSpec as P

PUP = 128
OV = 16
HALF = 8
STRIDE = PUP - OV
BLOCKS = 4
MESH = pl.DeviceIdType.MESH
F32 = jnp.float32
BF16 = jnp.bfloat16
XS, YS = 4, 2
SPEC_ROWS = 512 // (XS * YS)
PUP_ROWS = PUP // (XS * YS)
CHUNKS = [(block, part) for block in range(BLOCKS) for part in range(2)]
SPLIT = 4
BUNDLE_A = CHUNKS[:SPLIT]
BUNDLE_B = CHUNKS[SPLIT:] + [(None, part) for part in range(2)]


def bounds_of(bundle):
    bounds, start = [], 0
    for block, _ in bundle:
        stop = start + (PUP_ROWS if block is None else SPEC_ROWS)
        bounds.append((start, stop))
        start = stop
    return bounds


ROWS_A, ROWS_B = bounds_of(BUNDLE_A)[-1][1], bounds_of(BUNDLE_B)[-1][1]
SENT_A, SENT_B = 2 * (XS - 1), XS
CODE_ROWS = SENT_A * ROWS_A + SENT_B * ROWS_B
LEVELS = 32767.0
FORWARD_PAIRS = 7
SENDS = ((0, 14),)
PAIRS = 4
GROUP = 2 * PAIRS
VMEM_LIMIT = 24 * 1024 * 1024


def dft_tables():
    k = np.arange(PUP)
    angle = 2.0 * np.pi * ((k[:, None] * k[None, :]) % PUP) / PUP
    cosine, sine = np.cos(angle), np.sin(angle)
    inverse = np.block([[cosine, sine], [-sine, cosine]]) / PUP
    forward = np.block([[cosine, -sine], [sine, cosine]])
    parts = []
    for table in (inverse, forward):
        high = table.astype(ml_dtypes.bfloat16)
        low = (table - high.astype(np.float64)).astype(ml_dtypes.bfloat16)
        parts += [high, low]
    return np.stack(parts)


def split(x):
    high = x.astype(BF16)
    return high, (x - high.astype(F32)).astype(BF16)


def right_product(x, high, low):
    xh, xl = split(x)
    data = jnp.concatenate([xh, xl, xh], axis=1)
    table = jnp.concatenate([high, high, low], axis=0)
    return jnp.dot(data, table, preferred_element_type=F32)


def left_product(high, low, x):
    xh, xl = split(x)
    data = jnp.concatenate([xh, xl, xh], axis=0)
    table = jnp.concatenate([high, high, low], axis=1)
    return jnp.dot(table, data, preferred_element_type=F32)


def swap_blocks(x):
    top = jnp.concatenate([x[:PUP, :PUP], x[PUP:, :PUP]], axis=1)
    bottom = jnp.concatenate([x[:PUP, PUP:], x[PUP:, PUP:]], axis=1)
    return jnp.concatenate([top, bottom], axis=0)


def ramp_weights(widths_ref, tile, tiles):
    place = lax.broadcasted_iota(jnp.int32, (OV, PUP), 0).astype(F32)
    above = widths_ref[jnp.maximum(tile - 1, 0)].astype(F32)
    below = widths_ref[jnp.minimum(tile, tiles - 2)].astype(F32)
    top = 1.0 - jnp.clip(0.5 + (HALF - 0.5 - place) / above, 0.0, 1.0)
    bottom = jnp.clip(0.5 + (HALF - 0.5 - place) / below, 0.0, 1.0)
    ones = jnp.ones_like(place)
    return jnp.where(tile > 0, top, ones), jnp.where(tile < tiles - 1, bottom, ones)


def list_live(live_ref, order_ref):
    def body(led, count):
        order_ref[count] = led
        return count + live_ref[led]

    lamps = live_ref.shape[0]
    count = lax.fori_loop(0, lamps, body, jnp.int32(0))
    for extra in range(GROUP):
        order_ref[count + extra] = 0
    return count


def load_spectrum(spec_ref, planes):
    for block in range(BLOCKS):
        for part in range(2):
            planes[block, part] = spec_ref[part, :, block * PUP : (block + 1) * PUP].astype(F32)


def window_of(planes, row, col):
    first = col // PUP
    second = jnp.minimum(first + 1, BLOCKS - 1)
    lanes = lax.broadcasted_iota(jnp.int32, (PUP, PUP), 1)
    inside = lanes >= col % PUP
    return [
        jnp.where(inside, planes[first, part, pl.ds(row, PUP), :], planes[second, part, pl.ds(row, PUP), :])
        for part in range(2)
    ]


def forward_kernel(
    offsets_hbm, widths_hbm, spec_hbm, pupil_hbm, table_hbm, measured_hbm,
    waves, near, above, below, planes, pupil_ref, table_ref, measured_ref,
    edges, offsets_ref, widths_ref, spec_ref, local_sems, send_sems, recv_sems, image_send, image_recv
):
    tiles = lax.axis_size("tile")
    tile = lax.axis_index("tile")
    up, down = jnp.maximum(tile - 1, 0), jnp.minimum(tile + 1, tiles - 1)
    width = 2 * FORWARD_PAIRS
    steps = waves.shape[0] // width
    local = [
        pltpu.make_async_copy(source, target, local_sems.at[number])
        for number, (source, target) in enumerate(
            (
                (offsets_hbm, offsets_ref),
                (widths_hbm, widths_ref),
                (spec_hbm, spec_ref),
                (pupil_hbm, pupil_ref),
                (table_hbm, table_ref),
                (measured_hbm, measured_ref),
            )
        )
    ]
    for copy in local:
        copy.start()
    barrier = pltpu.get_barrier_semaphore()
    has_above, has_below = tile > 0, tile < tiles - 1

    def signal(other):
        pl.semaphore_signal(barrier, inc=1, device_id={"tile": other}, device_id_type=MESH)

    pl.when(has_above)(lambda: signal(up))
    pl.when(has_below)(lambda: signal(down))
    for copy in local[:3]:
        copy.wait()
    load_spectrum(spec_ref, planes)
    top, bottom = ramp_weights(widths_ref, tile, tiles)
    top2 = jnp.concatenate([top, top], axis=1)
    bottom2 = jnp.concatenate([bottom, bottom], axis=1)
    for copy in local[3:5]:
        copy.wait()
    pl.semaphore_wait(barrier, has_above.astype(jnp.int32) + has_below.astype(jnp.int32))

    def remote(source, target, send_sem, recv_sem, other):
        return pltpu.make_async_remote_copy(
            src_ref=source, dst_ref=target, send_sem=send_sem, recv_sem=recv_sem,
            device_id={"tile": other}, device_id_type=MESH,
        )

    sides = ((0, has_above, up), (1, has_below, down))
    strips = ((pl.ds(0, OV), below), (pl.ds(STRIDE - OV, OV), above))

    def image_copy(end, other):
        rows, target = strips[end]
        return remote(measured_hbm.at[:, rows], target, image_send.at[end], image_recv.at[end], other)

    def edge_copy(end, other, number, turn):
        here = pl.ds(number * width + SENDS[turn][0], SENDS[turn][1])
        return remote(
            edges.at[end, here], near.at[end, here], send_sems.at[end, number, turn], recv_sems.at[end, number, turn], other
        )

    for end, present, other in sides:
        pl.when(present)(lambda: image_copy(end, other).start())

    def field_of(led):
        row, col = offsets_ref[0, led], offsets_ref[1, led]
        win_re, win_im = window_of(planes, row, col)
        shift = col % PUP
        pup_re = pltpu.roll(pupil_ref[0].astype(F32), shift, axis=1)
        pup_im = pltpu.roll(pupil_ref[1].astype(F32), shift, axis=1)
        return jnp.concatenate(
            [pup_re * win_re - pup_im * win_im, pup_re * win_im + pup_im * win_re], axis=1
        )

    def step(number, carry):
        for inner in range(FORWARD_PAIRS):
            pair = number * FORWARD_PAIRS + inner
            field = jnp.concatenate([field_of(2 * pair), field_of(2 * pair + 1)], axis=0)
            mixed = right_product(field, table_ref[0], table_ref[1])
            wave = left_product(table_ref[2], table_ref[3], swap_blocks(mixed))
            first = wave[:OV], wave[PUP : PUP + OV]
            last = wave[STRIDE:PUP], wave[PUP + STRIDE :]
            first = (top2 * (first[0] * first[0] + first[1] * first[1])).astype(BF16)
            last = (bottom2 * (last[0] * last[0] + last[1] * last[1])).astype(BF16)
            for side in range(2):
                lo = side * PUP
                led = 2 * pair + side
                waves[led] = wave[:, lo : lo + PUP]
                edges[0, led] = first[:, lo : lo + PUP]
                edges[1, led] = last[:, lo : lo + PUP]
            for turn, (low, leds) in enumerate(SENDS):
                if 2 * (inner + 1) == low + leds:
                    for end, present, other in sides:
                        pl.when(present)(lambda: edge_copy(end, other, number, turn).start())
        return carry

    lax.fori_loop(0, steps, step, 0)

    def finish(number, carry):
        for turn in range(len(SENDS)):
            for end, present, other in sides:
                pl.when(present)(lambda: edge_copy(end, other, number, turn).wait_send())
                pl.when(sides[1 - end][1])(lambda: edge_copy(end, other, number, turn).wait_recv())
        return carry

    lax.fori_loop(0, steps, finish, 0)
    local[5].wait()
    for end, present, other in sides:
        pl.when(present)(lambda: image_copy(end, other).wait_send())
        pl.when(sides[1 - end][1])(lambda: image_copy(end, other).wait_recv())


def my_place():
    me = lax.axis_index("led")
    return me // XS, me % XS


def dest_of(line, place):
    return (line % YS) * XS + place % XS


def backward_kernel(
    scale, offsets_hbm, widths_hbm, live_hbm, planes, pupil_ref, table_ref, measured_ref, above_ref, below_ref, edge_ref, waves,
    spec_out, pupil_out, offsets_ref, widths_ref, live_ref, order_ref, sems
):
    tiles = lax.axis_size("tile")
    tile = lax.axis_index("tile")
    local = [
        pltpu.make_async_copy(source, target, sems.at[number])
        for number, (source, target) in enumerate(
            ((offsets_hbm, offsets_ref), (widths_hbm, widths_ref), (live_hbm, live_ref))
        )
    ]
    for copy in local:
        copy.start()
    spec_out[...] = jnp.zeros_like(spec_out)
    pupil_out[...] = jnp.zeros_like(pupil_out)
    for copy in local:
        copy.wait()
    count = list_live(live_ref, order_ref)
    steps = (count + GROUP - 1) // GROUP

    top, bottom = ramp_weights(widths_ref, tile, tiles)
    top2 = jnp.concatenate([top, top], axis=1)
    bottom2 = jnp.concatenate([bottom, bottom], axis=1)
    rows = lax.broadcasted_iota(jnp.int32, (OV, 2 * PUP), 0)
    top_inside = (tile > 0) | (rows >= HALF)
    bottom_inside = (tile < tiles - 1) | (rows < HALF)
    has_above = tile > 0
    has_below = tile < tiles - 1
    lanes = lax.broadcasted_iota(jnp.int32, (PUP, PUP), 1)

    def edges_of(end, leds):
        return jnp.concatenate([edge_ref[end, led].astype(F32) for led in leds], axis=1)

    def images(ref, leds, low, high):
        return jnp.concatenate([ref[led, low:high].astype(F32) for led in leds], axis=1)

    def step(number, carry):
        for inner in range(PAIRS):
            pair = number * PAIRS + inner
            leds = order_ref[2 * pair], order_ref[2 * pair + 1]
            side_of = lax.broadcasted_iota(jnp.int32, (1, 2 * PUP), 1) // PUP
            alive = jnp.where(2 * pair + side_of < count, scale, 0.0)
            wave = jnp.concatenate([waves[led] for led in leds], axis=1)
            wave_re, wave_im = wave[:PUP], wave[PUP:]
            intensity = wave_re * wave_re + wave_im * wave_im
            own = images(measured_ref, leds, 0, STRIDE)
            upper = images(above_ref, leds, OV - HALF, OV)
            lower = images(below_ref, leds, 0, HALF)
            near_top = jnp.where(has_above, edges_of(1, leds), 0.0)
            near_bottom = jnp.where(has_below, edges_of(0, leds), 0.0)
            first = 2.0 * top2 * (top2 * intensity[:OV] + near_top - jnp.concatenate([upper, own[: OV - HALF]], axis=0))
            middle = 2.0 * (intensity[OV:STRIDE] - own[HALF : STRIDE - HALF])
            last = 2.0 * bottom2 * (bottom2 * intensity[STRIDE:] + near_bottom - jnp.concatenate([own[STRIDE - HALF :], lower], axis=0))
            grad = alive * jnp.concatenate(
                [jnp.where(top_inside, first, 0.0), middle, jnp.where(bottom_inside, last, 0.0)], axis=0
            )
            grad_wave = jnp.concatenate([grad * wave_re, grad * wave_im], axis=0)
            back = right_product(swap_blocks(grad_wave), table_ref[2], table_ref[3])
            grad_field = left_product(table_ref[0], table_ref[1], swap_blocks(back))
            for side in range(2):
                led = leds[side]
                row, col = offsets_ref[0, led], offsets_ref[1, led]
                shift = col % PUP
                lo = side * PUP
                grad_re = grad_field[:PUP, lo : lo + PUP]
                grad_im = grad_field[PUP:, lo : lo + PUP]
                pup_re = pltpu.roll(pupil_ref[0].astype(F32), shift, axis=1)
                pup_im = pltpu.roll(pupil_ref[1].astype(F32), shift, axis=1)
                win_re, win_im = window_of(planes, row, col)
                pieces = (pup_re * grad_re + pup_im * grad_im, pup_re * grad_im - pup_im * grad_re)
                shares = (win_re * grad_re + win_im * grad_im, win_re * grad_im - win_im * grad_re)
                first_block = col // PUP
                second_block = jnp.minimum(first_block + 1, BLOCKS - 1)
                inside = lanes >= shift
                for part in range(2):
                    here_rows = pl.ds(row, PUP)
                    pupil_out[part] += pltpu.roll(shares[part], PUP - shift, axis=1)
                    spec_out[first_block, part, here_rows, :] += jnp.where(inside, pieces[part], 0.0)
                    spec_out[second_block, part, here_rows, :] += jnp.where(inside, 0.0, pieces[part])
        return carry

    lax.fori_loop(0, steps, step, 0)

def vmem():
    return pl.BlockSpec(memory_space=pltpu.VMEM)


def hbm():
    return pl.BlockSpec(memory_space=pltpu.HBM)


def in_hbm(*arrays):
    return [pltpu.with_memory_space_constraint(array, pltpu.HBM) for array in arrays]


def in_vmem(*arrays):
    return [pltpu.with_memory_space_constraint(array, pltpu.VMEM) for array in arrays]


def forward_call(offsets, widths, spectrum, pupil, tables, measured):
    lamps = measured.shape[0]
    side = spectrum.shape[-1]
    rows = pltpu.VMEM((lamps, OV, PUP), measured.dtype)
    edge = pltpu.VMEM((2, lamps, OV, PUP), BF16)
    chunks = lamps // (2 * FORWARD_PAIRS)
    return pl.pallas_call(
        forward_kernel,
        out_shape=(
            pltpu.VMEM((lamps, 2 * PUP, PUP), F32),
            edge,
            rows,
            rows,
            pltpu.VMEM((BLOCKS, 2, side, PUP), F32),
            pltpu.VMEM(pupil.shape, pupil.dtype),
            pltpu.VMEM(tables.shape, tables.dtype),
            pltpu.VMEM(measured.shape, measured.dtype),
        ),
        in_specs=[hbm()] * 6,
        out_specs=(vmem(),) * 8,
        scratch_shapes=[
            edge,
            pltpu.SMEM(offsets.shape, jnp.int32),
            pltpu.SMEM(widths.shape, jnp.int32),
            pltpu.VMEM(spectrum.shape, spectrum.dtype),
            pltpu.SemaphoreType.DMA((6,)),
            pltpu.SemaphoreType.DMA((2, chunks, len(SENDS))),
            pltpu.SemaphoreType.DMA((2, chunks, len(SENDS))),
            pltpu.SemaphoreType.DMA((2,)),
            pltpu.SemaphoreType.DMA((2,)),
        ],
        compiler_params=pltpu.CompilerParams(
            collective_id=1, has_side_effects=True, vmem_limit_bytes=VMEM_LIMIT
        ),
        name="forward",
    )(*in_hbm(offsets, widths, spectrum, pupil, tables, measured))


def backward_call(scale, offsets, widths, live, planes, pupil, tables, measured, above, below, edges, waves):
    lamps = measured.shape[0]
    return pl.pallas_call(
        partial(backward_kernel, scale),
        out_shape=(pltpu.VMEM(planes.shape, F32), pltpu.VMEM(pupil.shape, F32)),
        in_specs=[hbm()] * 3 + [vmem()] * 8,
        out_specs=(vmem(), vmem()),
        scratch_shapes=[
            pltpu.SMEM(offsets.shape, jnp.int32),
            pltpu.SMEM(widths.shape, jnp.int32),
            pltpu.SMEM(live.shape, jnp.int32),
            pltpu.SMEM((lamps + GROUP,), jnp.int32),
            pltpu.SemaphoreType.DMA((3,)),
        ],
        compiler_params=pltpu.CompilerParams(vmem_limit_bytes=VMEM_LIMIT),
        name="backward",
    )(*in_hbm(offsets, widths, live), *in_vmem(planes, pupil, tables, measured, above, below, edges, waves))


def gather_kernel(
    spec_ref, pupil_ref, spec_out, pupil_out, codes, scales, held, held_scales, codes2, scales2, held2, held_scales2,
    send_sems, recv_sems
):
    line, place = my_place()
    opposite = dest_of(line + 1, place)
    beside = [dest_of(line, place + 1 + hop) for hop in range(XS - 1)]
    barrier = pltpu.get_barrier_semaphore()
    for other in [opposite, *beside]:
        pl.semaphore_signal(barrier, inc=1, device_id={"led": other}, device_id_type=MESH)

    def piece(block, part, dest):
        if block is None:
            return pupil_ref[part, pl.ds(pl.multiple_of(dest * PUP_ROWS, PUP_ROWS), PUP_ROWS), :]
        return spec_ref[block, part, pl.ds(pl.multiple_of(dest * SPEC_ROWS, SPEC_ROWS), SPEC_ROWS), :]

    def totals(bundle, dest, parts):
        for number, ((block, part), (low, high)) in enumerate(zip(bundle, bounds_of(bundle))):
            value = piece(block, part, dest)
            for code, scale in parts:
                value += code[low:high, :].astype(F32) * scale[number : number + 1, :]
            yield number, low, high, block, part, value

    def encode(bundle, dest, parts, code, scale):
        for number, low, high, _, _, value in totals(bundle, dest, parts):
            most = jnp.maximum(jnp.max(jnp.abs(value), axis=0, keepdims=True), 1e-30)
            code[low:high, :] = jnp.round(value * (LEVELS / most)).astype(jnp.int16)
            scale[number : number + 1, :] = most * (1.0 / LEVELS)

    def finish(bundle, parts):
        for _, _, _, block, part, value in totals(bundle, mine, parts):
            if block is None:
                pupil_out[part] = value
            else:
                spec_out[part, :, block * PUP : (block + 1) * PUP] = value

    def first_rows(number):
        if number < SENT_A:
            return pl.ds(number * ROWS_A, ROWS_A)
        return pl.ds(SENT_A * ROWS_A + (number - SENT_A) * ROWS_B, ROWS_B)

    def second_rows(number):
        return pl.ds(0, ROWS_A) if number == 0 else pl.ds(ROWS_A + (number - 1) * ROWS_B, ROWS_B)

    used = [0]

    def send(number, rows, other, code, scale, held_code, held_scale):
        pair = []
        here = pl.ds(8 * number, 8)
        targets = held_code.at[rows], held_scale.at[here]
        for src, dst in zip((code.at[rows], scale.at[here]), targets):
            sem = used[0]
            used[0] += 1
            pair.append(
                pltpu.make_async_remote_copy(
                    src_ref=src, dst_ref=dst, send_sem=send_sems.at[sem], recv_sem=recv_sems.at[sem],
                    device_id={"led": other}, device_id_type=MESH,
                )
            )
            pair[-1].start()
        return pair, targets

    def arrive(message, sent=False):
        for copy in message[0]:
            if not sent:
                copy.wait_send()
            copy.wait_recv()
        return message[1]

    def first(number, other):
        return send(number, first_rows(number), other, codes, scales, held, held_scales)

    def second(number, other):
        return send(number, second_rows(number), other, codes2, scales2, held2, held_scales2)

    hops = (1, 0, 2)
    mine = dest_of(line, place)

    def encode_first(number, bundle, dest):
        encode(bundle, dest, [], codes.at[first_rows(number)], scales.at[pl.ds(8 * number, 8)])

    for hop in hops:
        encode_first(SENT_A + hop, BUNDLE_B, dest_of(line + 1, place + 1 + hop))
        encode_first(hop, BUNDLE_A, dest_of(line + 1, place + 1 + hop))
    for hop in hops:
        encode_first(XS - 1 + hop, BUNDLE_A, beside[hop])
    encode_first(SENT_A + XS - 1, BUNDLE_B, opposite)
    pl.semaphore_wait(barrier, XS)

    first_b, first_a, last_a, second_b = {}, {}, {}, {}
    for hop in hops:
        first_b[hop] = first(SENT_A + hop, opposite)
        first_a[hop] = first(hop, beside[hop])
    last_b = first(SENT_A + XS - 1, opposite)
    for hop in hops:
        for copy in first_a[hop][0]:
            copy.wait_send()
    for hop in hops:
        last_a[hop] = first(XS - 1 + hop, beside[hop])

    def pass_on(hop):
        parts = [arrive(first_b[hop])]
        encode(BUNDLE_B, beside[hop], parts, codes2.at[second_rows(1 + hop)], scales2.at[pl.ds(8 * (1 + hop), 8)])
        second_b[hop] = second(1 + hop, beside[hop])

    pass_on(hops[0])
    parts = [arrive(first_a[hop], sent=True) for hop in hops]
    encode(BUNDLE_A, opposite, parts, codes2.at[second_rows(0)], scales2.at[pl.ds(0, 8)])
    second_a = second(0, opposite)
    pass_on(hops[1])
    pass_on(hops[2])
    parts = [*(arrive(last_a[hop]) for hop in hops), arrive(second_a)]
    finish(BUNDLE_A, parts)
    parts = [arrive(last_b), *(arrive(second_b[hop]) for hop in hops)]
    finish(BUNDLE_B, parts)


def gather_call(spec_part, pupil_part):
    moved = 2 * (SENT_A + SENT_B + XS)
    code = pltpu.VMEM((CODE_ROWS, PUP), jnp.int16)
    scale = pltpu.VMEM((8 * (SENT_A + SENT_B), PUP), F32)
    code2 = pltpu.VMEM((ROWS_A + (XS - 1) * ROWS_B, PUP), jnp.int16)
    scale2 = pltpu.VMEM((8 * XS, PUP), F32)
    return pl.pallas_call(
        gather_kernel,
        out_shape=(
            pltpu.VMEM((2, SPEC_ROWS, BLOCKS * PUP), F32),
            pltpu.VMEM((2, PUP_ROWS, PUP), F32),
        ),
        in_specs=[vmem()] * 2,
        out_specs=(vmem(), vmem()),
        scratch_shapes=[
            *(code, scale, code, scale),
            *(code2, scale2, code2, scale2),
            pltpu.SemaphoreType.DMA((moved,)),
            pltpu.SemaphoreType.DMA((moved,)),
        ],
        compiler_params=pltpu.CompilerParams(
            collective_id=2, has_side_effects=True, vmem_limit_bytes=VMEM_LIMIT
        ),
        name="reduce_scatter",
    )(*in_vmem(spec_part, pupil_part))


def store_kernel(spec_ref, pupil_ref, spec_out, pupil_out, sems):
    copies = [
        pltpu.make_async_copy(spec_ref, spec_out, sems.at[0]),
        pltpu.make_async_copy(pupil_ref, pupil_out, sems.at[1]),
    ]
    for copy in copies:
        copy.start()
    for copy in copies:
        copy.wait()


def store_call(spec_share, pupil_share):
    return pl.pallas_call(
        store_kernel,
        out_shape=(
            jax.ShapeDtypeStruct(spec_share.shape, F32),
            jax.ShapeDtypeStruct(pupil_share.shape, F32),
        ),
        in_specs=[vmem()] * 2,
        out_specs=(hbm(), hbm()),
        scratch_shapes=[pltpu.SemaphoreType.DMA((2,))],
        compiler_params=pltpu.CompilerParams(vmem_limit_bytes=VMEM_LIMIT),
        name="store",
    )(*in_vmem(spec_share, pupil_share))


def on_device(tables, spectrum, pupil, offsets, widths, live, measured):
    groups = lax.axis_size("led")
    lamps = measured.shape[0]
    scale = 1.0 / math.sqrt(lamps * groups)
    spectrum, pupil, offsets = spectrum[0], pupil[0], offsets[0].T
    waves, near, above, below, planes, pupil, tables, measured = forward_call(
        offsets, widths, spectrum, pupil, tables, measured
    )
    parts = backward_call(
        scale, offsets, widths, live, planes, pupil, tables, measured, above, below, near, waves
    )
    spec_share, pupil_share = store_call(*gather_call(*parts))
    return spec_share[None], pupil_share[None]


def solution(mesh):
    tables = dft_tables()

    def run(spectrum, pupil, offsets, widths, live, measured):
        return jax.shard_map(
            on_device,
            mesh=mesh,
            in_specs=(
                P(),
                P("tile", None, None, None),
                P("tile", None, None, None),
                P("tile", "led", None),
                P(),
                P("led"),
                P("led", "tile", None),
            ),
            out_specs=(P("tile", None, "led", None), P("tile", None, "led", None)),
            check_vma=False,
        )(jnp.asarray(tables), spectrum, pupil, offsets, widths, live, measured)

    return run
```

```python
from functools import partial
import math

import jax
import jax.numpy as jnp
import ml_dtypes
import numpy as np
from jax import lax
from jax.experimental import pallas as pl
from jax.experimental.pallas import tpu as pltpu
from jax.sharding import PartitionSpec as P

PUP = 128
OV = 16
HALF = 8
STRIDE = PUP - OV
BLOCKS = 4
MESH = pl.DeviceIdType.MESH
F32 = jnp.float32
BF16 = jnp.bfloat16
XS, YS = 4, 2
SPEC_ROWS = 512 // (XS * YS)
PUP_ROWS = PUP // (XS * YS)
CHUNKS = [(block, part) for block in range(BLOCKS) for part in range(2)]
SPLIT = 4
BUNDLE_A = CHUNKS[:SPLIT] + [(None, part) for part in range(2)]
BUNDLE_B = CHUNKS[SPLIT:]


def bounds_of(bundle):
    bounds, start = [], 0
    for block, _ in bundle:
        stop = start + (PUP_ROWS if block is None else SPEC_ROWS)
        bounds.append((start, stop))
        start = stop
    return bounds


ROWS_A, ROWS_B = bounds_of(BUNDLE_A)[-1][1], bounds_of(BUNDLE_B)[-1][1]
SENT_A, SENT_B = 2 * (XS - 1), XS
CODE_ROWS = SENT_A * ROWS_A + SENT_B * ROWS_B
LEVELS = 32767.0
FORWARD_PAIRS = 7
SENDS = ((0, 14),)
PAIRS = 6
GROUP = 2 * PAIRS
VMEM_LIMIT = 24 * 1024 * 1024


def dft_tables():
    k = np.arange(PUP)
    angle = 2.0 * np.pi * ((k[:, None] * k[None, :]) % PUP) / PUP
    cosine, sine = np.cos(angle), np.sin(angle)
    inverse = np.block([[cosine, sine], [-sine, cosine]]) / PUP
    forward = np.block([[cosine, -sine], [sine, cosine]])
    parts = []
    for table in (inverse, forward):
        high = table.astype(ml_dtypes.bfloat16)
        low = (table - high.astype(np.float64)).astype(ml_dtypes.bfloat16)
        parts += [high, low]
    return np.stack(parts)


def split(x):
    high = x.astype(BF16)
    return high, (x - high.astype(F32)).astype(BF16)


def right_product(x, high, low):
    xh, xl = split(x)
    product = partial(jnp.dot, preferred_element_type=F32)
    return product(xh, high) + product(xl, high) + product(xh, low)


def left_product(high, low, x):
    xh, xl = split(x)
    data = jnp.concatenate([xh, xl, xh], axis=0)
    table = jnp.concatenate([high, high, low], axis=1)
    return jnp.dot(table, data, preferred_element_type=F32)


def swap_blocks(x):
    top = jnp.concatenate([x[:PUP, :PUP], x[PUP:, :PUP]], axis=1)
    bottom = jnp.concatenate([x[:PUP, PUP:], x[PUP:, PUP:]], axis=1)
    return jnp.concatenate([top, bottom], axis=0)


def ramp_weights(widths_ref, tile, tiles):
    place = lax.broadcasted_iota(jnp.int32, (OV, PUP), 0).astype(F32)
    above = widths_ref[jnp.maximum(tile - 1, 0)].astype(F32)
    below = widths_ref[jnp.minimum(tile, tiles - 2)].astype(F32)
    top = 1.0 - jnp.clip(0.5 + (HALF - 0.5 - place) / above, 0.0, 1.0)
    bottom = jnp.clip(0.5 + (HALF - 0.5 - place) / below, 0.0, 1.0)
    ones = jnp.ones_like(place)
    return jnp.where(tile > 0, top, ones), jnp.where(tile < tiles - 1, bottom, ones)


def list_live(live_ref, order_ref):
    def body(led, count):
        order_ref[count] = led
        return count + live_ref[led]

    lamps = live_ref.shape[0]
    count = lax.fori_loop(0, lamps, body, jnp.int32(0))
    for extra in range(GROUP):
        order_ref[count + extra] = 0
    return count


def load_spectrum(spec_ref, planes, part):
    for block in range(BLOCKS):
        planes[block, part] = spec_ref[part, :, block * PUP : (block + 1) * PUP].astype(F32)


def window_of(planes, row, col):
    first = col // PUP
    second = jnp.minimum(first + 1, BLOCKS - 1)
    lanes = lax.broadcasted_iota(jnp.int32, (PUP, PUP), 1)
    inside = lanes >= col % PUP
    return [
        jnp.where(inside, planes[first, part, pl.ds(row, PUP), :], planes[second, part, pl.ds(row, PUP), :])
        for part in range(2)
    ]


def forward_kernel(
    offsets_hbm, widths_hbm, live_hbm, spec_hbm, pupil_hbm, table_hbm, measured_hbm,
    waves, near, above, below, planes, pupil_ref, table_ref, measured_ref, offsets_ref, widths_ref, live_ref,
    edges, spec_ref, local_sems, send_sems, recv_sems, image_send, image_recv
):
    tiles = lax.axis_size("tile")
    tile = lax.axis_index("tile")
    up, down = jnp.maximum(tile - 1, 0), jnp.minimum(tile + 1, tiles - 1)
    width = 2 * FORWARD_PAIRS
    steps = waves.shape[0] // width
    local = [
        pltpu.make_async_copy(source, target, local_sems.at[number])
        for number, (source, target) in enumerate(
            (
                (offsets_hbm, offsets_ref),
                (widths_hbm, widths_ref),
                (live_hbm, live_ref),
                (spec_hbm.at[0], spec_ref.at[0]),
                (spec_hbm.at[1], spec_ref.at[1]),
                (pupil_hbm, pupil_ref),
                (table_hbm, table_ref),
                (measured_hbm, measured_ref),
            )
        )
    ]
    for copy in local[:-1]:
        copy.start()
    barrier = pltpu.get_barrier_semaphore()
    has_above, has_below = tile > 0, tile < tiles - 1

    def signal(other):
        pl.semaphore_signal(barrier, inc=1, device_id={"tile": other}, device_id_type=MESH)

    pl.when(has_above)(lambda: signal(up))
    pl.when(has_below)(lambda: signal(down))
    for part in range(2):
        local[3 + part].wait()
        load_spectrum(spec_ref, planes, part)
    local[-1].start()
    for copy in local[:3]:
        copy.wait()
    top, bottom = ramp_weights(widths_ref, tile, tiles)
    top2 = jnp.concatenate([top, top], axis=1)
    bottom2 = jnp.concatenate([bottom, bottom], axis=1)
    for copy in local[5:-1]:
        copy.wait()
    pl.semaphore_wait(barrier, has_above.astype(jnp.int32) + has_below.astype(jnp.int32))

    def remote(source, target, send_sem, recv_sem, other):
        return pltpu.make_async_remote_copy(
            src_ref=source, dst_ref=target, send_sem=send_sem, recv_sem=recv_sem,
            device_id={"tile": other}, device_id_type=MESH,
        )

    sides = ((0, has_above, up), (1, has_below, down))
    strips = ((pl.ds(0, OV), below), (pl.ds(STRIDE - OV, OV), above))

    def image_copy(end, other):
        rows, target = strips[end]
        return remote(measured_hbm.at[:, rows], target, image_send.at[end], image_recv.at[end], other)

    def edge_copy(end, other, number, turn):
        here = pl.ds(number * width + SENDS[turn][0], SENDS[turn][1])
        return remote(
            edges.at[end, here], near.at[end, here], send_sems.at[end, number, turn], recv_sems.at[end, number, turn], other
        )

    for end, present, other in sides:
        pl.when(present)(lambda: image_copy(end, other).start())

    def field_of(led):
        row, col = offsets_ref[0, led], offsets_ref[1, led]
        win_re, win_im = window_of(planes, row, col)
        shift = col % PUP
        pup_re = pltpu.roll(pupil_ref[0].astype(F32), shift, axis=1)
        pup_im = pltpu.roll(pupil_ref[1].astype(F32), shift, axis=1)
        return jnp.concatenate(
            [pup_re * win_re - pup_im * win_im, pup_re * win_im + pup_im * win_re], axis=1
        )

    def step(number, carry):
        for inner in range(FORWARD_PAIRS):
            pair = number * FORWARD_PAIRS + inner
            field = jnp.concatenate([field_of(2 * pair), field_of(2 * pair + 1)], axis=0)
            mixed = right_product(field, table_ref[0], table_ref[1])
            wave = left_product(table_ref[2], table_ref[3], swap_blocks(mixed))
            first = wave[:OV], wave[PUP : PUP + OV]
            last = wave[STRIDE:PUP], wave[PUP + STRIDE :]
            first = (top2 * (first[0] * first[0] + first[1] * first[1])).astype(BF16)
            last = (bottom2 * (last[0] * last[0] + last[1] * last[1])).astype(BF16)
            for side in range(2):
                lo = side * PUP
                led = 2 * pair + side
                waves[led] = wave[:, lo : lo + PUP]
                edges[0, led] = first[:, lo : lo + PUP]
                edges[1, led] = last[:, lo : lo + PUP]
            for turn, (low, leds) in enumerate(SENDS):
                if 2 * (inner + 1) == low + leds:
                    for end, present, other in sides:
                        pl.when(present)(lambda: edge_copy(end, other, number, turn).start())
        return carry

    lax.fori_loop(0, steps, step, 0)

    def finish(number, carry):
        for turn in range(len(SENDS)):
            for end, present, other in sides:
                pl.when(present)(lambda: edge_copy(end, other, number, turn).wait_send())
                pl.when(sides[1 - end][1])(lambda: edge_copy(end, other, number, turn).wait_recv())
        return carry

    lax.fori_loop(0, steps, finish, 0)
    local[-1].wait()
    for end, present, other in sides:
        pl.when(present)(lambda: image_copy(end, other).wait_send())
        pl.when(sides[1 - end][1])(lambda: image_copy(end, other).wait_recv())


def my_place():
    me = lax.axis_index("led")
    return me // XS, me % XS


def dest_of(line, place):
    return (line % YS) * XS + place % XS


def backward_kernel(
    scale, offsets_ref, widths_ref, live_ref, planes, pupil_ref, table_ref, measured_ref, above_ref, below_ref, edge_ref, waves,
    spec_out, pupil_out, order_ref
):
    tiles = lax.axis_size("tile")
    tile = lax.axis_index("tile")
    spec_out[...] = jnp.zeros_like(spec_out)
    pupil_out[...] = jnp.zeros_like(pupil_out)
    count = list_live(live_ref, order_ref)
    steps = (count + GROUP - 1) // GROUP

    top, bottom = ramp_weights(widths_ref, tile, tiles)
    top2 = jnp.concatenate([top, top], axis=1)
    bottom2 = jnp.concatenate([bottom, bottom], axis=1)
    rows = lax.broadcasted_iota(jnp.int32, (OV, 2 * PUP), 0)
    top_inside = (tile > 0) | (rows >= HALF)
    bottom_inside = (tile < tiles - 1) | (rows < HALF)
    has_above = tile > 0
    has_below = tile < tiles - 1
    lanes = lax.broadcasted_iota(jnp.int32, (PUP, PUP), 1)

    def edges_of(end, leds):
        return jnp.concatenate([edge_ref[end, led].astype(F32) for led in leds], axis=1)

    def images(ref, leds, low, high):
        return jnp.concatenate([ref[led, low:high].astype(F32) for led in leds], axis=1)

    def step(number, carry):
        for inner in range(PAIRS):
            pair = number * PAIRS + inner
            leds = order_ref[2 * pair], order_ref[2 * pair + 1]
            side_of = lax.broadcasted_iota(jnp.int32, (1, 2 * PUP), 1) // PUP
            alive = jnp.where(2 * pair + side_of < count, scale, 0.0)
            wave = jnp.concatenate([waves[led] for led in leds], axis=1)
            wave_re, wave_im = wave[:PUP], wave[PUP:]
            intensity = wave_re * wave_re + wave_im * wave_im
            own = images(measured_ref, leds, 0, STRIDE)
            upper = images(above_ref, leds, OV - HALF, OV)
            lower = images(below_ref, leds, 0, HALF)
            near_top = jnp.where(has_above, edges_of(1, leds), 0.0)
            near_bottom = jnp.where(has_below, edges_of(0, leds), 0.0)
            first = 2.0 * top2 * (top2 * intensity[:OV] + near_top - jnp.concatenate([upper, own[: OV - HALF]], axis=0))
            middle = 2.0 * (intensity[OV:STRIDE] - own[HALF : STRIDE - HALF])
            last = 2.0 * bottom2 * (bottom2 * intensity[STRIDE:] + near_bottom - jnp.concatenate([own[STRIDE - HALF :], lower], axis=0))
            grad = alive * jnp.concatenate(
                [jnp.where(top_inside, first, 0.0), middle, jnp.where(bottom_inside, last, 0.0)], axis=0
            )
            grad_wave = jnp.concatenate([grad * wave_re, grad * wave_im], axis=0)
            back = right_product(swap_blocks(grad_wave), table_ref[2], table_ref[3])
            grad_field = left_product(table_ref[0], table_ref[1], swap_blocks(back))
            for side in range(2):
                led = leds[side]
                row, col = offsets_ref[0, led], offsets_ref[1, led]
                shift = col % PUP
                lo = side * PUP
                grad_re = grad_field[:PUP, lo : lo + PUP]
                grad_im = grad_field[PUP:, lo : lo + PUP]
                pup_re = pltpu.roll(pupil_ref[0].astype(F32), shift, axis=1)
                pup_im = pltpu.roll(pupil_ref[1].astype(F32), shift, axis=1)
                win_re, win_im = window_of(planes, row, col)
                pieces = (pup_re * grad_re + pup_im * grad_im, pup_re * grad_im - pup_im * grad_re)
                shares = (win_re * grad_re + win_im * grad_im, win_re * grad_im - win_im * grad_re)
                first_block = col // PUP
                second_block = jnp.minimum(first_block + 1, BLOCKS - 1)
                inside = lanes >= shift
                for part in range(2):
                    here_rows = pl.ds(row, PUP)
                    pupil_out[part] += pltpu.roll(shares[part], PUP - shift, axis=1)
                    spec_out[first_block, part, here_rows, :] += jnp.where(inside, pieces[part], 0.0)
                    spec_out[second_block, part, here_rows, :] += jnp.where(inside, 0.0, pieces[part])
        return carry

    lax.fori_loop(0, steps, step, 0)

def vmem():
    return pl.BlockSpec(memory_space=pltpu.VMEM)


def smem():
    return pl.BlockSpec(memory_space=pltpu.SMEM)


def hbm():
    return pl.BlockSpec(memory_space=pltpu.HBM)


def in_hbm(*arrays):
    return [pltpu.with_memory_space_constraint(array, pltpu.HBM) for array in arrays]


def in_smem(*arrays):
    return [pltpu.with_memory_space_constraint(array, pltpu.SMEM) for array in arrays]


def in_vmem(*arrays):
    return [pltpu.with_memory_space_constraint(array, pltpu.VMEM) for array in arrays]


def forward_call(offsets, widths, live, spectrum, pupil, tables, measured):
    lamps = measured.shape[0]
    side = spectrum.shape[-1]
    rows = pltpu.VMEM((lamps, OV, PUP), measured.dtype)
    edge = pltpu.VMEM((2, lamps, OV, PUP), BF16)
    chunks = lamps // (2 * FORWARD_PAIRS)
    return pl.pallas_call(
        forward_kernel,
        out_shape=(
            pltpu.VMEM((lamps, 2 * PUP, PUP), F32),
            edge,
            rows,
            rows,
            pltpu.VMEM((BLOCKS, 2, side, PUP), F32),
            pltpu.VMEM(pupil.shape, pupil.dtype),
            pltpu.VMEM(tables.shape, tables.dtype),
            pltpu.VMEM(measured.shape, measured.dtype),
            pltpu.SMEM(offsets.shape, jnp.int32),
            pltpu.SMEM(widths.shape, jnp.int32),
            pltpu.SMEM(live.shape, jnp.int32),
        ),
        in_specs=[hbm()] * 7,
        out_specs=(vmem(),) * 8 + (smem(),) * 3,
        scratch_shapes=[
            edge,
            pltpu.VMEM(spectrum.shape, spectrum.dtype),
            pltpu.SemaphoreType.DMA((8,)),
            pltpu.SemaphoreType.DMA((2, chunks, len(SENDS))),
            pltpu.SemaphoreType.DMA((2, chunks, len(SENDS))),
            pltpu.SemaphoreType.DMA((2,)),
            pltpu.SemaphoreType.DMA((2,)),
        ],
        compiler_params=pltpu.CompilerParams(
            collective_id=1, has_side_effects=True, vmem_limit_bytes=VMEM_LIMIT
        ),
        name="forward",
    )(*in_hbm(offsets, widths, live, spectrum, pupil, tables, measured))


def backward_call(scale, offsets, widths, live, planes, pupil, tables, measured, above, below, edges, waves):
    lamps = measured.shape[0]
    return pl.pallas_call(
        partial(backward_kernel, scale),
        out_shape=(pltpu.VMEM(planes.shape, F32), pltpu.VMEM(pupil.shape, F32)),
        in_specs=[smem()] * 3 + [vmem()] * 8,
        out_specs=(vmem(), vmem()),
        scratch_shapes=[pltpu.SMEM((lamps + GROUP,), jnp.int32)],
        compiler_params=pltpu.CompilerParams(vmem_limit_bytes=VMEM_LIMIT),
        name="backward",
    )(*in_smem(offsets, widths, live), *in_vmem(planes, pupil, tables, measured, above, below, edges, waves))


def gather_kernel(
    spec_ref, pupil_ref, spec_out, pupil_out, codes, scales, held, held_scales, codes2, scales2, held2, held_scales2,
    send_sems, recv_sems
):
    line, place = my_place()
    opposite = dest_of(line + 1, place)
    beside = [dest_of(line, place + 1 + hop) for hop in range(XS - 1)]
    barrier = pltpu.get_barrier_semaphore()
    for other in [opposite, *beside]:
        pl.semaphore_signal(barrier, inc=1, device_id={"led": other}, device_id_type=MESH)

    def piece(block, part, dest):
        if block is None:
            return pupil_ref[part, pl.ds(pl.multiple_of(dest * PUP_ROWS, PUP_ROWS), PUP_ROWS), :]
        return spec_ref[block, part, pl.ds(pl.multiple_of(dest * SPEC_ROWS, SPEC_ROWS), SPEC_ROWS), :]

    def totals(bundle, dest, parts):
        for number, ((block, part), (low, high)) in enumerate(zip(bundle, bounds_of(bundle))):
            value = piece(block, part, dest)
            for code, scale in parts:
                value += code[low:high, :].astype(F32) * scale[number : number + 1, :]
            yield number, low, high, block, part, value

    def encode(bundle, dest, parts, code, scale):
        for number, low, high, _, _, value in totals(bundle, dest, parts):
            most = jnp.maximum(jnp.max(jnp.abs(value), axis=0, keepdims=True), 1e-30)
            code[low:high, :] = jnp.round(value * (LEVELS / most)).astype(jnp.int16)
            scale[number : number + 1, :] = most * (1.0 / LEVELS)

    def finish(bundle, parts):
        for _, _, _, block, part, value in totals(bundle, mine, parts):
            if block is None:
                pupil_out[part] = value
            else:
                spec_out[part, :, block * PUP : (block + 1) * PUP] = value

    def first_rows(number):
        if number < SENT_A:
            return pl.ds(number * ROWS_A, ROWS_A)
        return pl.ds(SENT_A * ROWS_A + (number - SENT_A) * ROWS_B, ROWS_B)

    def second_rows(number):
        return pl.ds(0, ROWS_A) if number == 0 else pl.ds(ROWS_A + (number - 1) * ROWS_B, ROWS_B)

    used = [0]

    def send(number, rows, other, code, scale, held_code, held_scale):
        pair = []
        here = pl.ds(8 * number, 8)
        targets = held_code.at[rows], held_scale.at[here]
        for src, dst in zip((scale.at[here], code.at[rows]), reversed(targets)):
            sem = used[0]
            used[0] += 1
            pair.append(
                pltpu.make_async_remote_copy(
                    src_ref=src, dst_ref=dst, send_sem=send_sems.at[sem], recv_sem=recv_sems.at[sem],
                    device_id={"led": other}, device_id_type=MESH,
                )
            )
            pair[-1].start()
        return pair, targets

    def arrive(message, sent=False):
        for copy in message[0]:
            if not sent:
                copy.wait_send()
            copy.wait_recv()
        return message[1]

    def first(number, other):
        return send(number, first_rows(number), other, codes, scales, held, held_scales)

    def second(number, other):
        return send(number, second_rows(number), other, codes2, scales2, held2, held_scales2)

    hops = (1, 0, 2)
    mine = dest_of(line, place)

    def encode_first(number, bundle, dest):
        encode(bundle, dest, [], codes.at[first_rows(number)], scales.at[pl.ds(8 * number, 8)])

    for hop in hops:
        encode_first(SENT_A + hop, BUNDLE_B, dest_of(line + 1, place + 1 + hop))
        encode_first(hop, BUNDLE_A, dest_of(line + 1, place + 1 + hop))
    for hop in hops:
        encode_first(XS - 1 + hop, BUNDLE_A, beside[hop])
    encode_first(SENT_A + XS - 1, BUNDLE_B, opposite)
    pl.semaphore_wait(barrier, XS)

    first_b, first_a, last_a, second_b = {}, {}, {}, {}
    for hop in hops:
        first_b[hop] = first(SENT_A + hop, opposite)
        first_a[hop] = first(hop, beside[hop])
    last_b = first(SENT_A + XS - 1, opposite)
    for hop in hops:
        for copy in first_a[hop][0]:
            copy.wait_send()
    for hop in hops:
        last_a[hop] = first(XS - 1 + hop, beside[hop])

    def pass_on(hop):
        parts = [arrive(first_b[hop])]
        encode(BUNDLE_B, beside[hop], parts, codes2.at[second_rows(1 + hop)], scales2.at[pl.ds(8 * (1 + hop), 8)])
        second_b[hop] = second(1 + hop, beside[hop])

    pass_on(hops[0])
    parts = [arrive(first_a[hop], sent=True) for hop in hops]
    encode(BUNDLE_A, opposite, parts, codes2.at[second_rows(0)], scales2.at[pl.ds(0, 8)])
    second_a = second(0, opposite)
    pass_on(hops[1])
    pass_on(hops[2])
    parts = [*(arrive(last_a[hop]) for hop in hops), arrive(second_a)]
    finish(BUNDLE_A, parts)
    parts = [arrive(last_b), *(arrive(second_b[hop]) for hop in hops)]
    finish(BUNDLE_B, parts)


def gather_call(spec_part, pupil_part):
    moved = 2 * (SENT_A + SENT_B + XS)
    code = pltpu.VMEM((CODE_ROWS, PUP), jnp.int16)
    scale = pltpu.VMEM((8 * (SENT_A + SENT_B), PUP), F32)
    code2 = pltpu.VMEM((ROWS_A + (XS - 1) * ROWS_B, PUP), jnp.int16)
    scale2 = pltpu.VMEM((8 * XS, PUP), F32)
    return pl.pallas_call(
        gather_kernel,
        out_shape=(
            pltpu.VMEM((2, SPEC_ROWS, BLOCKS * PUP), F32),
            pltpu.VMEM((2, PUP_ROWS, PUP), F32),
        ),
        in_specs=[vmem()] * 2,
        out_specs=(vmem(), vmem()),
        scratch_shapes=[
            *(code, scale, code, scale),
            *(code2, scale2, code2, scale2),
            pltpu.SemaphoreType.DMA((moved,)),
            pltpu.SemaphoreType.DMA((moved,)),
        ],
        compiler_params=pltpu.CompilerParams(
            collective_id=2, has_side_effects=True, vmem_limit_bytes=VMEM_LIMIT
        ),
        name="reduce_scatter",
    )(*in_vmem(spec_part, pupil_part))


def store_kernel(spec_ref, pupil_ref, spec_out, pupil_out, sems):
    copies = [
        pltpu.make_async_copy(spec_ref, spec_out, sems.at[0]),
        pltpu.make_async_copy(pupil_ref, pupil_out, sems.at[1]),
    ]
    for copy in copies:
        copy.start()
    for copy in copies:
        copy.wait()


def store_call(spec_share, pupil_share):
    return pl.pallas_call(
        store_kernel,
        out_shape=(
            jax.ShapeDtypeStruct(spec_share.shape, F32),
            jax.ShapeDtypeStruct(pupil_share.shape, F32),
        ),
        in_specs=[vmem()] * 2,
        out_specs=(hbm(), hbm()),
        scratch_shapes=[pltpu.SemaphoreType.DMA((2,))],
        compiler_params=pltpu.CompilerParams(vmem_limit_bytes=VMEM_LIMIT),
        name="store",
    )(*in_vmem(spec_share, pupil_share))


def on_device(tables, spectrum, pupil, offsets, widths, live, measured):
    groups = lax.axis_size("led")
    lamps = measured.shape[0]
    scale = 1.0 / math.sqrt(lamps * groups)
    spectrum, pupil, offsets = spectrum[0], pupil[0], offsets[0].T
    waves, near, above, below, planes, pupil, tables, measured, offsets, widths, live = forward_call(
        offsets, widths, live, spectrum, pupil, tables, measured
    )
    parts = backward_call(
        scale, offsets, widths, live, planes, pupil, tables, measured, above, below, near, waves
    )
    spec_share, pupil_share = store_call(*gather_call(*parts))
    return spec_share[None], pupil_share[None]


def solution(mesh):
    tables = dft_tables()

    def run(spectrum, pupil, offsets, widths, live, measured):
        return jax.shard_map(
            on_device,
            mesh=mesh,
            in_specs=(
                P(),
                P("tile", None, None, None),
                P("tile", None, None, None),
                P("tile", "led", None),
                P(),
                P("led"),
                P("led", "tile", None),
            ),
            out_specs=(P("tile", None, "led", None), P("tile", None, "led", None)),
            check_vma=False,
        )(jnp.asarray(tables), spectrum, pupil, offsets, widths, live, measured)

    return run
```

```python
from functools import partial
import math

import jax
import jax.numpy as jnp
import ml_dtypes
import numpy as np
from jax import lax
from jax.experimental import pallas as pl
from jax.experimental.pallas import tpu as pltpu
from jax.sharding import PartitionSpec as P

PUP = 128
OV = 16
HALF = 8
STRIDE = PUP - OV
INNER = STRIDE - OV
BLOCKS = 4
MESH = pl.DeviceIdType.MESH
F32 = jnp.float32
BF16 = jnp.bfloat16
XS, YS = 4, 2
SPEC_ROWS = 512 // (XS * YS)
PUP_ROWS = PUP // (XS * YS)
CHUNKS = [(block, part) for block in range(BLOCKS) for part in range(2)]
SPLIT = 4
BUNDLE_A = CHUNKS[:SPLIT] + [(None, part) for part in range(2)]
BUNDLE_B = CHUNKS[SPLIT:]


def bounds_of(bundle):
    bounds, start = [], 0
    for block, _ in bundle:
        stop = start + (PUP_ROWS if block is None else SPEC_ROWS)
        bounds.append((start, stop))
        start = stop
    return bounds


ROWS_A, ROWS_B = bounds_of(BUNDLE_A)[-1][1], bounds_of(BUNDLE_B)[-1][1]
SENT_A, SENT_B = 2 * (XS - 1), XS
CODE_ROWS = SENT_A * ROWS_A + SENT_B * ROWS_B
LEVELS = 32767.0
FORWARD_PAIRS = 7
SENDS = ((0, 14),)
PAIRS = 6
GROUP = 2 * PAIRS
VMEM_LIMIT = 24 * 1024 * 1024


def dft_tables():
    k = np.arange(PUP)
    angle = 2.0 * np.pi * ((k[:, None] * k[None, :]) % PUP) / PUP
    cosine, sine = np.cos(angle), np.sin(angle)
    inverse = np.block([[cosine, sine], [-sine, cosine]]) / PUP
    forward = np.block([[cosine, -sine], [sine, cosine]])
    parts = []
    for table in (inverse, forward):
        high = table.astype(ml_dtypes.bfloat16)
        low = (table - high.astype(np.float64)).astype(ml_dtypes.bfloat16)
        parts += [high, low]
    return np.stack(parts)


def split(x):
    high = x.astype(BF16)
    return high, (x - high.astype(F32)).astype(BF16)


def right_product(x, high, low):
    xh, xl = split(x)
    product = partial(jnp.dot, preferred_element_type=F32)
    return product(xh, high) + product(xl, high) + product(xh, low)


def left_product(high, low, xh, xl):
    data = jnp.concatenate([xh, xl, xh], axis=0)
    table = jnp.concatenate([high, high, low], axis=1)
    return jnp.dot(table, data, preferred_element_type=F32)


def swap_blocks(x):
    top = jnp.concatenate([x[:PUP, :PUP], x[PUP:, :PUP]], axis=1)
    bottom = jnp.concatenate([x[:PUP, PUP:], x[PUP:, PUP:]], axis=1)
    return jnp.concatenate([top, bottom], axis=0)


def ramp_weights(widths_ref, tile, tiles):
    place = lax.broadcasted_iota(jnp.int32, (OV, PUP), 0).astype(F32)
    above = widths_ref[jnp.maximum(tile - 1, 0)].astype(F32)
    below = widths_ref[jnp.minimum(tile, tiles - 2)].astype(F32)
    top = 1.0 - jnp.clip(0.5 + (HALF - 0.5 - place) / above, 0.0, 1.0)
    bottom = jnp.clip(0.5 + (HALF - 0.5 - place) / below, 0.0, 1.0)
    ones = jnp.ones_like(place)
    return jnp.where(tile > 0, top, ones), jnp.where(tile < tiles - 1, bottom, ones)


def list_live(live_ref, order_ref):
    def body(led, count):
        order_ref[count] = led
        return count + live_ref[led]

    lamps = live_ref.shape[0]
    count = lax.fori_loop(0, lamps, body, jnp.int32(0))
    for extra in range(GROUP):
        order_ref[count + extra] = lamps
    return count


def load_spectrum(spec_ref, planes, part):
    for block in range(BLOCKS):
        planes[block, part] = spec_ref[part, :, block * PUP : (block + 1) * PUP].astype(F32)


def window_of(planes, row, col):
    first = col // PUP
    second = jnp.minimum(first + 1, BLOCKS - 1)
    lanes = lax.broadcasted_iota(jnp.int32, (PUP, PUP), 1)
    inside = lanes >= col % PUP
    return [
        jnp.where(inside, planes[first, part, pl.ds(row, PUP), :], planes[second, part, pl.ds(row, PUP), :])
        for part in range(2)
    ]


def forward_kernel(
    scale,
    offsets_hbm, widths_hbm, live_hbm, spec_hbm, pupil_hbm, table_hbm, measured_hbm,
    middle, ends, near, above, below, planes, pupil_ref, table_ref, measured_ref, offsets_ref, widths_ref, live_ref,
    waves, edges, spec_ref, local_sems, send_sems, recv_sems, image_send, image_recv
):
    tiles = lax.axis_size("tile")
    tile = lax.axis_index("tile")
    up, down = jnp.maximum(tile - 1, 0), jnp.minimum(tile + 1, tiles - 1)
    width = 2 * FORWARD_PAIRS
    steps = waves.shape[0] // width
    local = [
        pltpu.make_async_copy(source, target, local_sems.at[number])
        for number, (source, target) in enumerate(
            (
                (offsets_hbm, offsets_ref),
                (widths_hbm, widths_ref),
                (live_hbm, live_ref),
                (spec_hbm.at[0], spec_ref.at[0]),
                (spec_hbm.at[1], spec_ref.at[1]),
                (pupil_hbm, pupil_ref),
                (table_hbm, table_ref),
                (measured_hbm, measured_ref),
            )
        )
    ]
    for copy in local[:-1]:
        copy.start()
    barrier = pltpu.get_barrier_semaphore()
    has_above, has_below = tile > 0, tile < tiles - 1

    def signal(other):
        pl.semaphore_signal(barrier, inc=1, device_id={"tile": other}, device_id_type=MESH)

    pl.when(has_above)(lambda: signal(up))
    pl.when(has_below)(lambda: signal(down))
    for part in range(2):
        local[3 + part].wait()
        load_spectrum(spec_ref, planes, part)
    local[-1].start()
    for copy in local[:3]:
        copy.wait()
    top, bottom = ramp_weights(widths_ref, tile, tiles)
    top2 = jnp.concatenate([top, top], axis=1)
    bottom2 = jnp.concatenate([bottom, bottom], axis=1)
    for copy in local[5:-1]:
        copy.wait()
    pl.semaphore_wait(barrier, has_above.astype(jnp.int32) + has_below.astype(jnp.int32))

    def remote(source, target, send_sem, recv_sem, other):
        return pltpu.make_async_remote_copy(
            src_ref=source, dst_ref=target, send_sem=send_sem, recv_sem=recv_sem,
            device_id={"tile": other}, device_id_type=MESH,
        )

    sides = ((0, has_above, up), (1, has_below, down))
    strips = ((pl.ds(0, OV), below), (pl.ds(STRIDE - OV, OV), above))

    def image_copy(end, other):
        rows, target = strips[end]
        return remote(measured_hbm.at[:, rows], target, image_send.at[end], image_recv.at[end], other)

    def edge_copy(end, other, number, turn):
        here = pl.ds(number * width + SENDS[turn][0], SENDS[turn][1])
        return remote(
            edges.at[end, here], near.at[end, here], send_sems.at[end, number, turn], recv_sems.at[end, number, turn], other
        )

    for end, present, other in sides:
        pl.when(present)(lambda: image_copy(end, other).start())

    def field_of(led):
        row, col = offsets_ref[0, led], offsets_ref[1, led]
        win_re, win_im = window_of(planes, row, col)
        shift = col % PUP
        pup_re = pltpu.roll(pupil_ref[0].astype(F32), shift, axis=1)
        pup_im = pltpu.roll(pupil_ref[1].astype(F32), shift, axis=1)
        return jnp.concatenate(
            [pup_re * win_re - pup_im * win_im, pup_re * win_im + pup_im * win_re], axis=1
        )

    def step(number, carry):
        for inner in range(FORWARD_PAIRS):
            pair = number * FORWARD_PAIRS + inner
            field = jnp.concatenate([field_of(2 * pair), field_of(2 * pair + 1)], axis=0)
            mixed = right_product(field, table_ref[0], table_ref[1])
            wave = left_product(table_ref[2], table_ref[3], *split(swap_blocks(mixed)))
            first = wave[:OV], wave[PUP : PUP + OV]
            last = wave[STRIDE:PUP], wave[PUP + STRIDE :]
            first = (top2 * (first[0] * first[0] + first[1] * first[1])).astype(BF16)
            last = (bottom2 * (last[0] * last[0] + last[1] * last[1])).astype(BF16)
            for side in range(2):
                lo = side * PUP
                led = 2 * pair + side
                waves[led] = wave[:, lo : lo + PUP]
                for part in range(2):
                    ends[led, part, :OV] = wave[part * PUP : part * PUP + OV, lo : lo + PUP]
                    ends[led, part, OV:] = wave[part * PUP + STRIDE : (part + 1) * PUP, lo : lo + PUP]
                edges[0, led] = first[:, lo : lo + PUP]
                edges[1, led] = last[:, lo : lo + PUP]
            for turn, (low, leds) in enumerate(SENDS):
                if 2 * (inner + 1) == low + leds:
                    for end, present, other in sides:
                        pl.when(present)(lambda: edge_copy(end, other, number, turn).start())
        return carry

    lax.fori_loop(0, steps, step, 0)
    local[-1].wait()

    def inner_rows(led):
        rows = [waves[led, part * PUP + OV : part * PUP + STRIDE] for part in range(2)]
        seen = measured_ref[led].astype(F32)[HALF : STRIDE - HALF]
        grad = (2.0 * scale) * (rows[0] * rows[0] + rows[1] * rows[1] - seen)
        return jnp.concatenate([grad * rows[0], grad * rows[1]], axis=1)

    def inner_step(number, carry):
        for inner in range(FORWARD_PAIRS):
            leds = [2 * (number * FORWARD_PAIRS + inner) + side for side in range(2)]
            rows = jnp.concatenate([inner_rows(led) for led in leds], axis=0)
            for kind, value in enumerate(split(right_product(rows, table_ref[2], table_ref[3]))):
                for side, led in enumerate(leds):
                    for part in range(2):
                        middle[kind, led, part] = value[side * INNER : (side + 1) * INNER, part * PUP : (part + 1) * PUP]
        return carry

    lax.fori_loop(0, steps, inner_step, 0)
    lamps = waves.shape[0]
    for part in range(2):
        ends[lamps, part] = jnp.zeros((2 * OV, PUP), F32)
        for kind in range(2):
            middle[kind, lamps, part] = jnp.zeros((INNER, PUP), BF16)

    def finish(number, carry):
        for turn in range(len(SENDS)):
            for end, present, other in sides:
                pl.when(present)(lambda: edge_copy(end, other, number, turn).wait_send())
                pl.when(sides[1 - end][1])(lambda: edge_copy(end, other, number, turn).wait_recv())
        return carry

    lax.fori_loop(0, steps, finish, 0)
    for end, present, other in sides:
        pl.when(present)(lambda: image_copy(end, other).wait_send())
        pl.when(sides[1 - end][1])(lambda: image_copy(end, other).wait_recv())


def my_place():
    me = lax.axis_index("led")
    return me // XS, me % XS


def dest_of(line, place):
    return (line % YS) * XS + place % XS


def backward_kernel(
    scale, offsets_ref, widths_ref, live_ref, planes, pupil_ref, table_ref, measured_ref, above_ref, below_ref, edge_ref, middle, ends,
    spec_out, pupil_out, order_ref
):
    tiles = lax.axis_size("tile")
    tile = lax.axis_index("tile")
    spec_out[...] = jnp.zeros_like(spec_out)
    pupil_out[...] = jnp.zeros_like(pupil_out)
    count = list_live(live_ref, order_ref)
    steps = (count + GROUP - 1) // GROUP

    top, bottom = ramp_weights(widths_ref, tile, tiles)
    top2 = jnp.concatenate([top, top], axis=1)
    bottom2 = jnp.concatenate([bottom, bottom], axis=1)
    rows = lax.broadcasted_iota(jnp.int32, (OV, 2 * PUP), 0)
    top_inside = (tile > 0) | (rows >= HALF)
    bottom_inside = (tile < tiles - 1) | (rows < HALF)
    has_above = tile > 0
    has_below = tile < tiles - 1
    lanes = lax.broadcasted_iota(jnp.int32, (PUP, PUP), 1)

    lamps = measured_ref.shape[0]

    def spots_of(leds):
        return [jnp.minimum(led, lamps - 1) for led in leds]

    def edges_of(end, spots):
        return jnp.concatenate([edge_ref[end, spot].astype(F32) for spot in spots], axis=1)

    def images(ref, spots, low, high):
        return jnp.concatenate([ref[spot, low:high].astype(F32) for spot in spots], axis=1)

    def end_rows(leds):
        spots = spots_of(leds)
        wave = [jnp.concatenate([ends[led, part] for led in leds], axis=1) for part in range(2)]
        intensity = wave[0] * wave[0] + wave[1] * wave[1]
        upper = images(above_ref, spots, OV - HALF, OV)
        lower = images(below_ref, spots, 0, HALF)
        own_top = images(measured_ref, spots, 0, OV)[: OV - HALF]
        own_bottom = images(measured_ref, spots, STRIDE - OV, STRIDE)[OV - HALF :]
        near_top = jnp.where(has_above, edges_of(1, spots), 0.0)
        near_bottom = jnp.where(has_below, edges_of(0, spots), 0.0)
        first = top2 * (top2 * intensity[:OV] + near_top - jnp.concatenate([upper, own_top], axis=0))
        last = bottom2 * (bottom2 * intensity[OV:] + near_bottom - jnp.concatenate([own_bottom, lower], axis=0))
        grad = (2.0 * scale) * jnp.concatenate(
            [jnp.where(top_inside, first, 0.0), jnp.where(bottom_inside, last, 0.0)], axis=0
        )
        grad_wave = [grad * wave[part] for part in range(2)]
        return [
            jnp.concatenate([grad_wave[part][:, side * PUP : (side + 1) * PUP] for part in range(2)], axis=1)
            for side in range(2)
        ]

    def step(number, carry):
        pairs = [
            [order_ref[2 * (number * PAIRS + inner) + side] for side in range(2)] for inner in range(PAIRS)
        ]
        rows = jnp.concatenate([row for leds in pairs for row in end_rows(leds)], axis=0)
        outer = split(right_product(rows, table_ref[2], table_ref[3]))
        for inner, leds in enumerate(pairs):

            def column(kind, side, part):
                start = 2 * OV * (2 * inner + side)
                lanes_of = slice(part * PUP, (part + 1) * PUP)
                return jnp.concatenate(
                    [
                        outer[kind][start : start + OV, lanes_of],
                        middle[kind, leds[side], part],
                        outer[kind][start + OV : start + 2 * OV, lanes_of],
                    ],
                    axis=0,
                )

            def data(kind):
                columns = [
                    jnp.concatenate([column(kind, side, part) for part in range(2)], axis=0) for side in range(2)
                ]
                return jnp.concatenate(columns, axis=1)

            grad_field = left_product(table_ref[0], table_ref[1], data(0), data(1))
            spots = spots_of(leds)
            for side in range(2):
                row, col = offsets_ref[0, spots[side]], offsets_ref[1, spots[side]]
                shift = col % PUP
                lo = side * PUP
                grad_re = grad_field[:PUP, lo : lo + PUP]
                grad_im = grad_field[PUP:, lo : lo + PUP]
                pup_re = pltpu.roll(pupil_ref[0].astype(F32), shift, axis=1)
                pup_im = pltpu.roll(pupil_ref[1].astype(F32), shift, axis=1)
                win_re, win_im = window_of(planes, row, col)
                pieces = (pup_re * grad_re + pup_im * grad_im, pup_re * grad_im - pup_im * grad_re)
                shares = (win_re * grad_re + win_im * grad_im, win_re * grad_im - win_im * grad_re)
                first_block = col // PUP
                second_block = jnp.minimum(first_block + 1, BLOCKS - 1)
                inside = lanes >= shift
                for part in range(2):
                    here_rows = pl.ds(row, PUP)
                    pupil_out[part] += pltpu.roll(shares[part], PUP - shift, axis=1)
                    spec_out[first_block, part, here_rows, :] += jnp.where(inside, pieces[part], 0.0)
                    spec_out[second_block, part, here_rows, :] += jnp.where(inside, 0.0, pieces[part])
        return carry

    lax.fori_loop(0, steps, step, 0)

def vmem():
    return pl.BlockSpec(memory_space=pltpu.VMEM)


def smem():
    return pl.BlockSpec(memory_space=pltpu.SMEM)


def hbm():
    return pl.BlockSpec(memory_space=pltpu.HBM)


def in_hbm(*arrays):
    return [pltpu.with_memory_space_constraint(array, pltpu.HBM) for array in arrays]


def in_smem(*arrays):
    return [pltpu.with_memory_space_constraint(array, pltpu.SMEM) for array in arrays]


def in_vmem(*arrays):
    return [pltpu.with_memory_space_constraint(array, pltpu.VMEM) for array in arrays]


def forward_call(scale, offsets, widths, live, spectrum, pupil, tables, measured):
    lamps = measured.shape[0]
    side = spectrum.shape[-1]
    rows = pltpu.VMEM((lamps, OV, PUP), measured.dtype)
    edge = pltpu.VMEM((2, lamps, OV, PUP), BF16)
    chunks = lamps // (2 * FORWARD_PAIRS)
    return pl.pallas_call(
        partial(forward_kernel, scale),
        out_shape=(
            pltpu.VMEM((2, lamps + 1, 2, INNER, PUP), BF16),
            pltpu.VMEM((lamps + 1, 2, 2 * OV, PUP), F32),
            edge,
            rows,
            rows,
            pltpu.VMEM((BLOCKS, 2, side, PUP), F32),
            pltpu.VMEM(pupil.shape, pupil.dtype),
            pltpu.VMEM(tables.shape, tables.dtype),
            pltpu.VMEM(measured.shape, measured.dtype),
            pltpu.SMEM(offsets.shape, jnp.int32),
            pltpu.SMEM(widths.shape, jnp.int32),
            pltpu.SMEM(live.shape, jnp.int32),
        ),
        in_specs=[hbm()] * 7,
        out_specs=(vmem(),) * 9 + (smem(),) * 3,
        scratch_shapes=[
            pltpu.VMEM((lamps, 2 * PUP, PUP), F32),
            edge,
            pltpu.VMEM(spectrum.shape, spectrum.dtype),
            pltpu.SemaphoreType.DMA((8,)),
            pltpu.SemaphoreType.DMA((2, chunks, len(SENDS))),
            pltpu.SemaphoreType.DMA((2, chunks, len(SENDS))),
            pltpu.SemaphoreType.DMA((2,)),
            pltpu.SemaphoreType.DMA((2,)),
        ],
        compiler_params=pltpu.CompilerParams(
            collective_id=1, has_side_effects=True, vmem_limit_bytes=VMEM_LIMIT
        ),
        name="forward",
    )(*in_hbm(offsets, widths, live, spectrum, pupil, tables, measured))


def backward_call(scale, offsets, widths, live, planes, pupil, tables, measured, above, below, edges, middle, ends):
    lamps = measured.shape[0]
    return pl.pallas_call(
        partial(backward_kernel, scale),
        out_shape=(pltpu.VMEM(planes.shape, F32), pltpu.VMEM(pupil.shape, F32)),
        in_specs=[smem()] * 3 + [vmem()] * 9,
        out_specs=(vmem(), vmem()),
        scratch_shapes=[pltpu.SMEM((lamps + GROUP,), jnp.int32)],
        compiler_params=pltpu.CompilerParams(vmem_limit_bytes=VMEM_LIMIT),
        name="backward",
    )(*in_smem(offsets, widths, live), *in_vmem(planes, pupil, tables, measured, above, below, edges, middle, ends))


def gather_kernel(
    spec_ref, pupil_ref, spec_out, pupil_out, codes, scales, held, held_scales, codes2, scales2, held2, held_scales2,
    send_sems, recv_sems
):
    line, place = my_place()
    opposite = dest_of(line + 1, place)
    beside = [dest_of(line, place + 1 + hop) for hop in range(XS - 1)]
    barrier = pltpu.get_barrier_semaphore()
    for other in [opposite, *beside]:
        pl.semaphore_signal(barrier, inc=1, device_id={"led": other}, device_id_type=MESH)

    def piece(block, part, dest):
        if block is None:
            return pupil_ref[part, pl.ds(pl.multiple_of(dest * PUP_ROWS, PUP_ROWS), PUP_ROWS), :]
        return spec_ref[block, part, pl.ds(pl.multiple_of(dest * SPEC_ROWS, SPEC_ROWS), SPEC_ROWS), :]

    def totals(bundle, dest, parts):
        for number, ((block, part), (low, high)) in enumerate(zip(bundle, bounds_of(bundle))):
            value = piece(block, part, dest)
            for code, scale in parts:
                value += code[low:high, :].astype(F32) * scale[number : number + 1, :]
            yield number, low, high, block, part, value

    def encode(bundle, dest, parts, code, scale):
        for number, low, high, _, _, value in totals(bundle, dest, parts):
            most = jnp.maximum(jnp.max(jnp.abs(value), axis=0, keepdims=True), 1e-30)
            code[low:high, :] = jnp.round(value * (LEVELS / most)).astype(jnp.int16)
            scale[number : number + 1, :] = most * (1.0 / LEVELS)

    def finish(bundle, parts):
        for _, _, _, block, part, value in totals(bundle, mine, parts):
            if block is None:
                pupil_out[part] = value
            else:
                spec_out[part, :, block * PUP : (block + 1) * PUP] = value

    def first_rows(number):
        if number < SENT_A:
            return pl.ds(number * ROWS_A, ROWS_A)
        return pl.ds(SENT_A * ROWS_A + (number - SENT_A) * ROWS_B, ROWS_B)

    def second_rows(number):
        return pl.ds(0, ROWS_A) if number == 0 else pl.ds(ROWS_A + (number - 1) * ROWS_B, ROWS_B)

    used = [0]

    def send(number, rows, other, code, scale, held_code, held_scale):
        pair = []
        here = pl.ds(8 * number, 8)
        targets = held_code.at[rows], held_scale.at[here]
        for src, dst in zip((scale.at[here], code.at[rows]), reversed(targets)):
            sem = used[0]
            used[0] += 1
            pair.append(
                pltpu.make_async_remote_copy(
                    src_ref=src, dst_ref=dst, send_sem=send_sems.at[sem], recv_sem=recv_sems.at[sem],
                    device_id={"led": other}, device_id_type=MESH,
                )
            )
            pair[-1].start()
        return pair, targets

    def arrive(message, sent=False):
        for copy in message[0]:
            if not sent:
                copy.wait_send()
            copy.wait_recv()
        return message[1]

    def first(number, other):
        return send(number, first_rows(number), other, codes, scales, held, held_scales)

    def second(number, other):
        return send(number, second_rows(number), other, codes2, scales2, held2, held_scales2)

    hops = (1, 0, 2)
    mine = dest_of(line, place)

    def encode_first(number, bundle, dest):
        encode(bundle, dest, [], codes.at[first_rows(number)], scales.at[pl.ds(8 * number, 8)])

    for hop in hops:
        encode_first(SENT_A + hop, BUNDLE_B, dest_of(line + 1, place + 1 + hop))
        encode_first(hop, BUNDLE_A, dest_of(line + 1, place + 1 + hop))
    for hop in hops:
        encode_first(XS - 1 + hop, BUNDLE_A, beside[hop])
    encode_first(SENT_A + XS - 1, BUNDLE_B, opposite)
    pl.semaphore_wait(barrier, XS)

    first_b, first_a, last_a, second_b = {}, {}, {}, {}
    for hop in hops:
        first_b[hop] = first(SENT_A + hop, opposite)
        first_a[hop] = first(hop, beside[hop])
    last_b = first(SENT_A + XS - 1, opposite)
    for hop in hops:
        for copy in first_a[hop][0]:
            copy.wait_send()
    for hop in hops:
        last_a[hop] = first(XS - 1 + hop, beside[hop])

    def pass_on(hop):
        parts = [arrive(first_b[hop])]
        encode(BUNDLE_B, beside[hop], parts, codes2.at[second_rows(1 + hop)], scales2.at[pl.ds(8 * (1 + hop), 8)])
        second_b[hop] = second(1 + hop, beside[hop])

    pass_on(hops[0])
    parts = [arrive(first_a[hop], sent=True) for hop in hops]
    encode(BUNDLE_A, opposite, parts, codes2.at[second_rows(0)], scales2.at[pl.ds(0, 8)])
    second_a = second(0, opposite)
    pass_on(hops[1])
    pass_on(hops[2])
    parts = [*(arrive(last_a[hop]) for hop in hops), arrive(second_a)]
    finish(BUNDLE_A, parts)
    parts = [arrive(last_b), *(arrive(second_b[hop]) for hop in hops)]
    finish(BUNDLE_B, parts)


def gather_call(spec_part, pupil_part):
    moved = 2 * (SENT_A + SENT_B + XS)
    code = pltpu.VMEM((CODE_ROWS, PUP), jnp.int16)
    scale = pltpu.VMEM((8 * (SENT_A + SENT_B), PUP), F32)
    code2 = pltpu.VMEM((ROWS_A + (XS - 1) * ROWS_B, PUP), jnp.int16)
    scale2 = pltpu.VMEM((8 * XS, PUP), F32)
    return pl.pallas_call(
        gather_kernel,
        out_shape=(
            pltpu.VMEM((2, SPEC_ROWS, BLOCKS * PUP), F32),
            pltpu.VMEM((2, PUP_ROWS, PUP), F32),
        ),
        in_specs=[vmem()] * 2,
        out_specs=(vmem(), vmem()),
        scratch_shapes=[
            *(code, scale, code, scale),
            *(code2, scale2, code2, scale2),
            pltpu.SemaphoreType.DMA((moved,)),
            pltpu.SemaphoreType.DMA((moved,)),
        ],
        compiler_params=pltpu.CompilerParams(
            collective_id=2, has_side_effects=True, vmem_limit_bytes=VMEM_LIMIT
        ),
        name="reduce_scatter",
    )(*in_vmem(spec_part, pupil_part))


def store_kernel(spec_ref, pupil_ref, spec_out, pupil_out, sems):
    copies = [
        pltpu.make_async_copy(spec_ref, spec_out, sems.at[0]),
        pltpu.make_async_copy(pupil_ref, pupil_out, sems.at[1]),
    ]
    for copy in copies:
        copy.start()
    for copy in copies:
        copy.wait()


def store_call(spec_share, pupil_share):
    return pl.pallas_call(
        store_kernel,
        out_shape=(
            jax.ShapeDtypeStruct(spec_share.shape, F32),
            jax.ShapeDtypeStruct(pupil_share.shape, F32),
        ),
        in_specs=[vmem()] * 2,
        out_specs=(hbm(), hbm()),
        scratch_shapes=[pltpu.SemaphoreType.DMA((2,))],
        compiler_params=pltpu.CompilerParams(vmem_limit_bytes=VMEM_LIMIT),
        name="store",
    )(*in_vmem(spec_share, pupil_share))


def on_device(tables, spectrum, pupil, offsets, widths, live, measured):
    groups = lax.axis_size("led")
    lamps = measured.shape[0]
    scale = 1.0 / math.sqrt(lamps * groups)
    spectrum, pupil, offsets = spectrum[0], pupil[0], offsets[0].T
    middle, ends, near, above, below, planes, pupil, tables, measured, offsets, widths, live = forward_call(
        scale, offsets, widths, live, spectrum, pupil, tables, measured
    )
    parts = backward_call(
        scale, offsets, widths, live, planes, pupil, tables, measured, above, below, near, middle, ends
    )
    spec_share, pupil_share = store_call(*gather_call(*parts))
    return spec_share[None], pupil_share[None]


def solution(mesh):
    tables = dft_tables()

    def run(spectrum, pupil, offsets, widths, live, measured):
        return jax.shard_map(
            on_device,
            mesh=mesh,
            in_specs=(
                P(),
                P("tile", None, None, None),
                P("tile", None, None, None),
                P("tile", "led", None),
                P(),
                P("led"),
                P("led", "tile", None),
            ),
            out_specs=(P("tile", None, "led", None), P("tile", None, "led", None)),
            check_vma=False,
        )(jnp.asarray(tables), spectrum, pupil, offsets, widths, live, measured)

    return run
```

```python
from functools import partial
import math

import jax
import jax.numpy as jnp
import ml_dtypes
import numpy as np
from jax import lax
from jax.experimental import pallas as pl
from jax.experimental.pallas import tpu as pltpu
from jax.sharding import PartitionSpec as P

PUP = 128
OV = 16
HALF = 8
STRIDE = PUP - OV
INNER = STRIDE - OV
BLOCKS = 4
MESH = pl.DeviceIdType.MESH
F32 = jnp.float32
BF16 = jnp.bfloat16
XS, YS = 4, 2
SPEC_ROWS = 512 // (XS * YS)
PUP_ROWS = PUP // (XS * YS)
CHUNKS = [(block, part) for block in range(BLOCKS) for part in range(2)]
SPLIT = 4
BUNDLE_A = CHUNKS[:SPLIT] + [(None, part) for part in range(2)]
BUNDLE_B = CHUNKS[SPLIT:]


def bounds_of(bundle):
    bounds, start = [], 0
    for block, _ in bundle:
        stop = start + (PUP_ROWS if block is None else SPEC_ROWS)
        bounds.append((start, stop))
        start = stop
    return bounds


ROWS_A, ROWS_B = bounds_of(BUNDLE_A)[-1][1], bounds_of(BUNDLE_B)[-1][1]
SENT_A, SENT_B = 2 * (XS - 1), XS
CODE_ROWS = SENT_A * ROWS_A + SENT_B * ROWS_B
LEVELS = 32767.0
FORWARD_PAIRS = 7
SENDS = ((0, 14),)
PAIRS = 6
GROUP = 2 * PAIRS
VMEM_LIMIT = 24 * 1024 * 1024


def dft_tables():
    k = np.arange(PUP)
    angle = 2.0 * np.pi * ((k[:, None] * k[None, :]) % PUP) / PUP
    cosine, sine = np.cos(angle), np.sin(angle)
    inverse = np.block([[cosine, sine], [-sine, cosine]]) / PUP
    forward = np.block([[cosine, -sine], [sine, cosine]])
    parts = []
    for table in (inverse, forward):
        high = table.astype(ml_dtypes.bfloat16)
        low = (table - high.astype(np.float64)).astype(ml_dtypes.bfloat16)
        parts += [high, low]
    return np.stack(parts)


def split(x):
    high = x.astype(BF16)
    return high, (x - high.astype(F32)).astype(BF16)


def right_product(x, high, low):
    xh, xl = split(x)
    product = partial(jnp.dot, preferred_element_type=F32)
    return product(xh, high) + product(xl, high) + product(xh, low)


def left_product(high, low, xh, xl):
    data = jnp.concatenate([xh, xl, xh], axis=0)
    table = jnp.concatenate([high, high, low], axis=1)
    return jnp.dot(table, data, preferred_element_type=F32)


def swap_blocks(x):
    top = jnp.concatenate([x[:PUP, :PUP], x[PUP:, :PUP]], axis=1)
    bottom = jnp.concatenate([x[:PUP, PUP:], x[PUP:, PUP:]], axis=1)
    return jnp.concatenate([top, bottom], axis=0)


def ramp_weights(widths_ref, tile, tiles):
    place = lax.broadcasted_iota(jnp.int32, (OV, PUP), 0).astype(F32)
    above = widths_ref[jnp.maximum(tile - 1, 0)].astype(F32)
    below = widths_ref[jnp.minimum(tile, tiles - 2)].astype(F32)
    top = 1.0 - jnp.clip(0.5 + (HALF - 0.5 - place) / above, 0.0, 1.0)
    bottom = jnp.clip(0.5 + (HALF - 0.5 - place) / below, 0.0, 1.0)
    ones = jnp.ones_like(place)
    return jnp.where(tile > 0, top, ones), jnp.where(tile < tiles - 1, bottom, ones)


def list_live(live_ref, order_ref):
    def body(led, count):
        order_ref[count] = led
        return count + live_ref[led]

    lamps = live_ref.shape[0]
    count = lax.fori_loop(0, lamps, body, jnp.int32(0))
    for extra in range(GROUP):
        order_ref[count + extra] = lamps
    return count


def load_spectrum(spec_ref, planes, part):
    for block in range(BLOCKS):
        planes[block, part] = spec_ref[part, :, block * PUP : (block + 1) * PUP].astype(F32)


def window_of(planes, row, col):
    first = col // PUP
    second = jnp.minimum(first + 1, BLOCKS - 1)
    lanes = lax.broadcasted_iota(jnp.int32, (PUP, PUP), 1)
    inside = lanes >= col % PUP
    return [
        jnp.where(inside, planes[first, part, pl.ds(row, PUP), :], planes[second, part, pl.ds(row, PUP), :])
        for part in range(2)
    ]


def forward_kernel(
    scale,
    offsets_hbm, widths_hbm, live_hbm, spec_hbm, pupil_hbm, table_hbm, measured_hbm,
    middle, ends, near, above, below, planes, pupil_ref, table_ref, measured_ref, offsets_ref, widths_ref, live_ref,
    waves, edges, spec_ref, local_sems, send_sems, recv_sems, image_send, image_recv
):
    tiles = lax.axis_size("tile")
    tile = lax.axis_index("tile")
    up, down = jnp.maximum(tile - 1, 0), jnp.minimum(tile + 1, tiles - 1)
    width = 2 * FORWARD_PAIRS
    steps = waves.shape[0] // width
    local = [
        pltpu.make_async_copy(source, target, local_sems.at[number])
        for number, (source, target) in enumerate(
            (
                (offsets_hbm, offsets_ref),
                (widths_hbm, widths_ref),
                (live_hbm, live_ref),
                (spec_hbm.at[0], spec_ref.at[0]),
                (spec_hbm.at[1], spec_ref.at[1]),
                (pupil_hbm, pupil_ref),
                (table_hbm, table_ref),
                (measured_hbm, measured_ref),
            )
        )
    ]
    for copy in local[:-1]:
        copy.start()
    barrier = pltpu.get_barrier_semaphore()
    has_above, has_below = tile > 0, tile < tiles - 1

    def signal(other):
        pl.semaphore_signal(barrier, inc=1, device_id={"tile": other}, device_id_type=MESH)

    pl.when(has_above)(lambda: signal(up))
    pl.when(has_below)(lambda: signal(down))
    for part in range(2):
        local[3 + part].wait()
        load_spectrum(spec_ref, planes, part)
    local[-1].start()
    for copy in local[:3]:
        copy.wait()
    top, bottom = ramp_weights(widths_ref, tile, tiles)
    top2 = jnp.concatenate([top, top], axis=1)
    bottom2 = jnp.concatenate([bottom, bottom], axis=1)
    for copy in local[5:-1]:
        copy.wait()
    pl.semaphore_wait(barrier, has_above.astype(jnp.int32) + has_below.astype(jnp.int32))

    def remote(source, target, send_sem, recv_sem, other):
        return pltpu.make_async_remote_copy(
            src_ref=source, dst_ref=target, send_sem=send_sem, recv_sem=recv_sem,
            device_id={"tile": other}, device_id_type=MESH,
        )

    sides = ((0, has_above, up), (1, has_below, down))
    strips = ((pl.ds(0, OV), below), (pl.ds(STRIDE - OV, OV), above))

    def image_copy(end, other):
        rows, target = strips[end]
        return remote(measured_hbm.at[:, rows], target, image_send.at[end], image_recv.at[end], other)

    def edge_copy(end, other, number, turn):
        here = pl.ds(number * width + SENDS[turn][0], SENDS[turn][1])
        return remote(
            edges.at[end, here], near.at[end, here], send_sems.at[end, number, turn], recv_sems.at[end, number, turn], other
        )

    for end, present, other in sides:
        pl.when(present)(lambda: image_copy(end, other).start())

    def field_of(led):
        row, col = offsets_ref[0, led], offsets_ref[1, led]
        win_re, win_im = window_of(planes, row, col)
        shift = col % PUP
        pup_re = pltpu.roll(pupil_ref[0].astype(F32), shift, axis=1)
        pup_im = pltpu.roll(pupil_ref[1].astype(F32), shift, axis=1)
        return jnp.concatenate(
            [pup_re * win_re - pup_im * win_im, pup_re * win_im + pup_im * win_re], axis=1
        )

    def step(number, carry):
        for inner in range(FORWARD_PAIRS):
            pair = number * FORWARD_PAIRS + inner
            field = jnp.concatenate([field_of(2 * pair), field_of(2 * pair + 1)], axis=0)
            mixed = right_product(field, table_ref[0], table_ref[1])
            wave = left_product(table_ref[2], table_ref[3], *split(swap_blocks(mixed)))
            first = wave[:OV], wave[PUP : PUP + OV]
            last = wave[STRIDE:PUP], wave[PUP + STRIDE :]
            first = (top2 * (first[0] * first[0] + first[1] * first[1])).astype(BF16)
            last = (bottom2 * (last[0] * last[0] + last[1] * last[1])).astype(BF16)
            for side in range(2):
                lo = side * PUP
                led = 2 * pair + side
                waves[led] = wave[:, lo : lo + PUP]
                for part in range(2):
                    ends[led, part, :OV] = wave[part * PUP : part * PUP + OV, lo : lo + PUP]
                    ends[led, part, OV:] = wave[part * PUP + STRIDE : (part + 1) * PUP, lo : lo + PUP]
                edges[0, led] = first[:, lo : lo + PUP]
                edges[1, led] = last[:, lo : lo + PUP]
            for turn, (low, leds) in enumerate(SENDS):
                if 2 * (inner + 1) == low + leds:
                    for end, present, other in sides:
                        pl.when(present)(lambda: edge_copy(end, other, number, turn).start())
        return carry

    lax.fori_loop(0, steps, step, 0)
    local[-1].wait()

    def inner_rows(led):
        rows = [waves[led, part * PUP + OV : part * PUP + STRIDE] for part in range(2)]
        seen = measured_ref[led].astype(F32)[HALF : STRIDE - HALF]
        grad = (2.0 * scale) * (rows[0] * rows[0] + rows[1] * rows[1] - seen)
        return jnp.concatenate([grad * rows[0], grad * rows[1]], axis=1)

    def inner_step(number, carry):
        for inner in range(FORWARD_PAIRS):
            leds = [2 * (number * FORWARD_PAIRS + inner) + side for side in range(2)]
            rows = jnp.concatenate([inner_rows(led) for led in leds], axis=0)
            for kind, value in enumerate(split(right_product(rows, table_ref[2], table_ref[3]))):
                for side, led in enumerate(leds):
                    for part in range(2):
                        middle[kind, led, part] = value[side * INNER : (side + 1) * INNER, part * PUP : (part + 1) * PUP]
        return carry

    lax.fori_loop(0, steps, inner_step, 0)
    lamps = waves.shape[0]
    for part in range(2):
        ends[lamps, part] = jnp.zeros((2 * OV, PUP), F32)
        for kind in range(2):
            middle[kind, lamps, part] = jnp.zeros((INNER, PUP), BF16)

    def finish(number, carry):
        for turn in range(len(SENDS)):
            for end, present, other in sides:
                pl.when(present)(lambda: edge_copy(end, other, number, turn).wait_send())
                pl.when(sides[1 - end][1])(lambda: edge_copy(end, other, number, turn).wait_recv())
        return carry

    lax.fori_loop(0, steps, finish, 0)
    for end, present, other in sides:
        pl.when(present)(lambda: image_copy(end, other).wait_send())
        pl.when(sides[1 - end][1])(lambda: image_copy(end, other).wait_recv())


def my_place():
    me = lax.axis_index("led")
    return me // XS, me % XS


def dest_of(line, place):
    return (line % YS) * XS + place % XS


def backward_kernel(
    scale, offsets_ref, widths_ref, live_ref, planes, pupil_ref, table_ref, measured_ref, above_ref, below_ref, edge_ref, middle, ends,
    spec_out, pupil_out, order_ref
):
    tiles = lax.axis_size("tile")
    tile = lax.axis_index("tile")
    spec_out[...] = jnp.zeros_like(spec_out)
    pupil_out[...] = jnp.zeros_like(pupil_out)
    count = list_live(live_ref, order_ref)
    steps = (count + GROUP - 1) // GROUP

    top, bottom = ramp_weights(widths_ref, tile, tiles)
    top2 = jnp.concatenate([top, top], axis=1)
    bottom2 = jnp.concatenate([bottom, bottom], axis=1)
    rows = lax.broadcasted_iota(jnp.int32, (OV, 2 * PUP), 0)
    top_inside = (tile > 0) | (rows >= HALF)
    bottom_inside = (tile < tiles - 1) | (rows < HALF)
    has_above = tile > 0
    has_below = tile < tiles - 1
    lanes = lax.broadcasted_iota(jnp.int32, (PUP, PUP), 1)

    lamps = measured_ref.shape[0]

    def spots_of(leds):
        return [jnp.minimum(led, lamps - 1) for led in leds]

    def edges_of(end, spots):
        return jnp.concatenate([edge_ref[end, spot].astype(F32) for spot in spots], axis=1)

    def images(ref, spots, low, high):
        return jnp.concatenate([ref[spot, low:high].astype(F32) for spot in spots], axis=1)

    def end_rows(leds):
        spots = spots_of(leds)
        wave = [jnp.concatenate([ends[led, part] for led in leds], axis=1) for part in range(2)]
        intensity = wave[0] * wave[0] + wave[1] * wave[1]
        upper = images(above_ref, spots, OV - HALF, OV)
        lower = images(below_ref, spots, 0, HALF)
        own_top = images(measured_ref, spots, 0, OV)[: OV - HALF]
        own_bottom = images(measured_ref, spots, STRIDE - OV, STRIDE)[OV - HALF :]
        near_top = jnp.where(has_above, edges_of(1, spots), 0.0)
        near_bottom = jnp.where(has_below, edges_of(0, spots), 0.0)
        first = top2 * (top2 * intensity[:OV] + near_top - jnp.concatenate([upper, own_top], axis=0))
        last = bottom2 * (bottom2 * intensity[OV:] + near_bottom - jnp.concatenate([own_bottom, lower], axis=0))
        grad = (2.0 * scale) * jnp.concatenate(
            [jnp.where(top_inside, first, 0.0), jnp.where(bottom_inside, last, 0.0)], axis=0
        )
        grad_wave = [grad * wave[part] for part in range(2)]
        return [
            jnp.concatenate([grad_wave[part][:, side * PUP : (side + 1) * PUP] for part in range(2)], axis=1)
            for side in range(2)
        ]

    def step(number, carry):
        pairs = [
            [order_ref[2 * (number * PAIRS + inner) + side] for side in range(2)] for inner in range(PAIRS)
        ]
        rows = jnp.concatenate([row for leds in pairs for row in end_rows(leds)], axis=0)
        outer = split(right_product(rows, table_ref[2], table_ref[3]))
        for inner, leds in enumerate(pairs):

            def column(kind, side, part):
                start = 2 * OV * (2 * inner + side)
                lanes_of = slice(part * PUP, (part + 1) * PUP)
                return jnp.concatenate(
                    [
                        outer[kind][start : start + OV, lanes_of],
                        middle[kind, leds[side], part],
                        outer[kind][start + OV : start + 2 * OV, lanes_of],
                    ],
                    axis=0,
                )

            def data(kind):
                columns = [
                    jnp.concatenate([column(kind, side, part) for part in range(2)], axis=0) for side in range(2)
                ]
                return jnp.concatenate(columns, axis=1)

            grad_field = left_product(table_ref[0], table_ref[1], data(0), data(1))
            spots = spots_of(leds)
            for side in range(2):
                row, col = offsets_ref[0, spots[side]], offsets_ref[1, spots[side]]
                shift = col % PUP
                lo = side * PUP
                grad_re = grad_field[:PUP, lo : lo + PUP]
                grad_im = grad_field[PUP:, lo : lo + PUP]
                pup_re = pltpu.roll(pupil_ref[0].astype(F32), shift, axis=1)
                pup_im = pltpu.roll(pupil_ref[1].astype(F32), shift, axis=1)
                win_re, win_im = window_of(planes, row, col)
                pieces = (pup_re * grad_re + pup_im * grad_im, pup_re * grad_im - pup_im * grad_re)
                shares = (win_re * grad_re + win_im * grad_im, win_re * grad_im - win_im * grad_re)
                first_block = col // PUP
                second_block = jnp.minimum(first_block + 1, BLOCKS - 1)
                inside = lanes >= shift
                for part in range(2):
                    here_rows = pl.ds(row, PUP)
                    pupil_out[part] += pltpu.roll(shares[part], PUP - shift, axis=1)
                    spec_out[first_block, part, here_rows, :] += jnp.where(inside, pieces[part], 0.0)
                    spec_out[second_block, part, here_rows, :] += jnp.where(inside, 0.0, pieces[part])
        return carry

    lax.fori_loop(0, steps, step, 0)

def vmem():
    return pl.BlockSpec(memory_space=pltpu.VMEM)


def smem():
    return pl.BlockSpec(memory_space=pltpu.SMEM)


def hbm():
    return pl.BlockSpec(memory_space=pltpu.HBM)


def in_hbm(*arrays):
    return [pltpu.with_memory_space_constraint(array, pltpu.HBM) for array in arrays]


def in_smem(*arrays):
    return [pltpu.with_memory_space_constraint(array, pltpu.SMEM) for array in arrays]


def in_vmem(*arrays):
    return [pltpu.with_memory_space_constraint(array, pltpu.VMEM) for array in arrays]


def forward_call(scale, offsets, widths, live, spectrum, pupil, tables, measured):
    lamps = measured.shape[0]
    side = spectrum.shape[-1]
    rows = pltpu.VMEM((lamps, OV, PUP), measured.dtype)
    edge = pltpu.VMEM((2, lamps, OV, PUP), BF16)
    chunks = lamps // (2 * FORWARD_PAIRS)
    return pl.pallas_call(
        partial(forward_kernel, scale),
        out_shape=(
            pltpu.VMEM((2, lamps + 1, 2, INNER, PUP), BF16),
            pltpu.VMEM((lamps + 1, 2, 2 * OV, PUP), F32),
            edge,
            rows,
            rows,
            pltpu.VMEM((BLOCKS, 2, side, PUP), F32),
            pltpu.VMEM(pupil.shape, pupil.dtype),
            pltpu.VMEM(tables.shape, tables.dtype),
            pltpu.VMEM(measured.shape, measured.dtype),
            pltpu.SMEM(offsets.shape, jnp.int32),
            pltpu.SMEM(widths.shape, jnp.int32),
            pltpu.SMEM(live.shape, jnp.int32),
        ),
        in_specs=[hbm()] * 7,
        out_specs=(vmem(),) * 9 + (smem(),) * 3,
        scratch_shapes=[
            pltpu.VMEM((lamps, 2 * PUP, PUP), F32),
            edge,
            pltpu.VMEM(spectrum.shape, spectrum.dtype),
            pltpu.SemaphoreType.DMA((8,)),
            pltpu.SemaphoreType.DMA((2, chunks, len(SENDS))),
            pltpu.SemaphoreType.DMA((2, chunks, len(SENDS))),
            pltpu.SemaphoreType.DMA((2,)),
            pltpu.SemaphoreType.DMA((2,)),
        ],
        compiler_params=pltpu.CompilerParams(
            collective_id=1, has_side_effects=True, vmem_limit_bytes=VMEM_LIMIT
        ),
        name="forward",
    )(*in_hbm(offsets, widths, live, spectrum, pupil, tables, measured))


def backward_call(scale, offsets, widths, live, planes, pupil, tables, measured, above, below, edges, middle, ends):
    lamps = measured.shape[0]
    return pl.pallas_call(
        partial(backward_kernel, scale),
        out_shape=(pltpu.VMEM(planes.shape, F32), pltpu.VMEM(pupil.shape, F32)),
        in_specs=[smem()] * 3 + [vmem()] * 9,
        out_specs=(vmem(), vmem()),
        scratch_shapes=[pltpu.SMEM((lamps + GROUP,), jnp.int32)],
        compiler_params=pltpu.CompilerParams(vmem_limit_bytes=VMEM_LIMIT),
        name="backward",
    )(*in_smem(offsets, widths, live), *in_vmem(planes, pupil, tables, measured, above, below, edges, middle, ends))


def gather_kernel(
    spec_ref, pupil_ref, spec_out, pupil_out, codes, scales, held, held_scales, codes2, scales2, held2, held_scales2,
    send_sems, recv_sems
):
    line, place = my_place()
    opposite = dest_of(line + 1, place)
    beside = [dest_of(line, place + 1 + hop) for hop in range(XS - 1)]
    barrier = pltpu.get_barrier_semaphore()
    for other in [opposite, *beside]:
        pl.semaphore_signal(barrier, inc=1, device_id={"led": other}, device_id_type=MESH)

    def piece(block, part, dest):
        if block is None:
            return pupil_ref[part, pl.ds(pl.multiple_of(dest * PUP_ROWS, PUP_ROWS), PUP_ROWS), :]
        return spec_ref[block, part, pl.ds(pl.multiple_of(dest * SPEC_ROWS, SPEC_ROWS), SPEC_ROWS), :]

    def totals(bundle, dest, parts):
        for number, ((block, part), (low, high)) in enumerate(zip(bundle, bounds_of(bundle))):
            value = piece(block, part, dest)
            for code, scale in parts:
                value += code[low:high, :].astype(F32) * scale[number : number + 1, :]
            yield number, low, high, block, part, value

    def encode(bundle, dest, parts, code, scale):
        for number, low, high, _, _, value in totals(bundle, dest, parts):
            most = jnp.maximum(jnp.max(jnp.abs(value), axis=0, keepdims=True), 1e-30)
            code[low:high, :] = jnp.round(value * (LEVELS / most)).astype(jnp.int16)
            scale[number : number + 1, :] = most * (1.0 / LEVELS)

    def finish(bundle, parts):
        for _, _, _, block, part, value in totals(bundle, mine, parts):
            if block is None:
                pupil_out[part] = value
            else:
                spec_out[part, :, block * PUP : (block + 1) * PUP] = value

    def first_rows(number):
        if number < SENT_A:
            return pl.ds(number * ROWS_A, ROWS_A)
        return pl.ds(SENT_A * ROWS_A + (number - SENT_A) * ROWS_B, ROWS_B)

    def second_rows(number):
        return pl.ds(0, ROWS_A) if number == 0 else pl.ds(ROWS_A + (number - 1) * ROWS_B, ROWS_B)

    used = [0]

    def remote(src, dst, other):
        sem = used[0]
        used[0] += 1
        copy = pltpu.make_async_remote_copy(
            src_ref=src, dst_ref=dst, send_sem=send_sems.at[sem], recv_sem=recv_sems.at[sem],
            device_id={"led": other}, device_id_type=MESH,
        )
        copy.start()
        return copy

    def first_scale(number):
        slot = number if number >= SENT_A else number % (XS - 1) * 2 + number // (XS - 1)
        return pl.ds(8 * slot, 8)

    def arrive(message, sent=False):
        for copy in message[0]:
            if not sent:
                copy.wait_send()
            copy.wait_recv()
        return message[1]

    def first(number, other):
        here = first_rows(number)
        return [remote(codes.at[here], held.at[here], other)], (held.at[here], held_scales.at[first_scale(number)])

    def first_scales(start, rows, other):
        here = pl.ds(start, rows)
        return remote(scales.at[here], held_scales.at[here], other)

    def second(number, other):
        here, scale = second_rows(number), pl.ds(8 * number, 8)
        targets = held2.at[here], held_scales2.at[scale]
        copies = [remote(scales2.at[scale], targets[1], other), remote(codes2.at[here], targets[0], other)]
        return copies, targets

    hops = (1, 0, 2)
    mine = dest_of(line, place)

    def encode_first(number, bundle, dest):
        encode(bundle, dest, [], codes.at[first_rows(number)], scales.at[first_scale(number)])

    for hop in hops:
        encode_first(SENT_A + hop, BUNDLE_B, dest_of(line + 1, place + 1 + hop))
        encode_first(hop, BUNDLE_A, dest_of(line + 1, place + 1 + hop))
    for hop in hops:
        encode_first(XS - 1 + hop, BUNDLE_A, beside[hop])
    encode_first(SENT_A + XS - 1, BUNDLE_B, opposite)
    pl.semaphore_wait(barrier, XS)

    first_b, first_a, last_a, second_b = {}, {}, {}, {}
    scales_b = first_scales(8 * SENT_A, 8 * SENT_B, opposite)
    scales_a = [first_scales(16 * hop, 16, beside[hop]) for hop in hops]
    for hop in hops:
        first_b[hop] = first(SENT_A + hop, opposite)
        first_a[hop] = first(hop, beside[hop])
    last_b = first(SENT_A + XS - 1, opposite)
    for hop in hops:
        for copy in first_a[hop][0]:
            copy.wait_send()
    for hop in hops:
        last_a[hop] = first(XS - 1 + hop, beside[hop])

    def pass_on(hop):
        parts = [arrive(first_b[hop])]
        encode(BUNDLE_B, beside[hop], parts, codes2.at[second_rows(1 + hop)], scales2.at[pl.ds(8 * (1 + hop), 8)])
        second_b[hop] = second(1 + hop, beside[hop])

    scales_b.wait()
    pass_on(hops[0])
    for copy in scales_a:
        copy.wait()
    parts = [arrive(first_a[hop], sent=True) for hop in hops]
    encode(BUNDLE_A, opposite, parts, codes2.at[second_rows(0)], scales2.at[pl.ds(0, 8)])
    second_a = second(0, opposite)
    pass_on(hops[1])
    pass_on(hops[2])
    parts = [*(arrive(last_a[hop]) for hop in hops), arrive(second_a)]
    finish(BUNDLE_A, parts)
    parts = [arrive(last_b), *(arrive(second_b[hop]) for hop in hops)]
    finish(BUNDLE_B, parts)


def gather_call(spec_part, pupil_part):
    moved = 2 * (SENT_A + SENT_B + XS)
    code = pltpu.VMEM((CODE_ROWS, PUP), jnp.int16)
    scale = pltpu.VMEM((8 * (SENT_A + SENT_B), PUP), F32)
    code2 = pltpu.VMEM((ROWS_A + (XS - 1) * ROWS_B, PUP), jnp.int16)
    scale2 = pltpu.VMEM((8 * XS, PUP), F32)
    return pl.pallas_call(
        gather_kernel,
        out_shape=(
            pltpu.VMEM((2, SPEC_ROWS, BLOCKS * PUP), F32),
            pltpu.VMEM((2, PUP_ROWS, PUP), F32),
        ),
        in_specs=[vmem()] * 2,
        out_specs=(vmem(), vmem()),
        scratch_shapes=[
            *(code, scale, code, scale),
            *(code2, scale2, code2, scale2),
            pltpu.SemaphoreType.DMA((moved,)),
            pltpu.SemaphoreType.DMA((moved,)),
        ],
        compiler_params=pltpu.CompilerParams(
            collective_id=2, has_side_effects=True, vmem_limit_bytes=VMEM_LIMIT
        ),
        name="reduce_scatter",
    )(*in_vmem(spec_part, pupil_part))


def store_kernel(spec_ref, pupil_ref, spec_out, pupil_out, sems):
    copies = [
        pltpu.make_async_copy(spec_ref, spec_out, sems.at[0]),
        pltpu.make_async_copy(pupil_ref, pupil_out, sems.at[1]),
    ]
    for copy in copies:
        copy.start()
    for copy in copies:
        copy.wait()


def store_call(spec_share, pupil_share):
    return pl.pallas_call(
        store_kernel,
        out_shape=(
            jax.ShapeDtypeStruct(spec_share.shape, F32),
            jax.ShapeDtypeStruct(pupil_share.shape, F32),
        ),
        in_specs=[vmem()] * 2,
        out_specs=(hbm(), hbm()),
        scratch_shapes=[pltpu.SemaphoreType.DMA((2,))],
        compiler_params=pltpu.CompilerParams(vmem_limit_bytes=VMEM_LIMIT),
        name="store",
    )(*in_vmem(spec_share, pupil_share))


def on_device(tables, spectrum, pupil, offsets, widths, live, measured):
    groups = lax.axis_size("led")
    lamps = measured.shape[0]
    scale = 1.0 / math.sqrt(lamps * groups)
    spectrum, pupil, offsets = spectrum[0], pupil[0], offsets[0].T
    middle, ends, near, above, below, planes, pupil, tables, measured, offsets, widths, live = forward_call(
        scale, offsets, widths, live, spectrum, pupil, tables, measured
    )
    parts = backward_call(
        scale, offsets, widths, live, planes, pupil, tables, measured, above, below, near, middle, ends
    )
    spec_share, pupil_share = store_call(*gather_call(*parts))
    return spec_share[None], pupil_share[None]


def solution(mesh):
    tables = dft_tables()

    def run(spectrum, pupil, offsets, widths, live, measured):
        return jax.shard_map(
            on_device,
            mesh=mesh,
            in_specs=(
                P(),
                P("tile", None, None, None),
                P("tile", None, None, None),
                P("tile", "led", None),
                P(),
                P("led"),
                P("led", "tile", None),
            ),
            out_specs=(P("tile", None, "led", None), P("tile", None, "led", None)),
            check_vma=False,
        )(jnp.asarray(tables), spectrum, pupil, offsets, widths, live, measured)

    return run
```
